32 devices in a mesh: groups: 2 (over y), fsdp: 4 (over z), resp: 2 (over x), tp: 2 (over core).
Axes of the slice: x: 2, y: 2, z: 4, core: 2. Of those that a mesh axis runs over, the one named last changes fastest.
Arguments:
- hidden: bfloat16 [8, 4, 128, 8192], P(('groups', 'fsdp'), 'resp', None, 'tp'), parts along dimension 0, may hold values from -6 to 6
- queries: bfloat16 [8, 4, 128, 4096], P(('groups', 'fsdp'), 'resp', None, 'tp'), parts along dimension 0, may hold values from -140 to 140
- prompt_keys: bfloat16 [8, 1024, 512], P(('groups', 'fsdp'), 'resp', 'tp'), parts along dimension 0, may hold values from -4.5 to 4.5
- prompt_values: bfloat16 [8, 1024, 512], P(('groups', 'fsdp'), 'resp', 'tp'), parts along dimension 0, may hold values from -6 to 6
- key_weight: bfloat16 [8192, 512], P(('fsdp', 'resp'), 'tp'), may hold values from -0.0625 to 0.0625
- value_weight: bfloat16 [8192, 512], P(('fsdp', 'resp'), 'tp'), may hold values from -0.0625 to 0.0625
- counts: int32 [8], P(('groups', 'fsdp')), parts along dimension 0, may hold values from 1 to 4
Outputs:
- attended: bfloat16 [8, 4, 128, 4096], P(('groups', 'fsdp'), 'resp', None, 'tp'), parts along dimension 0
The draws below stay inside these ranges and needn't reach their ends.
There are 2 independent parts, one for each index of `groups`. The reference program is written for one: setup_inputs(seed, part) draws one part's arguments, and reference() takes and returns one part's arrays. A program takes and returns all parts, laid end to end along the dimension named above; an argument that names none is the same for every part. Nothing has to cross between parts.
All inputs are finite; a program needn't handle non-finite values.
Results may differ from the reference program's by a relative error of at most 0.0069.
Values may be sent and summed in bfloat16 or wider, within the bound.
No kernel may reach another device: no remote copies, remote signals or barrier semaphores. Data moves between devices by JAX's collectives and lax.ppermute only.
A program may use at most 128 MiB of HBM per device.

```python
import math
import jax
import jax.numpy as jnp
from jax import lax

D = 8192
HD = 128
QH = 32
KVH = 4
RLEN = 128
PLEN = 1024
PROMPTS = 4
SLOTS = 4


def shared_keys(key):
    normals = jax.random.normal(jax.random.fold_in(key, 11), (PROMPTS, PLEN, KVH * HD), jnp.float32)
    return jnp.clip(normals, -4.5, 4.5)


def draw_prompt_keys(key, part):
    cached = shared_keys(key)
    return cached.astype(jnp.bfloat16)


def draw_queries(key, part):
    key = jax.random.fold_in(key, 5)
    normals = jax.random.normal(key, (PROMPTS, SLOTS, RLEN, QH * HD), jnp.float32)
    normals = 2.0 * jnp.clip(normals, -6.0, 6.0)
    return normals.astype(jnp.bfloat16)


def touch_ends(drawn, stream_key, low, high):
    index_at = [jax.random.randint(jax.random.fold_in(stream_key, axis), (), 0, length) for axis, length in enumerate(drawn.shape)]
    widest = drawn.shape.index(max(drawn.shape))
    next_to = index_at[:widest] + [(index_at[widest] + 1) % drawn.shape[widest]] + index_at[widest + 1:]
    return drawn.at[tuple(index_at)].set(low).at[tuple(next_to)].set(high)


def level_of(key, shape, pieces, low, largest):
    loudness = 1.0
    for position, parts in pieces:
        heights = jax.random.uniform(jax.random.fold_in(jax.random.fold_in(key, 6), position), (parts,), jnp.float32, low / len(pieces), largest / len(pieces))
        loudness = loudness * jnp.repeat(jnp.exp(heights), shape[position] // parts).reshape((-1,) + (1,) * (len(shape) - 1 - position))
    return loudness


def normal_values(stream_key, shape, spread, bound, pieces=(), kind=jnp.bfloat16):
    drawn = spread * jax.random.normal(stream_key, shape, jnp.float32)
    if pieces:
        drawn = drawn * level_of(stream_key, shape, pieces, -0.22, 0.18)
    return jnp.clip(drawn, -bound, bound).astype(kind)


def setup_inputs(seed: int = 0, part: int = 0) -> dict:
    streams_of = jax.random.split(jax.random.key(seed), 8)
    part_keys = jax.random.split(jax.random.fold_in(streams_of[7], part), 8)
    return {
        "hidden": normal_values(part_keys[0], (PROMPTS, SLOTS, RLEN, D), 1.0, 6.0, ((0, 4), (1, 2), (3, 2))),
        "queries": draw_queries(jax.random.fold_in(jax.random.fold_in(streams_of[7], part), 71), part),
        "prompt_keys": draw_prompt_keys(jax.random.fold_in(jax.random.fold_in(streams_of[7], part), 71), part),
        "prompt_values": normal_values(part_keys[3], (PROMPTS, PLEN, KVH * HD), 1.0, 6.0, ((0, 4), (1, 2), (2, 2))),
        "key_weight": normal_values(streams_of[4], (D, KVH * HD), D ** -0.5, 0.0625, ((0, 8), (1, 2))),
        "value_weight": normal_values(streams_of[5], (D, KVH * HD), D ** -0.5, 0.0625, ((0, 8), (1, 2))),
        "counts": touch_ends(jax.random.randint(part_keys[6], (PROMPTS,), 1, SLOTS + 1), jax.random.fold_in(part_keys[6], 1), 1, SLOTS).astype(jnp.int32),
    }


def rotate(vectors, offset):
    half_size = vectors.shape[-1] // 2
    extent = vectors.shape[-3]
    orders = jnp.arange(half_size, dtype=jnp.float32)
    inverse = jnp.exp(-(2.0 * orders / vectors.shape[-1]) * math.log(500000.0))
    places = (offset + jnp.arange(extent)).astype(jnp.float32)
    angles = places[:, None] * inverse[None, :]
    cosine = jnp.cos(angles)[:, None, :]
    sine_table = jnp.sin(angles)[:, None, :]
    leading = vectors[..., :half_size]
    second = vectors[..., half_size:]
    return jnp.concatenate([leading * cosine - second * sine_table, second * cosine + leading * sine_table], axis=-1)


def rounded(values):
    return lax.optimization_barrier(values.astype(jnp.bfloat16)).astype(jnp.float32)


def reference(hidden, queries, prompt_keys, prompt_values, key_weight, value_weight, counts):
    slot_count = hidden.shape[1]
    resp_len = hidden.shape[2]
    feature_width = hidden.shape[3]
    group_size = QH // KVH
    score_scale = HD ** -0.5
    causal = (jnp.arange(resp_len)[:, None] >= jnp.arange(resp_len)[None, :])[:, None, None, :]

    def one_prompt(prompt_items):
        tokens, queried, cache_keys, cache_values, live_count = prompt_items
        flat_rows = tokens.reshape(slot_count * resp_len, feature_width)
        key_sums = jnp.dot(flat_rows, key_weight, preferred_element_type=jnp.float32)
        own_keys = rotate(key_sums.reshape(slot_count, resp_len, KVH, HD), PLEN).astype(jnp.bfloat16)
        own_values = jnp.dot(flat_rows, value_weight, preferred_element_type=jnp.float32).astype(jnp.bfloat16)
        own_values = own_values.reshape(slot_count, resp_len, KVH, HD)
        far_keys = cache_keys.reshape(PLEN, KVH, HD).astype(jnp.float32)
        far_values = cache_values.reshape(PLEN, KVH, HD).astype(jnp.float32)

        def one_slot(slot_items):
            query_rows, slot_keys, slot_values, slot_index = slot_items
            query_float = query_rows.reshape(resp_len, KVH, group_size, HD).astype(jnp.float32)
            far_scores = jnp.einsum("rkgd,lkd->rkgl", query_float, far_keys) * score_scale
            near_scores = jnp.einsum("rkgd,lkd->rkgl", query_float, slot_keys.astype(jnp.float32)) * score_scale
            near_scores = jnp.where(causal, near_scores, -1e30)
            row_top = jnp.maximum(jnp.max(far_scores, axis=-1), jnp.max(near_scores, axis=-1))
            far_weights = jnp.exp(far_scores - row_top[..., None])
            near_weights = jnp.exp(near_scores - row_top[..., None])
            row_total = jnp.sum(far_weights, axis=-1) + jnp.sum(near_weights, axis=-1)
            mixed_sum = jnp.einsum("rkgl,lkd->rkgd", rounded(far_weights), far_values)
            mixed_sum = mixed_sum + jnp.einsum("rkgl,lkd->rkgd", rounded(near_weights), slot_values.astype(jnp.float32))
            result = mixed_sum / row_total[..., None]
            is_live = slot_index < live_count
            result = jnp.where(is_live, result, 0.0)
            return result.reshape(resp_len, QH * HD).astype(jnp.bfloat16)

        slot_numbers = jnp.arange(slot_count).astype(jnp.int32)
        return lax.map(one_slot, (queried, own_keys, own_values, slot_numbers))

    return lax.map(one_prompt, (hidden, queries, prompt_keys, prompt_values, counts))
```

```python
import functools
import math

import jax
import jax.numpy as jnp
from jax import lax
from jax.experimental import pallas as pl
from jax.experimental.pallas import tpu as pltpu
from jax.sharding import PartitionSpec as P

HD = 128
PLEN = 1024
LOG2E = 1.4426950408889634
MIB = 1 << 20


def dot_nt(a, b):
    return lax.dot_general(a, b, (((1,), (1,)), ((), ())), preferred_element_type=jnp.float32)


def dot_nn(a, b):
    return lax.dot_general(a, b, (((1,), (0,)), ((), ())), preferred_element_type=jnp.float32)


def stacked_heads(ref, first, count):
    return jnp.concatenate(
        [ref[:, (first + n) * HD : (first + n + 1) * HD] for n in range(count)], axis=0
    )


def prompt_kernel(sources, group_size, factor, q_ref, *refs):
    keys = refs[:sources]
    values = refs[sources : 2 * sources]
    acc_ref, stat_ref = refs[2 * sources :]
    tokens = q_ref.shape[0]
    wide = [
        jnp.concatenate([v[...], jnp.ones(v.shape, v.dtype)], axis=1) for v in values
    ]
    lane = lax.broadcasted_iota(jnp.int32, (tokens, HD), 1)
    stats = jnp.zeros((tokens, HD), jnp.float32)
    pair = 2 if group_size % 2 == 0 else 1
    for first in range(0, group_size, pair):
        q = stacked_heads(q_ref, first, pair)
        scores = [dot_nt(q, k[...]) for k in keys]
        top = functools.reduce(
            jnp.maximum, [jnp.max(s, axis=1, keepdims=True) for s in scores]
        )
        out = None
        for s, v in zip(scores, wide):
            probs = jnp.exp2((s - top) * factor).astype(jnp.bfloat16)
            part = dot_nn(probs, v)
            out = part if out is None else out + part
        for n in range(pair):
            rows = slice(n * tokens, (n + 1) * tokens)
            head = first + n
            acc_ref[:, head * HD : (head + 1) * HD] = out[rows, :HD]
            stats = jnp.where(lane == head, top[rows], stats)
            stats = jnp.where(lane == group_size + head, out[rows, HD:], stats)
    stat_ref[...] = stats


def prompt_attention(slot, head, tokens, group_size, queries, keys, values):
    width = group_size * HD
    count = len(keys)
    length = keys[0].shape[0]
    spec_q = pl.BlockSpec((tokens, width), lambda _: (slot, head))
    spec_c = pl.BlockSpec((length, HD), lambda _: (0, head))
    work = tokens * group_size * length * count
    return pl.pallas_call(
        functools.partial(prompt_kernel, count, group_size, HD**-0.5 * LOG2E),
        grid=(1,),
        in_specs=[spec_q] + [spec_c] * (2 * count),
        out_specs=[
            pl.BlockSpec((tokens, width), lambda _: (0, 0)),
            pl.BlockSpec((tokens, HD), lambda _: (0, 0)),
        ],
        out_shape=[
            jax.ShapeDtypeStruct((tokens, width), jnp.float32),
            jax.ShapeDtypeStruct((tokens, HD), jnp.float32),
        ],
        compiler_params=pltpu.CompilerParams(vmem_limit_bytes=24 * MIB),
        cost_estimate=pl.CostEstimate(
            flops=6 * work * HD, bytes_accessed=2 * MIB, transcendentals=work
        ),
        name="prompt_attention",
    )(queries, *keys, *values)


def project(meta, near, far, pieces, start, dtype):
    rows = near.shape[1]
    columns = pieces[0][0].shape[1]
    vmem = pl.BlockSpec(memory_space=pltpu.VMEM)
    operands = [near, far]
    for parts in pieces:
        operands.extend(parts)
    if start is not None:
        operands.append(start)
    halves = [len(parts) == 2 for parts in pieces]

    def body(meta_ref, near_ref, far_ref, *refs):
        project_kernel_body(halves, start is not None, meta_ref, near_ref, far_ref, refs)

    return pl.pallas_call(
        body,
        in_specs=[pl.BlockSpec(memory_space=pltpu.SMEM)] + [vmem] * len(operands),
        out_specs=vmem,
        out_shape=jax.ShapeDtypeStruct((rows, columns), dtype),
        compiler_params=pltpu.CompilerParams(vmem_limit_bytes=24 * MIB),
        cost_estimate=pl.CostEstimate(
            flops=2 * rows * columns * near.shape[2] * len(pieces),
            bytes_accessed=2 * MIB,
            transcendentals=0,
        ),
        name="project",
    )(meta, *operands)


def project_kernel_body(halves, started, meta_ref, near_ref, far_ref, refs):
    refs = list(refs)
    out_ref = refs.pop()
    total = refs.pop()[...] if started else None
    group = meta_ref[0]
    for n, split in enumerate(halves):
        place = meta_ref[1 + 2 * n]
        near = meta_ref[2 + 2 * n] == 1
        features = jnp.where(near, near_ref[place], far_ref[place])
        if split:
            mine, other = refs.pop(0)[...], refs.pop(0)[...]
            weight = jnp.concatenate(
                [jnp.where(group == 0, mine, other), jnp.where(group == 0, other, mine)], axis=0
            )
        else:
            weight = refs.pop(0)[...]
        part = dot_nn(features, weight)
        total = part if total is None else total + part
    out_ref[...] = total.astype(out_ref.dtype)


def own_kernel(received, kv_heads, group_size, factor, meta_ref, *refs):
    refs = list(refs)
    q_ref, cos_ref, sin_ref = refs[:3]
    key_refs = refs[3 : 4 + received]
    value_refs = refs[4 + received : 5 + 2 * received]
    state = refs[5 + 2 * received : -1]
    out_ref = refs[-1]
    tokens = cos_ref.shape[0]
    slots = q_ref.shape[0] // tokens
    row = lax.broadcasted_iota(jnp.int32, (tokens, tokens), 0)
    column = lax.broadcasted_iota(jnp.int32, (tokens, tokens), 1)
    causal = row >= column
    pair = 2 if group_size % 2 == 0 else 1
    causal_rows = jnp.concatenate([causal] * pair, axis=0) if pair > 1 else causal
    for slot in range(slots):
        live = slot < meta_ref[0]
        rows_of = slice(slot * tokens, (slot + 1) * tokens)
        for head in range(kv_heads):
            lanes = slice(head * HD, (head + 1) * HD)
            key = key_refs[0][rows_of, lanes].astype(jnp.float32)
            for ref in key_refs[1:]:
                key = key + ref[rows_of, lanes].astype(jnp.float32)
            key = key * cos_ref[...] + pltpu.roll(key, HD // 2, 1) * sin_ref[...]
            key = key.astype(jnp.bfloat16)
            value = value_refs[0][rows_of, lanes].astype(jnp.float32)
            for ref in value_refs[1:]:
                value = value + ref[rows_of, lanes].astype(jnp.float32)
            value = value.astype(jnp.bfloat16)
            wide = jnp.concatenate([value, jnp.ones(value.shape, value.dtype)], axis=1)
            acc_ref, stat_ref = state[2 * (slot * kv_heads + head) :][:2]
            for first in range(0, group_size, pair):
                base = head * group_size + first
                q = jnp.concatenate(
                    [q_ref[rows_of, (base + n) * HD : (base + n + 1) * HD] for n in range(pair)],
                    axis=0,
                )
                scores = jnp.where(causal_rows, dot_nt(q, key), -1e30)
                old_top = jnp.concatenate(
                    [stat_ref[:, first + n : first + n + 1] for n in range(pair)], axis=0
                )
                old_total = jnp.concatenate(
                    [
                        stat_ref[:, group_size + first + n : group_size + first + n + 1]
                        for n in range(pair)
                    ],
                    axis=0,
                )
                top = jnp.maximum(old_top, jnp.max(scores, axis=1, keepdims=True))
                probs = jnp.exp2((scores - top) * factor).astype(jnp.bfloat16)
                shrink = jnp.exp2((old_top - top) * factor)
                out = dot_nn(probs, wide)
                old = stacked_heads(acc_ref, first, pair)
                mixed = old * shrink + out[:, :HD]
                total = old_total * shrink + out[:, HD:]
                result = jnp.where(live, mixed / total, 0.0).astype(out_ref.dtype)
                for n in range(pair):
                    out_ref[rows_of, (base + n) * HD : (base + n + 1) * HD] = result[
                        n * tokens : (n + 1) * tokens
                    ]


def own_attention(meta, queries, cosine, sine, key_parts, value_parts, states, group_size):
    kv_heads = key_parts[0].shape[1] // HD
    vmem = pl.BlockSpec(memory_space=pltpu.VMEM)
    operands = [queries, cosine, sine, *key_parts, *value_parts]
    for acc, stats in states:
        operands.extend((acc, stats))

    def body(meta_ref, *refs):
        own_kernel(
            len(key_parts) - 1, kv_heads, group_size, HD**-0.5 * LOG2E, meta_ref, *refs
        )

    work = queries.shape[0] * queries.shape[1]
    return pl.pallas_call(
        body,
        in_specs=[pl.BlockSpec(memory_space=pltpu.SMEM)] + [vmem] * len(operands),
        out_specs=vmem,
        out_shape=jax.ShapeDtypeStruct(queries.shape, queries.dtype),
        compiler_params=pltpu.CompilerParams(vmem_limit_bytes=24 * MIB),
        cost_estimate=pl.CostEstimate(
            flops=6 * work * HD, bytes_accessed=5 * MIB, transcendentals=work
        ),
        name="own_attention",
    )(meta, *operands)


def rotation_tables(extent, offset):
    half = HD // 2
    orders = jnp.arange(half, dtype=jnp.float32)
    inverse = jnp.exp(-(2.0 * orders / HD) * math.log(500000.0))
    places = (offset + jnp.arange(extent)).astype(jnp.float32)
    angles = places[:, None] * inverse[None, :]
    cosine, sine = jnp.cos(angles), jnp.sin(angles)
    return jnp.concatenate([cosine, cosine], axis=1), jnp.concatenate([-sine, sine], axis=1)


def pick(index, choices):
    chosen = choices[0]
    for n in range(1, len(choices)):
        chosen = jnp.where(index == n, choices[n], chosen)
    return chosen


def line_ring(size):
    return list(range(0, size, 2)) + list(range(1, size, 2))[::-1]


def on_device(sizes, hidden, queries, prompt_keys, prompt_values, key_weight, value_weight, counts):
    n_groups, n_fsdp, n_resp, n_tp = sizes
    _, slots, tokens, part_width = hidden.shape
    block, columns = key_weight.shape
    kv_heads = columns // HD
    group_size = queries.shape[3] // columns
    rows = slots * tokens
    per_core = n_fsdp // n_tp
    group = lax.axis_index("groups")
    fsdp = lax.axis_index("fsdp")
    resp = lax.axis_index("resp")
    core = lax.axis_index("tp")

    ring = line_ring(n_fsdp)
    hops = [(ring[n], ring[(n + 1) % n_fsdp]) for n in range(n_fsdp)]
    twins = [(n, n_groups - 1 - n) for n in range(n_groups)]
    cores = [(n, (n + 1) % n_tp) for n in range(n_tp)]
    half = block // n_groups

    def share(weight):
        return pick(group, [weight[n * half : (n + 1) * half] for n in range(n_groups)])

    def shift(number):
        return [(n, (n + number) % n_resp) for n in range(n_resp)]

    caches = [(prompt_keys[0], prompt_values[0])]
    for number in range(1, n_resp):
        caches.append(
            (
                lax.ppermute(prompt_keys[0], "resp", shift(number)),
                lax.ppermute(prompt_values[0], "resp", shift(number)),
            )
        )

    moving = [share(key_weight), share(value_weight)]
    pieces = [[(key_weight,)], [(value_weight,)]]
    for _ in range(n_fsdp - 1):
        for chunk in range(2):
            moving[chunk] = lax.ppermute(moving[chunk], "fsdp", hops)
            pieces[chunk].append((moving[chunk], lax.ppermute(moving[chunk], "groups", twins)))

    flat = hidden.reshape(rows, part_width)

    def features_of(target):
        return jnp.stack(
            [
                pick(
                    target,
                    [
                        flat[:, (n * n_resp + r) * block : (n * n_resp + r + 1) * block]
                        for r in range(n_resp)
                    ],
                )
                for n in range(per_core)
            ]
        )

    near = [features_of(resp)]
    for number in range(1, n_resp):
        near.append(
            lax.ppermute(features_of((resp + number) % n_resp), "resp", shift(number))
        )
    far = [lax.ppermute(x, "tp", cores) for x in near]

    ring_table = jnp.array(ring, jnp.int32)
    place_table = jnp.array([ring.index(n) for n in range(n_fsdp)], jnp.int32)
    place = place_table[fsdp]
    owners = [ring_table[(place + n_fsdp - n) % n_fsdp] for n in range(n_fsdp)]

    def meta_of(chosen):
        fields = [group.astype(jnp.int32)]
        for n in chosen:
            fields.append(owners[n] % per_core)
            fields.append((owners[n] // per_core == core).astype(jnp.int32))
        return jnp.stack(fields)

    early = list(range(n_fsdp - 1))
    late = [n_fsdp - 1]
    meta_early, meta_late = meta_of(early), meta_of(late)

    flat_queries = queries.reshape(rows, queries.shape[3])
    states = []
    for slot in range(slots):
        for head in range(kv_heads):
            states.append(
                prompt_attention(
                    slot,
                    head,
                    tokens,
                    group_size,
                    flat_queries,
                    [c[0] for c in caches],
                    [c[1] for c in caches],
                )
            )

    sums = []
    for chunk in range(2):
        started = [
            project(
                meta_early, near[n], far[n], [pieces[chunk][p] for p in early], None, jnp.float32
            )
            for n in range(n_resp)
        ]
        parts = []
        for number in range(1, n_resp):
            sent = project(
                meta_late,
                near[number],
                far[number],
                [pieces[chunk][p] for p in late],
                started[number],
                jnp.bfloat16,
            )
            parts.append(lax.ppermute(sent, "resp", shift(n_resp - number)))
        kept = project(
            meta_late,
            near[0],
            far[0],
            [pieces[chunk][p] for p in late],
            started[0],
            jnp.float32,
        )
        sums.append([kept, *parts])

    cosine, sine = rotation_tables(tokens, PLEN)
    live = (counts[0] - resp * slots).astype(jnp.int32)[None]
    out = own_attention(
        live, flat_queries, cosine, sine, sums[0], sums[1], states, group_size
    )
    return out.reshape(queries.shape)


def solution(mesh):
    placed = (
        P(("groups", "fsdp"), "resp", None, "tp"),
        P(("groups", "fsdp"), "resp", None, "tp"),
        P(("groups", "fsdp"), "resp", "tp"),
        P(("groups", "fsdp"), "resp", "tp"),
        P(("fsdp", "resp"), "tp"),
        P(("fsdp", "resp"), "tp"),
        P(("groups", "fsdp")),
    )
    sizes = tuple(mesh.shape[name] for name in ("groups", "fsdp", "resp", "tp"))
    return jax.shard_map(
        functools.partial(on_device, sizes),
        mesh=mesh,
        in_specs=placed,
        out_specs=P(("groups", "fsdp"), "resp", None, "tp"),
        check_vma=False,
    )
```

```python
import functools
import math

import jax
import jax.numpy as jnp
from jax import lax
from jax.experimental import pallas as pl
from jax.experimental.pallas import tpu as pltpu
from jax.sharding import PartitionSpec as P

HD = 128
PLEN = 1024
LOG2E = 1.4426950408889634
FACTOR = HD**-0.5 * LOG2E
MIB = 1 << 20
VMEM = pl.BlockSpec(memory_space=pltpu.VMEM)
SMEM = pl.BlockSpec(memory_space=pltpu.SMEM)
ANYWHERE = pl.BlockSpec(memory_space=pl.ANY)
HBM = pl.BlockSpec(memory_space=pltpu.HBM)


def dot_nt(a, b):
    return lax.dot_general(a, b, (((1,), (1,)), ((), ())), preferred_element_type=jnp.float32)


def dot_nn(a, b):
    return lax.dot_general(a, b, (((1,), (0,)), ((), ())), preferred_element_type=jnp.float32)


def take_heads(ref, first, count):
    return jnp.concatenate(
        [ref[:, (first + n) * HD : (first + n + 1) * HD] for n in range(count)], axis=0
    )


def put_heads(ref, first, count, stacked):
    tokens = ref.shape[0]
    for n in range(count):
        ref[:, (first + n) * HD : (first + n + 1) * HD] = stacked[
            n * tokens : (n + 1) * tokens
        ].astype(ref.dtype)


def take_column(ref, first, count):
    return jnp.concatenate([ref[:, first + n : first + n + 1] for n in range(count)], axis=0)


def put_column(stats, lane, first, count, stacked):
    tokens = stats.shape[0]
    for n in range(count):
        stats = jnp.where(lane == first + n, stacked[n * tokens : (n + 1) * tokens], stats)
    return stats


def with_ones(values):
    return jnp.concatenate([values, jnp.ones(values.shape, values.dtype)], axis=1)


def pack(sizes, hidden, key_weight, value_weight, prompt_keys, prompt_values):
    n_groups, n_fsdp, n_resp, n_tp = sizes
    rows = hidden.shape[0]
    block, columns = key_weight.shape
    per_core = n_fsdp // n_tp
    half = block // n_groups
    length = prompt_keys.shape[0]
    sets = [(a, b) for a in range(n_groups) for b in range(n_resp)]

    if half % HD:

        def cut(target_group, target_resp):
            parts = []
            for n in range(per_core):
                start = (n * n_resp + target_resp) * block + target_group * half
                parts.append(lax.dynamic_slice_in_dim(hidden, start, half, axis=1))
            return jnp.concatenate(parts, axis=1)

        group, resp = lax.axis_index("groups"), lax.axis_index("resp")
        features = [cut((group + a) % n_groups, (resp + b) % n_resp) for a, b in sets]
        shares = [
            lax.dynamic_slice_in_dim(w, group * half, half, axis=0)
            for w in (key_weight, value_weight)
        ]
        return features, shares, jnp.concatenate([prompt_keys, prompt_values], axis=0)

    def body(hidden_ref, kw_ref, vw_ref, pk_ref, pv_ref, *refs):
        outs, sems = refs[:-1], refs[-1]
        group, resp = lax.axis_index("groups"), lax.axis_index("resp")
        moves = []
        rows_of = pl.ds(pl.multiple_of(group * half, half), half)
        moves.append((kw_ref.at[rows_of, :], outs[len(sets)]))
        moves.append((vw_ref.at[rows_of, :], outs[len(sets) + 1]))
        for (a, b), out in zip(sets, outs):
            target_group, target_resp = (group + a) % n_groups, (resp + b) % n_resp
            for n in range(per_core):
                start = (n * n_resp + target_resp) * block + target_group * half
                moves.append(
                    (
                        hidden_ref.at[:, pl.ds(pl.multiple_of(start, HD), half)],
                        out.at[:, pl.ds(n * half, half)],
                    )
                )
        moves.append((pk_ref, outs[-1].at[pl.ds(0, length), :]))
        moves.append((pv_ref, outs[-1].at[pl.ds(length, length), :]))
        copies = [
            pltpu.make_async_copy(source, target, sems.at[n])
            for n, (source, target) in enumerate(moves)
        ]
        for copy in copies:
            copy.start()
        for copy in copies:
            copy.wait()

    kind = hidden.dtype
    shapes = [jax.ShapeDtypeStruct((rows, per_core * half), kind)] * len(sets)
    shapes += [jax.ShapeDtypeStruct((half, columns), kind)] * 2
    shapes += [jax.ShapeDtypeStruct((2 * length, columns), kind)]
    outs = pl.pallas_call(
        body,
        in_specs=[HBM] * 5,
        out_specs=[ANYWHERE] * len(shapes),
        out_shape=shapes,
        scratch_shapes=[pltpu.SemaphoreType.DMA((4 + per_core * len(sets),))],
        cost_estimate=pl.CostEstimate(flops=0, bytes_accessed=6 * MIB, transcendentals=0),
        name="pack",
    )(hidden, key_weight, value_weight, prompt_keys, prompt_values)
    return outs[: len(sets)], list(outs[len(sets) : len(sets) + 2]), outs[-1]


def project(sets, weight, dtype):
    rows, depth = sets[0][0].shape
    columns = weight.shape[1]
    count = len(sets)

    def body(weight_ref, *refs):
        core = lax.axis_index("tp")
        first = pl.ds(pl.multiple_of(core * depth, depth), depth)
        second = pl.ds(pl.multiple_of((1 - core) * depth, depth), depth)
        near_weight, far_weight = weight_ref[first, :], weight_ref[second, :]
        for n in range(count):
            near_ref, far_ref = refs[2 * n], refs[2 * n + 1]
            out_ref = refs[2 * count + n]
            total = dot_nn(near_ref[...], near_weight) + dot_nn(far_ref[...], far_weight)
            out_ref[...] = total.astype(out_ref.dtype)

    return pl.pallas_call(
        body,
        in_specs=[VMEM] * (1 + 2 * count),
        out_specs=[VMEM] * count,
        out_shape=[jax.ShapeDtypeStruct((rows, columns), dtype)] * count,
        compiler_params=pltpu.CompilerParams(vmem_limit_bytes=24 * MIB),
        cost_estimate=pl.CostEstimate(
            flops=4 * rows * columns * depth * count, bytes_accessed=3 * MIB, transcendentals=0
        ),
        name="project",
    )(weight, *[x for pair in sets for x in pair])


def attend(slot, head, tokens, group_size, queries, keys, values, own=None, state=None):
    width = group_size * HD
    pair = 2 if group_size % 2 == 0 else 1
    count = len(keys)
    own_parts, tables = own if own is not None else ([], [])
    extra = len(own_parts)

    def body(q_ref, *refs):
        refs = list(refs)
        key_refs = [refs.pop(0) for _ in range(count)]
        value_refs = [refs.pop(0) for _ in range(count)]
        own_refs = [refs.pop(0) for _ in range(extra)]
        if extra:
            cos_ref, sin_ref = refs.pop(0), refs.pop(0)
        if state is not None:
            old_acc_ref, old_stat_ref = refs.pop(0), refs.pop(0)
        acc_ref, stat_ref = refs[:2]
        wide = [with_ones(v[...]) for v in value_refs]
        lane = lax.broadcasted_iota(jnp.int32, (tokens, HD), 1)
        stats = jnp.zeros((tokens, HD), jnp.float32)
        if extra:
            key = own_refs[0][...].astype(jnp.float32)
            for ref in own_refs[1:]:
                key = key + ref[...].astype(jnp.float32)
            key = key * cos_ref[...] + pltpu.roll(key, HD // 2, 1) * sin_ref[...]
            own_key = key.astype(jnp.bfloat16)
            ones = jnp.ones((tokens, HD), jnp.bfloat16)
            causal = lax.broadcasted_iota(jnp.int32, (tokens, tokens), 0) >= (
                lax.broadcasted_iota(jnp.int32, (tokens, tokens), 1)
            )
            causal = jnp.concatenate([causal] * pair, axis=0)
        for first in range(0, group_size, pair):
            q = take_heads(q_ref, first, pair)
            scores = [dot_nt(q, k[...]) for k in key_refs]
            if extra:
                scores.append(jnp.where(causal, dot_nt(q, own_key), -1e30))
            tops = [jnp.max(s, axis=1, keepdims=True) for s in scores]
            if state is not None:
                old_top = take_column(old_stat_ref, first, pair)
                tops.append(old_top)
            top = functools.reduce(jnp.maximum, tops)
            probs = [jnp.exp2((s - top) * FACTOR).astype(jnp.bfloat16) for s in scores]
            out = functools.reduce(jnp.add, [dot_nn(p, v) for p, v in zip(probs, wide)])
            mixed, total = out[:, :HD], out[:, HD:]
            if extra:
                total = total + dot_nn(probs[-1], ones)
                put_heads(refs[2], first, pair, probs[-1])
            if state is not None:
                shrink = jnp.exp2((old_top - top) * FACTOR)
                mixed = mixed + take_heads(old_acc_ref, first, pair) * shrink
                total = total + take_column(old_stat_ref, group_size + first, pair) * shrink
            if extra:
                inverse = 1.0 / total
                put_heads(acc_ref, first, pair, mixed * inverse)
                stats = put_column(stats, lane, first, pair, inverse)
            else:
                put_heads(acc_ref, first, pair, mixed)
                stats = put_column(stats, lane, first, pair, top)
                stats = put_column(stats, lane, group_size + first, pair, total)
        stat_ref[...] = stats

    length = keys[0].shape[0]
    spec_q = pl.BlockSpec((tokens, width), lambda _: (slot, head))
    spec_c = pl.BlockSpec((length, HD), lambda _: (0, head))
    spec_own = pl.BlockSpec((tokens, HD), lambda _: (slot, head))
    spec_table = pl.BlockSpec((tokens, HD), lambda _: (0, 0))
    spec_wide = pl.BlockSpec((tokens, width), lambda _: (0, 0))
    operands = [queries, *keys, *values, *own_parts, *tables]
    specs = [spec_q] + [spec_c] * (2 * count) + [spec_own] * extra + [spec_table] * len(tables)
    if state is not None:
        operands.extend(state)
        specs.extend([spec_wide, spec_table])
    out_specs = [spec_wide, spec_table]
    shapes = [
        jax.ShapeDtypeStruct((tokens, width), jnp.float32),
        jax.ShapeDtypeStruct((tokens, HD), jnp.float32),
    ]
    if extra:
        out_specs.append(spec_wide)
        shapes.append(jax.ShapeDtypeStruct((tokens, width), jnp.bfloat16))
    work = tokens * group_size * (length * count + (tokens if extra else 0))
    return pl.pallas_call(
        body,
        grid=(1,),
        in_specs=specs,
        out_specs=out_specs,
        out_shape=shapes,
        compiler_params=pltpu.CompilerParams(vmem_limit_bytes=24 * MIB),
        cost_estimate=pl.CostEstimate(
            flops=6 * work * HD, bytes_accessed=2 * MIB, transcendentals=work
        ),
        name="attend_rest" if extra else "attend_local",
    )(*operands)


def finish(live, value_parts, states, slots, group_size, shape, dtype):
    count = len(value_parts)
    rows, columns = value_parts[0].shape
    tokens = rows // slots
    kv_heads = columns // HD

    def body(live_ref, *refs):
        out_ref = refs[-1]
        total = value_refs_sum(refs[:count])
        values = total.astype(jnp.bfloat16)
        for slot in range(slots):
            alive = slot < live_ref[0]
            for head in range(kv_heads):
                acc_ref, stat_ref, probs_ref = refs[count + 3 * (slot * kv_heads + head) :][:3]
                value = values[slot * tokens : (slot + 1) * tokens, head * HD : (head + 1) * HD]
                for n in range(group_size):
                    lanes = slice(n * HD, (n + 1) * HD)
                    part = dot_nn(probs_ref[:, lanes], value) * stat_ref[:, n : n + 1]
                    result = jnp.where(alive, acc_ref[:, lanes] + part, 0.0)
                    start = (head * group_size + n) * HD
                    out_ref[slot * tokens : (slot + 1) * tokens, start : start + HD] = (
                        result.astype(out_ref.dtype)
                    )

    def value_refs_sum(refs):
        total = refs[0][...].astype(jnp.float32)
        for ref in refs[1:]:
            total = total + ref[...].astype(jnp.float32)
        return total

    operands = [*value_parts, *[x for state in states for x in state]]
    return pl.pallas_call(
        body,
        in_specs=[SMEM] + [VMEM] * len(operands),
        out_specs=VMEM,
        out_shape=jax.ShapeDtypeStruct(shape, dtype),
        compiler_params=pltpu.CompilerParams(vmem_limit_bytes=24 * MIB),
        cost_estimate=pl.CostEstimate(
            flops=2 * shape[0] * shape[1] * tokens, bytes_accessed=5 * MIB, transcendentals=0
        ),
        name="finish",
    )(live, *operands)


def rotation_tables(extent, offset):
    half = HD // 2
    orders = jnp.arange(half, dtype=jnp.float32)
    inverse = jnp.exp(-(2.0 * orders / HD) * math.log(500000.0))
    places = (offset + jnp.arange(extent)).astype(jnp.float32)
    angles = places[:, None] * inverse[None, :]
    cosine, sine = jnp.cos(angles), jnp.sin(angles)
    return jnp.concatenate([cosine, cosine], axis=1), jnp.concatenate([-sine, sine], axis=1)


def on_device(sizes, hidden, queries, prompt_keys, prompt_values, key_weight, value_weight, counts):
    n_groups, n_fsdp, n_resp, n_tp = sizes
    _, slots, tokens, part_width = hidden.shape
    columns = key_weight.shape[1]
    kv_heads = columns // HD
    group_size = queries.shape[3] // columns
    rows = slots * tokens
    length = prompt_keys.shape[1]
    sets = [(a, b) for a in range(n_groups) for b in range(n_resp)]
    plane = ("groups", "resp")
    cores = [(n, (n + 1) % n_tp) for n in range(n_tp)]

    def shift(a, b):
        return [
            (g * n_resp + r, (g + a) % n_groups * n_resp + (r + b) % n_resp)
            for g in range(n_groups)
            for r in range(n_resp)
        ]

    features, shares, cache = pack(
        sizes,
        hidden.reshape(rows, part_width),
        key_weight,
        value_weight,
        prompt_keys[0],
        prompt_values[0],
    )
    flat_queries = queries.reshape(rows, queries.shape[3])
    places = [(slot, head) for slot in range(slots) for head in range(kv_heads)]
    started = [
        attend(
            slot,
            head,
            tokens,
            group_size,
            flat_queries,
            [prompt_keys[0]],
            [prompt_values[0]],
        )
        for slot, head in places
    ]

    def after(value, *earlier):
        return lax.optimization_barrier((value, *earlier))[0]

    near = [features[0]]
    for (a, b), sent in zip(sets[1:], features[1:]):
        moved = lax.ppermute(sent, plane, shift(a, b))
        near.append(after(moved, started[-1][1]))
    far = [lax.ppermute(x, "tp", cores) for x in near]

    shares[1] = after(shares[1], started[0][1])
    gathered = [lax.all_gather(share, "fsdp", axis=0, tiled=True) for share in shares]

    held = after(cache, *near)
    others = [
        lax.ppermute(held, "resp", [(n, (n + b) % n_resp) for n in range(n_resp)])
        for b in range(1, n_resp)
    ]

    sums = []
    for weight in gathered:
        sent = project(list(zip(near[1:], far[1:])), weight, jnp.bfloat16)
        parts = [
            lax.ppermute(x, plane, shift(n_groups - a, n_resp - b))
            for (a, b), x in zip(sets[1:], sent)
        ]
        kept = project([(near[0], far[0])], weight, jnp.float32)
        sums.append([*kept, *parts])

    tables = rotation_tables(tokens, PLEN)
    states = [
        attend(
            slot,
            head,
            tokens,
            group_size,
            flat_queries,
            [x[:length] for x in others],
            [x[length:] for x in others],
            (sums[0], tables),
            state,
        )
        for (slot, head), state in zip(places, started)
    ]
    live = (counts[0] - lax.axis_index("resp") * slots).astype(jnp.int32)[None]
    out = finish(live, sums[1], states, slots, group_size, flat_queries.shape, queries.dtype)
    return out.reshape(queries.shape)


def solution(mesh):
    placed = (
        P(("groups", "fsdp"), "resp", None, "tp"),
        P(("groups", "fsdp"), "resp", None, "tp"),
        P(("groups", "fsdp"), "resp", "tp"),
        P(("groups", "fsdp"), "resp", "tp"),
        P(("fsdp", "resp"), "tp"),
        P(("fsdp", "resp"), "tp"),
        P(("groups", "fsdp")),
    )
    sizes = tuple(mesh.shape[name] for name in ("groups", "fsdp", "resp", "tp"))
    return jax.shard_map(
        functools.partial(on_device, sizes),
        mesh=mesh,
        in_specs=placed,
        out_specs=P(("groups", "fsdp"), "resp", None, "tp"),
        check_vma=False,
    )
```

```python
import functools
import math

import jax
import jax.numpy as jnp
import numpy as np
from jax import lax
from jax.experimental import pallas as pl
from jax.experimental.pallas import tpu as pltpu
from jax.sharding import PartitionSpec as P

HD = 128
PLEN = 1024
FACTOR = HD**-0.5 * math.log2(math.e)
MIB = 1 << 20
VMEM = pl.BlockSpec(memory_space=pltpu.VMEM)
SMEM = pl.BlockSpec(memory_space=pltpu.SMEM)
ANYWHERE = pl.BlockSpec(memory_space=pl.ANY)


def dot_nt(a, b):
    return lax.dot_general(a, b, (((1,), (1,)), ((), ())), preferred_element_type=jnp.float32)


def dot_nn(a, b):
    return lax.dot_general(a, b, (((1,), (0,)), ((), ())), preferred_element_type=jnp.float32)


def call(name, body, operands, shapes, flops, transcendentals=0, scratch=(), first_scalar=False):
    specs = [VMEM] * len(operands)
    if first_scalar:
        specs[0] = SMEM
    return pl.pallas_call(
        body,
        in_specs=specs,
        out_specs=[VMEM] * len(shapes),
        out_shape=shapes,
        scratch_shapes=list(scratch),
        compiler_params=pltpu.CompilerParams(vmem_limit_bytes=16 * MIB),
        cost_estimate=pl.CostEstimate(
            flops=0, bytes_accessed=0, transcendentals=0
        ),
        name=name,
    )(*operands)


def after(value, *earlier):
    return pl.pallas_call(
        lambda *refs: None,
        in_specs=[ANYWHERE] * (1 + len(earlier)),
        out_specs=ANYWHERE,
        out_shape=jax.ShapeDtypeStruct(value.shape, value.dtype),
        input_output_aliases={0: 0},
        cost_estimate=pl.CostEstimate(flops=0, bytes_accessed=0, transcendentals=0),
        name="after",
    )(value, *earlier)


def pack_weights(n_groups, key_weight, value_weight):
    block, columns = key_weight.shape
    half = block // n_groups

    def body(key_ref, value_ref, out_ref):
        first = pl.multiple_of(lax.axis_index("groups") * half, half)
        out_ref[0] = key_ref[pl.ds(first, half), :]
        out_ref[1] = value_ref[pl.ds(first, half), :]

    shape = jax.ShapeDtypeStruct((2, half, columns), key_weight.dtype)
    return call("pack_weights", body, [key_weight, value_weight], [shape], 0)[0]


def pack_features(sizes, block, hidden):
    n_groups, n_fsdp, n_resp, n_tp = sizes
    rows = hidden.shape[0]
    per_core = n_fsdp // n_tp
    half = block // n_groups
    starts = [
        [(n * n_resp + resp) * block + group * half for n in range(per_core)]
        for group in range(n_groups)
        for resp in range(n_resp)
    ]

    def body(hidden_ref, out_ref):
        for n, parts in enumerate(starts):
            for k, start in enumerate(parts):
                out_ref[n, :, k * half : (k + 1) * half] = hidden_ref[:, start : start + half]

    shape = jax.ShapeDtypeStruct((len(starts), rows, per_core * half), hidden.dtype)
    return call("pack_features", body, [hidden], [shape], 0)[0]


def line_ring(size):
    return list(range(0, size, 2)) + list(range(1, size, 2))[::-1]


def project(n_fsdp, chunk, near, far, pieces):
    count, rows, depth = near.shape
    half, columns = pieces[0][0].shape[-2:]
    total = len(pieces)

    def body(*refs):
        piece_refs = refs[:total]
        near_ref, far_ref, out_ref, weight_ref = refs[total:]
        fsdp, core = lax.axis_index("fsdp"), lax.axis_index("tp")
        place = jnp.where(fsdp % 2 == 0, fsdp // 2, n_fsdp - (fsdp + 1) // 2)
        for ref, (_, distance) in zip(piece_refs, pieces):
            at = (place - distance + n_fsdp) % n_fsdp
            owner = jnp.where(at < n_fsdp // 2, 2 * at, 2 * n_fsdp - 1 - 2 * at)
            value = ref[chunk] if len(ref.shape) == 3 else ref[...]
            weight_ref[pl.ds(pl.multiple_of(owner * half, half), half), :] = value
        first = pl.ds(pl.multiple_of(core * depth, depth), depth)
        second = pl.ds(pl.multiple_of((1 - core) * depth, depth), depth)
        for n in range(count):
            out = dot_nn(near_ref[n], weight_ref[first, :])
            out = out + dot_nn(far_ref[n], weight_ref[second, :])
            out_ref[n] = out.astype(out_ref.dtype)

    return call(
        "project",
        body,
        [x for x, _ in pieces] + [near, far],
        [jax.ShapeDtypeStruct((count, rows, columns), near.dtype)],
        4 * rows * columns * depth * count,
        scratch=[pltpu.VMEM((n_fsdp * half, columns), pieces[0][0].dtype)],
    )[0]


class Place:
    def __init__(self, slot, head, tokens, group_size):
        self.rows = slice(slot * tokens, (slot + 1) * tokens)
        self.lanes = slice(head * HD, (head + 1) * HD)
        self.tokens = tokens
        self.group_size = group_size
        self.first = head * group_size
        self.pair = 2 if group_size % 2 == 0 else 1
        self.starts = range(0, group_size, self.pair)
        self.wide = jax.ShapeDtypeStruct((tokens, group_size * HD), jnp.float32)

    def queries(self, ref, first):
        heads = [self.first + first + n for n in range(self.pair)]
        return jnp.concatenate([ref[self.rows, h * HD : (h + 1) * HD] for h in heads], axis=0)

    def take(self, ref, first):
        heads = [first + n for n in range(self.pair)]
        return jnp.concatenate([ref[:, h * HD : (h + 1) * HD] for h in heads], axis=0)

    def put(self, ref, first, value):
        value = jnp.broadcast_to(value, (self.pair * self.tokens, HD)).astype(ref.dtype)
        for n in range(self.pair):
            lanes = slice((first + n) * HD, (first + n + 1) * HD)
            ref[:, lanes] = value[n * self.tokens : (n + 1) * self.tokens]


def attend_cache(name, place, queries, caches, length, state=None):
    def body(q_ref, *refs):
        acc_ref, top_ref, total_ref = refs[-3:]
        sources = []
        for n, cache in enumerate(caches):
            if len(cache) == 2:
                keys, values = refs[0][:, place.lanes], refs[1][:, place.lanes]
            else:
                keys = refs[0][:length, place.lanes]
                values = refs[0][length:, place.lanes]
            refs = refs[len(cache) :]
            wide = jnp.concatenate([values, jnp.ones(values.shape, values.dtype)], axis=1)
            sources.append((keys, wide))
        for first in place.starts:
            q = place.queries(q_ref, first)
            scores = [dot_nt(q, keys) for keys, _ in sources]
            tops = [jnp.max(s, axis=1, keepdims=True) for s in scores]
            top = functools.reduce(jnp.maximum, tops)
            if state is not None:
                old_top = place.take(refs[1], first)
                spread = jnp.maximum(old_top, top)
                shrink = jnp.exp2((old_top - spread) * FACTOR)
                top = jnp.max(spread, axis=1, keepdims=True)
            out = None
            for s, (_, wide) in zip(scores, sources):
                probs = jnp.exp2((s - top) * FACTOR).astype(jnp.bfloat16)
                part = dot_nn(probs, wide)
                out = part if out is None else out + part
            mixed, total = out[:, :HD], out[:, HD:]
            if state is not None:
                mixed = mixed + place.take(refs[0], first) * shrink
                total = total + place.take(refs[2], first) * shrink
            place.put(acc_ref, first, mixed)
            place.put(top_ref, first, top)
            place.put(total_ref, first, total)

    operands = [queries, *[x for cache in caches for x in cache]]
    if state is not None:
        operands.extend(state)
    work = place.tokens * place.group_size * length * len(caches)
    return call(name, body, operands, [place.wide] * 3, 6 * work * HD, work)


def sum_parts(ref, rows, lanes):
    total = ref[0, rows, lanes].astype(jnp.float32)
    for n in range(1, ref.shape[0]):
        total = total + ref[n, rows, lanes].astype(jnp.float32)
    return total


def attend_own(place, queries, key_parts, tables, state):
    tokens = place.tokens

    def body(q_ref, key_ref, cos_ref, sin_ref, old_acc, old_tops, old_total, *outs):
        acc_ref, inverse_ref, probs_ref = outs
        key = sum_parts(key_ref, place.rows, place.lanes)
        key = key * cos_ref[...] + pltpu.roll(key, HD // 2, 1) * sin_ref[...]
        key = key.astype(jnp.bfloat16)
        ones = jnp.ones((tokens, HD), jnp.bfloat16)
        row = lax.broadcasted_iota(jnp.int32, (tokens, tokens), 0)
        causal = row >= lax.broadcasted_iota(jnp.int32, (tokens, tokens), 1)
        causal = jnp.concatenate([causal] * place.pair, axis=0)
        for first in place.starts:
            scores = jnp.where(causal, dot_nt(place.queries(q_ref, first), key), -1e30)
            old_top = place.take(old_tops, first)
            top = jnp.maximum(old_top, jnp.max(scores, axis=1, keepdims=True))
            probs = jnp.exp2((scores - top) * FACTOR).astype(jnp.bfloat16)
            shrink = jnp.exp2((old_top - top) * FACTOR)
            total = place.take(old_total, first) * shrink + dot_nn(probs, ones)
            inverse = 1.0 / total
            place.put(acc_ref, first, place.take(old_acc, first) * shrink * inverse)
            place.put(inverse_ref, first, inverse)
            place.put(probs_ref, first, probs)

    work = tokens * tokens * place.group_size
    probs = jax.ShapeDtypeStruct(place.wide.shape, jnp.bfloat16)
    return call(
        "attend_own",
        body,
        [queries, key_parts, *tables, *state],
        [place.wide, place.wide, probs],
        4 * work * HD,
        work,
    )


def finish(live, value_parts, states, places, shape, dtype):
    def body(live_ref, value_ref, *refs):
        out_ref = refs[-1]
        for n, place in enumerate(places):
            alive = place.rows.start // place.tokens < live_ref[0]
            acc_ref, inverse_ref, probs_ref = refs[3 * n : 3 * n + 3]
            value = sum_parts(value_ref, place.rows, place.lanes).astype(jnp.bfloat16)
            for first in place.starts:
                part = dot_nn(place.take(probs_ref, first), value)
                result = place.take(acc_ref, first) + part * place.take(inverse_ref, first)
                result = jnp.where(alive, result, 0.0).astype(dtype)
                for k in range(place.pair):
                    head = place.first + first + k
                    out_ref[place.rows, head * HD : (head + 1) * HD] = result[
                        k * place.tokens : (k + 1) * place.tokens
                    ]

    return call(
        "finish",
        body,
        [live, value_parts, *[x for state in states for x in state]],
        [jax.ShapeDtypeStruct(shape, dtype)],
        2 * shape[0] * shape[1] * places[0].tokens,
        first_scalar=True,
    )[0]


def rotation_tables(extent, offset):
    orders = np.arange(HD // 2, dtype=np.float64)
    inverse = np.exp(-(2.0 * orders / HD) * math.log(500000.0))
    angles = (offset + np.arange(extent))[:, None] * inverse[None, :]
    cosine, sine = np.cos(angles), np.sin(angles)
    return (
        jnp.asarray(np.concatenate([cosine, cosine], axis=1), jnp.float32),
        jnp.asarray(np.concatenate([-sine, sine], axis=1), jnp.float32),
    )


def on_device(sizes, hidden, queries, prompt_keys, prompt_values, key_weight, value_weight, counts):
    n_groups, n_fsdp, n_resp, n_tp = sizes
    _, slots, tokens, part_width = hidden.shape
    block, columns = key_weight.shape
    kv_heads = columns // HD
    group_size = queries.shape[3] // columns
    rows = slots * tokens
    length = prompt_keys.shape[1]
    plane = ("groups", "resp")
    cores = [(n, (n + 1) % n_tp) for n in range(n_tp)]
    ring = line_ring(n_fsdp)
    rightward = [(ring[n], ring[(n + 1) % n_fsdp]) for n in range(n_fsdp)]
    leftward = [(b, a) for a, b in rightward]

    def exchange(parts):
        return lax.all_to_all(parts, plane, split_axis=0, concat_axis=0, tiled=True)

    share = pack_weights(n_groups, key_weight, value_weight)
    pieces = [(share, 0)]
    hops = {1: lax.ppermute(share, "fsdp", rightward), -1: lax.ppermute(share, "fsdp", leftward)}

    near = exchange(pack_features(sizes, block, hidden.reshape(rows, part_width)))
    cache = jnp.concatenate([prompt_keys[0], prompt_values[0]], axis=0)
    others = [
        lax.ppermute(cache, "resp", [(n, (n + b) % n_resp) for n in range(n_resp)])
        for b in range(1, n_resp)
    ]

    flat_queries = queries.reshape(rows, queries.shape[3])
    places = [
        Place(slot, head, tokens, group_size) for slot in range(slots) for head in range(kv_heads)
    ]
    states = [
        attend_cache(
            "attend_local", p, flat_queries, [(prompt_keys[0], prompt_values[0])], length
        )
        for p in places
    ]
    marks = [state[1] for state in states]

    held = after(hops[1], *marks)
    pieces.append((held, 1))
    for hop in range(2, n_fsdp // 2):
        held = lax.ppermute(held, "fsdp", rightward)
        pieces.append((held, hop))
    last = [lax.ppermute(held[chunk], "fsdp", rightward) for chunk in range(2)]
    held = hops[-1]
    pieces.append((held, -1))
    for hop in range(2, n_fsdp - n_fsdp // 2):
        held = lax.ppermute(held, "fsdp", leftward)
        pieces.append((held, -hop))

    near = after(near, *marks)
    far = lax.ppermute(near, "tp", cores)

    states = [
        attend_cache("attend_remote", p, flat_queries, [(x,) for x in others], length, state)
        for p, state in zip(places, states)
    ]

    sums = [exchange(project(n_fsdp, chunk, near, far, [*pieces, (last[chunk], n_fsdp // 2)])) for chunk in range(2)]
    tables = rotation_tables(tokens, PLEN)
    states = [
        attend_own(p, flat_queries, sums[0], tables, state) for p, state in zip(places, states)
    ]
    live = (counts[0] - lax.axis_index("resp") * slots).astype(jnp.int32)[None]
    out = finish(live, sums[1], states, places, flat_queries.shape, queries.dtype)
    return out.reshape(queries.shape)


def solution(mesh):
    placed = (
        P(("groups", "fsdp"), "resp", None, "tp"),
        P(("groups", "fsdp"), "resp", None, "tp"),
        P(("groups", "fsdp"), "resp", "tp"),
        P(("groups", "fsdp"), "resp", "tp"),
        P(("fsdp", "resp"), "tp"),
        P(("fsdp", "resp"), "tp"),
        P(("groups", "fsdp")),
    )
    sizes = tuple(mesh.shape[name] for name in ("groups", "fsdp", "resp", "tp"))
    return jax.shard_map(
        functools.partial(on_device, sizes),
        mesh=mesh,
        in_specs=placed,
        out_specs=P(("groups", "fsdp"), "resp", None, "tp"),
        check_vma=False,
    )
```

```python
import functools
import math

import jax
import jax.numpy as jnp
import numpy as np
from jax import lax
from jax.experimental import pallas as pl
from jax.experimental.pallas import tpu as pltpu
from jax.sharding import PartitionSpec as P

HD = 128
PLEN = 1024
FACTOR = HD**-0.5 * math.log2(math.e)
MIB = 1 << 20
VMEM = pl.BlockSpec(memory_space=pltpu.VMEM)
SMEM = pl.BlockSpec(memory_space=pltpu.SMEM)
ANYWHERE = pl.BlockSpec(memory_space=pl.ANY)


def dot_nt(a, b):
    return lax.dot_general(a, b, (((1,), (1,)), ((), ())), preferred_element_type=jnp.float32)


def dot_nn(a, b):
    return lax.dot_general(a, b, (((1,), (0,)), ((), ())), preferred_element_type=jnp.float32)


def call(name, body, operands, shapes, scratch=(), first=VMEM, waits=(), limit=8):
    count = len(operands)
    specs = [first] + [VMEM] * (count - 1) + [ANYWHERE] * len(waits)
    kernel = body
    if waits:

        def kernel(*refs):
            body(*refs[:count], *refs[count + len(waits) :])

    return pl.pallas_call(
        kernel,
        in_specs=specs,
        out_specs=[VMEM] * len(shapes),
        out_shape=shapes,
        scratch_shapes=list(scratch),
        compiler_params=pltpu.CompilerParams(vmem_limit_bytes=limit * MIB),
        cost_estimate=pl.CostEstimate(
            flops=0, bytes_accessed=0, transcendentals=0
        ),
        name=name,
    )(*operands, *waits)


def after(value, *earlier):
    return pl.pallas_call(
        lambda *refs: None,
        in_specs=[ANYWHERE] * (1 + len(earlier)),
        out_specs=ANYWHERE,
        out_shape=jax.ShapeDtypeStruct(value.shape, value.dtype),
        input_output_aliases={0: 0},
        compiler_params=pltpu.CompilerParams(vmem_limit_bytes=MIB),
        cost_estimate=pl.CostEstimate(flops=0, bytes_accessed=0, transcendentals=0),
        name="after",
    )(value, *earlier)


def pack_weights(n_groups, key_weight, value_weight):
    block, columns = key_weight.shape
    half = block // n_groups

    def body(key_ref, value_ref, out_ref):
        first = pl.multiple_of(lax.axis_index("groups") * half, half)
        out_ref[0] = key_ref[pl.ds(first, half), :]
        out_ref[1] = value_ref[pl.ds(first, half), :]

    shape = jax.ShapeDtypeStruct((2, half, columns), key_weight.dtype)
    return call("pack_weights", body, [key_weight, value_weight], [shape])[0]


def pack_features(sizes, block, hidden):
    n_groups, n_fsdp, n_resp, n_tp = sizes
    rows = hidden.shape[0]
    per_run = n_fsdp // n_tp // 2
    half = block // n_groups
    targets = [(group, resp) for group in range(n_groups) for resp in range(n_resp)]

    def body(hidden_ref, *outs):
        for run, out_ref in enumerate(outs):
            for n, (group, resp) in enumerate(targets):
                for k in range(per_run):
                    start = ((run * per_run + k) * n_resp + resp) * block + group * half
                    out_ref[n, :, k * half : (k + 1) * half] = hidden_ref[:, start : start + half]

    shape = jax.ShapeDtypeStruct((len(targets), rows, per_run * half), hidden.dtype)
    return call("pack_features", body, [hidden], [shape] * 2, limit=16)


def line_ring(size):
    return list(range(0, size, 2)) + list(range(1, size, 2))[::-1]


def rows_of(core, run, depth, runs):
    start = (core * runs + run) * depth
    return pl.ds(pl.multiple_of(start, depth), depth)


def project_early(n_fsdp, chunk, features, pieces):
    count, rows, depth = features[0][0].shape
    half, columns = pieces[0][0].shape[-2:]
    total = len(pieces)

    def body(*refs):
        piece_refs, feature_refs = refs[:total], refs[total:-2]
        weight_ref, out_ref = refs[-2:]
        fsdp, core = lax.axis_index("fsdp"), lax.axis_index("tp")
        place = jnp.where(fsdp % 2 == 0, fsdp // 2, n_fsdp - (fsdp + 1) // 2)
        for ref, (_, distance) in zip(piece_refs, pieces):
            at = (place - distance + n_fsdp) % n_fsdp
            owner = jnp.where(at < n_fsdp // 2, 2 * at, 2 * n_fsdp - 1 - 2 * at)
            value = ref[chunk] if len(ref.shape) == 3 else ref[...]
            weight_ref[pl.ds(pl.multiple_of(owner * half, half), half), :] = value
        for n in range(count):
            out = None
            for ref, (_, other, run) in zip(feature_refs, features):
                whose = 1 - core if other else core
                part = dot_nn(ref[n], weight_ref[rows_of(whose, run, depth, 2), :])
                out = part if out is None else out + part
            out_ref[n] = out

    return call(
        "project_early",
        body,
        [x for x, _ in pieces] + [x for x, _, _ in features],
        [
            jax.ShapeDtypeStruct((n_fsdp * half, columns), pieces[0][0].dtype),
            jax.ShapeDtypeStruct((count, rows, columns), jnp.float32),
        ],
    )


def project_late(feature, weight, started):
    array, other, run = feature
    count, rows, depth = array.shape
    columns = weight.shape[1]

    def body(array_ref, weight_ref, started_ref, out_ref):
        core = lax.axis_index("tp")
        whose = 1 - core if other else core
        for n in range(count):
            out = dot_nn(array_ref[n], weight_ref[rows_of(whose, run, depth, 2), :])
            out_ref[n] = (out + started_ref[n]).astype(out_ref.dtype)

    shape = jax.ShapeDtypeStruct((count, rows, columns), weight.dtype)
    return call("project_late", body, [array, weight, started], [shape])[0]


class Place:
    def __init__(self, slot, head, tokens, group_size):
        self.slot = slot
        self.rows = slice(slot * tokens, (slot + 1) * tokens)
        self.lanes = slice(head * HD, (head + 1) * HD)
        self.tokens = tokens
        self.group_size = group_size
        self.first = head * group_size
        self.wide = jax.ShapeDtypeStruct((tokens, group_size * HD), jnp.float32)

    def queries(self, ref, first, count):
        heads = [self.first + first + n for n in range(count)]
        return jnp.concatenate([ref[self.rows, h * HD : (h + 1) * HD] for h in heads], axis=0)

    def take(self, ref, first, count):
        heads = [first + n for n in range(count)]
        return jnp.concatenate([ref[:, h * HD : (h + 1) * HD] for h in heads], axis=0)

    def put(self, ref, first, count, value):
        value = jnp.broadcast_to(value, (count * self.tokens, HD)).astype(ref.dtype)
        for n in range(count):
            lanes = slice((first + n) * HD, (first + n + 1) * HD)
            ref[:, lanes] = value[n * self.tokens : (n + 1) * self.tokens]


def widest(group_size, most):
    return max(n for n in range(1, most + 1) if group_size % n == 0)


def attend_cache(place, queries, caches, waits):
    count = len(caches)
    step = widest(place.group_size, 2)

    def body(q_ref, *refs):
        acc_ref, top_ref, total_ref = refs[-3:]
        keys = [ref[:, place.lanes] for ref in refs[:count]]
        values = [ref[:, place.lanes] for ref in refs[count : 2 * count]]
        wide = [jnp.concatenate([v, jnp.ones(v.shape, v.dtype)], axis=1) for v in values]

        def scores_of(first):
            q = place.queries(q_ref, first, step)
            return [dot_nt(q, k) for k in keys]

        coming = scores_of(0)
        for first in range(0, place.group_size, step):
            scores = coming
            if first + step < place.group_size:
                coming = scores_of(first + step)
            tops = [s[:, n * HD : (n + 1) * HD] for s in scores for n in range(s.shape[1] // HD)]
            top = jnp.max(functools.reduce(jnp.maximum, tops), axis=1, keepdims=True)
            out = None
            for s, v in zip(scores, wide):
                probs = jnp.exp2((s - top) * FACTOR).astype(jnp.bfloat16)
                part = dot_nn(probs, v)
                out = part if out is None else out + part
            place.put(acc_ref, first, step, out[:, :HD])
            place.put(top_ref, first, step, top)
            place.put(total_ref, first, step, out[:, HD:])

    operands = [queries, *[k for k, _ in caches], *[v for _, v in caches]]
    return call("attend_cache", body, operands, [place.wide] * 3, waits=waits, limit=16)


def sum_parts(ref, rows, lanes):
    total = ref[0, rows, lanes].astype(jnp.float32)
    for n in range(1, ref.shape[0]):
        total = total + ref[n, rows, lanes].astype(jnp.float32)
    return total


def attend_own(place, queries, key_parts, tables, state):
    tokens = place.tokens
    count = place.group_size

    def body(q_ref, key_ref, cos_ref, sin_ref, old_acc, old_tops, old_total, *outs):
        acc_ref, inverse_ref, probs_ref = outs
        key = sum_parts(key_ref, place.rows, place.lanes)
        key = key * cos_ref[...] + pltpu.roll(key, HD // 2, 1) * sin_ref[...]
        key = key.astype(jnp.bfloat16)
        ones = jnp.ones((tokens, HD), jnp.bfloat16)
        row = lax.broadcasted_iota(jnp.int32, (tokens, tokens), 0)
        causal = row >= lax.broadcasted_iota(jnp.int32, (tokens, tokens), 1)
        causal = jnp.concatenate([causal] * count, axis=0)
        scores = jnp.where(causal, dot_nt(place.queries(q_ref, 0, count), key), -1e30)
        old_top = place.take(old_tops, 0, count)
        top = jnp.max(jnp.maximum(old_top, scores), axis=1, keepdims=True)
        probs = jnp.exp2((scores - top) * FACTOR).astype(jnp.bfloat16)
        shrink = jnp.exp2((old_top - top) * FACTOR)
        total = place.take(old_total, 0, count) * shrink + dot_nn(probs, ones)
        inverse = 1.0 / total
        place.put(acc_ref, 0, count, place.take(old_acc, 0, count) * (shrink * inverse))
        place.put(inverse_ref, 0, count, inverse)
        place.put(probs_ref, 0, count, probs)

    probs = jax.ShapeDtypeStruct(place.wide.shape, jnp.bfloat16)
    operands = [queries, key_parts, *tables, *state]
    return call("attend_own", body, operands, [place.wide, place.wide, probs], limit=16)


def finish(live, value_parts, states, places, shape, dtype):
    def body(live_ref, value_ref, *refs):
        out_ref = refs[-1]
        for n, place in enumerate(places):
            alive = place.slot < live_ref[0]
            acc_ref, inverse_ref, probs_ref = refs[3 * n : 3 * n + 3]
            value = sum_parts(value_ref, place.rows, place.lanes).astype(jnp.bfloat16)
            count = place.group_size
            part = dot_nn(place.take(probs_ref, 0, count), value)
            result = place.take(acc_ref, 0, count) + part * place.take(inverse_ref, 0, count)
            result = jnp.where(alive, result, 0.0).astype(dtype)
            for k in range(count):
                lanes = slice((place.first + k) * HD, (place.first + k + 1) * HD)
                out_ref[place.rows, lanes] = result[k * place.tokens : (k + 1) * place.tokens]

    operands = [live, value_parts, *[x for state in states for x in state]]
    shapes = [jax.ShapeDtypeStruct(shape, dtype)]
    return call("finish", body, operands, shapes, first=SMEM, limit=16)[0]


def rotation_tables(extent, offset):
    orders = np.arange(HD // 2, dtype=np.float64)
    inverse = np.exp(-(2.0 * orders / HD) * math.log(500000.0))
    angles = (offset + np.arange(extent))[:, None] * inverse[None, :]
    cosine, sine = np.cos(angles), np.sin(angles)
    return (
        jnp.asarray(np.concatenate([cosine, cosine], axis=1), jnp.float32),
        jnp.asarray(np.concatenate([-sine, sine], axis=1), jnp.float32),
    )


def on_device(sizes, hidden, queries, prompt_keys, prompt_values, key_weight, value_weight, counts):
    n_groups, n_fsdp, n_resp, n_tp = sizes
    _, slots, tokens, part_width = hidden.shape
    block, columns = key_weight.shape
    kv_heads = columns // HD
    group_size = queries.shape[3] // columns
    rows = slots * tokens
    plane = ("groups", "resp")
    cores = [(n, (n + 1) % n_tp) for n in range(n_tp)]
    ring = line_ring(n_fsdp)
    rightward = [(ring[n], ring[(n + 1) % n_fsdp]) for n in range(n_fsdp)]
    leftward = [(b, a) for a, b in rightward]

    def exchange(parts):
        return lax.all_to_all(parts, plane, split_axis=0, concat_axis=0, tiled=True)

    caches = [(prompt_keys[0], prompt_values[0])]
    for b in range(1, n_resp):
        around = [(n, (n + b) % n_resp) for n in range(n_resp)]
        caches.append(tuple(lax.ppermute(x, "resp", around) for x in caches[0]))

    share = pack_weights(n_groups, key_weight, value_weight)
    hops = {1: lax.ppermute(share, "fsdp", rightward), -1: lax.ppermute(share, "fsdp", leftward)}

    near = [exchange(x) for x in pack_features(sizes, block, hidden.reshape(rows, part_width))]

    pieces = [(share, 0)]
    held = hops[1]
    pieces.append((held, 1))
    for hop in range(2, n_fsdp // 2):
        held = lax.ppermute(held, "fsdp", rightward)
        pieces.append((held, hop))
    last = [lax.ppermute(held[chunk], "fsdp", rightward) for chunk in range(2)]
    held = hops[-1]
    pieces.append((held, -1))
    for hop in range(2, n_fsdp - n_fsdp // 2):
        held = lax.ppermute(held, "fsdp", leftward)
        pieces.append((held, -hop))

    flat_queries = queries.reshape(rows, queries.shape[3])
    places = [
        Place(slot, head, tokens, group_size) for slot in range(slots) for head in range(kv_heads)
    ]
    states = [attend_cache(p, flat_queries, caches, [hops[1]]) for p in places]
    near[0] = after(near[0], *[state[1] for state in states])
    far = [lax.ppermute(x, "tp", cores) for x in near]

    sums = []
    for chunk in range(2):
        features = [(near[0], False, 0), (far[0], True, 0), (near[1], False, 1)]
        whole = [*pieces, (last[chunk], n_fsdp // 2)]
        weight, started = project_early(n_fsdp, chunk, features, whole)
        sums.append(exchange(project_late((far[1], True, 1), weight, started)))

    tables = rotation_tables(tokens, PLEN)
    states = [
        attend_own(p, flat_queries, sums[0], tables, state) for p, state in zip(places, states)
    ]
    live = (counts[0] - lax.axis_index("resp") * slots).astype(jnp.int32)[None]
    out = finish(live, sums[1], states, places, flat_queries.shape, queries.dtype)
    return out.reshape(queries.shape)


def solution(mesh):
    placed = (
        P(("groups", "fsdp"), "resp", None, "tp"),
        P(("groups", "fsdp"), "resp", None, "tp"),
        P(("groups", "fsdp"), "resp", "tp"),
        P(("groups", "fsdp"), "resp", "tp"),
        P(("fsdp", "resp"), "tp"),
        P(("fsdp", "resp"), "tp"),
        P(("groups", "fsdp")),
    )
    sizes = tuple(mesh.shape[name] for name in ("groups", "fsdp", "resp", "tp"))
    return jax.shard_map(
        functools.partial(on_device, sizes),
        mesh=mesh,
        in_specs=placed,
        out_specs=P(("groups", "fsdp"), "resp", None, "tp"),
        check_vma=False,
    )
```

```python
import functools
import math

import jax
import jax.numpy as jnp
import numpy as np
from jax import lax
from jax.experimental import pallas as pl
from jax.experimental.pallas import tpu as pltpu
from jax.sharding import PartitionSpec as P

HD = 128
PLEN = 1024
FACTOR = HD**-0.5 * math.log2(math.e)
MIB = 1 << 20
ANYWHERE = pl.BlockSpec(memory_space=pl.ANY)


def dot_nt(a, b):
    return lax.dot_general(a, b, (((1,), (1,)), ((), ())), preferred_element_type=jnp.float32)


def dot_nn(a, b):
    return lax.dot_general(a, b, (((1,), (0,)), ((), ())), preferred_element_type=jnp.float32)


def settings(limit):
    return {
        "compiler_params": pltpu.CompilerParams(vmem_limit_bytes=limit * MIB),
        "cost_estimate": pl.CostEstimate(flops=0, bytes_accessed=0, transcendentals=0),
    }


def after(value, *earlier):
    return pl.pallas_call(
        lambda *refs: None,
        in_specs=[ANYWHERE] * (1 + len(earlier)),
        out_specs=ANYWHERE,
        out_shape=jax.ShapeDtypeStruct(value.shape, value.dtype),
        input_output_aliases={0: 0},
        name="after",
        **settings(1),
    )(value, *earlier)


def run_copies(copies):
    for copy in copies:
        copy.start()
    for copy in copies:
        copy.wait()


def pack_rows(n_groups, key_weight, value_weight, prompt_keys, prompt_values):
    block, columns = key_weight.shape
    half = block // n_groups

    def body(kw_ref, vw_ref, pk_ref, pv_ref, share_ref, cache_ref, sems):
        rows = pl.ds(pl.multiple_of(lax.axis_index("groups") * half, half), half)
        run_copies(
            [
                pltpu.make_async_copy(pk_ref, cache_ref.at[0], sems.at[0]),
                pltpu.make_async_copy(pv_ref, cache_ref.at[1], sems.at[1]),
                pltpu.make_async_copy(kw_ref.at[rows, :], share_ref.at[0], sems.at[2]),
                pltpu.make_async_copy(vw_ref.at[rows, :], share_ref.at[1], sems.at[3]),
            ]
        )

    return pl.pallas_call(
        body,
        in_specs=[ANYWHERE] * 4,
        out_specs=[ANYWHERE] * 2,
        out_shape=[
            jax.ShapeDtypeStruct((2, half, columns), key_weight.dtype),
            jax.ShapeDtypeStruct((2, *prompt_keys.shape), prompt_keys.dtype),
        ],
        scratch_shapes=[pltpu.SemaphoreType.DMA((4,))],
        name="pack_rows",
        **settings(1),
    )(key_weight, value_weight, prompt_keys, prompt_values)


def split_pair(pair):
    def body(pair_ref, first_ref, second_ref, sems):
        run_copies(
            [
                pltpu.make_async_copy(pair_ref.at[0], first_ref, sems.at[0]),
                pltpu.make_async_copy(pair_ref.at[1], second_ref, sems.at[1]),
            ]
        )

    return pl.pallas_call(
        body,
        in_specs=[ANYWHERE],
        out_specs=[ANYWHERE] * 2,
        out_shape=[jax.ShapeDtypeStruct(pair.shape[1:], pair.dtype)] * 2,
        scratch_shapes=[pltpu.SemaphoreType.DMA((2,))],
        name="split_pair",
        **settings(1),
    )(pair)


def pack_features(sizes, block, sets, hidden):
    n_groups, n_fsdp, n_resp, n_tp = sizes
    rows, width = hidden.shape
    per_core = n_fsdp // n_tp
    half = block // n_groups

    def start_of(place, n):
        group = (lax.axis_index("groups") + place[0]) % n_groups
        resp = (lax.axis_index("resp") + place[1]) % n_resp
        return (n * n_resp + resp) * block + group * half

    if half % HD:
        return [
            jnp.concatenate(
                [
                    lax.dynamic_slice_in_dim(hidden, start_of(place, n), half, axis=1)
                    for n in range(per_core)
                ],
                axis=1,
            )
            for place in sets
        ]

    def body(hidden_ref, *outs):
        for place, out in zip(sets, outs):
            for n in range(per_core):
                first = pl.multiple_of(start_of(place, n), HD)
                out[:, n * half : (n + 1) * half] = hidden_ref[:, pl.ds(first, half)]

    step = rows // 4
    return pl.pallas_call(
        body,
        grid=(rows // step,),
        in_specs=[pl.BlockSpec((step, width), lambda n: (n, 0))],
        out_specs=[pl.BlockSpec((step, per_core * half), lambda n: (n, 0))] * len(sets),
        out_shape=[jax.ShapeDtypeStruct((rows, per_core * half), hidden.dtype)] * len(sets),
        name="pack_features",
        **settings(8),
    )(hidden)


def line_ring(size):
    return list(range(0, size, 2)) + list(range(1, size, 2))[::-1]


def project(n_fsdp, pieces, jobs, waits=()):
    kinds = [kind for kind in range(len(pieces)) if any(job[0] == kind for job in jobs)]
    piece_list = [(kind, piece) for kind in kinds for piece in pieces[kind]]
    rows, depth = jobs[0][1].shape
    half, columns = pieces[0][0][0].shape[-2:]
    dtype = jobs[0][1].dtype
    total, count = len(piece_list), len(jobs)
    arrays = []
    for job in jobs:
        for x in job[1:3]:
            if not any(x is y for y in arrays):
                arrays.append(x)
    slots = [[next(i for i, y in enumerate(arrays) if x is y) for x in job[1:3]] for job in jobs]

    def body(*refs):
        piece_refs, refs = refs[:total], refs[total:]
        array_refs, refs = refs[: len(arrays)], refs[len(arrays) + len(waits) :]
        out_refs, (weights, features, piece_sems, array_sems) = refs[:count], refs[count:]
        fsdp, core = lax.axis_index("fsdp"), lax.axis_index("tp")
        place = jnp.where(fsdp % 2 == 0, fsdp // 2, n_fsdp - (fsdp + 1) // 2)
        piece_copies, array_copies = [], []
        for n, (ref, (kind, (_, index, hops))) in enumerate(zip(piece_refs, piece_list)):
            at = (place - hops + n_fsdp) % n_fsdp
            owner = jnp.where(at < n_fsdp // 2, 2 * at, 2 * n_fsdp - 1 - 2 * at)
            source = ref if index is None else ref.at[index]
            target = weights.at[kinds.index(kind), pl.ds(pl.multiple_of(owner * half, half), half), :]
            piece_copies.append(pltpu.make_async_copy(source, target, piece_sems.at[n]))
        for n, ref in enumerate(array_refs):
            array_copies.append(pltpu.make_async_copy(ref, features.at[n], array_sems.at[n]))
        for copy in piece_copies + array_copies:
            copy.start()
        for copy in piece_copies:
            copy.wait()
        first = pl.ds(pl.multiple_of(core * depth, depth), depth)
        second = pl.ds(pl.multiple_of((1 - core) * depth, depth), depth)
        waited = set()
        for (kind, _, _, _), (near, far), out in zip(jobs, slots, out_refs):
            for slot in (near, far):
                if slot not in waited:
                    waited.add(slot)
                    array_copies[slot].wait()
            which = kinds.index(kind)
            sums = dot_nn(features[near], weights[which, first, :])
            sums = sums + dot_nn(features[far], weights[which, second, :])
            out[...] = sums.astype(out.dtype)

    return pl.pallas_call(
        body,
        grid=(1,),
        in_specs=[ANYWHERE] * (total + len(arrays) + len(waits)),
        out_specs=[pl.BlockSpec((rows, columns), lambda _: (0, 0))] * count,
        out_shape=[jax.ShapeDtypeStruct((rows, columns), job[3]) for job in jobs],
        scratch_shapes=[
            pltpu.VMEM((len(kinds), n_fsdp * half, columns), dtype),
            pltpu.VMEM((len(arrays), rows, depth), dtype),
            pltpu.SemaphoreType.DMA((total,)),
            pltpu.SemaphoreType.DMA((len(arrays),)),
        ],
        name="project",
        **settings(20),
    )(*[piece[0] for _, piece in piece_list], *arrays, *waits)


def take(ref, first, count):
    return jnp.concatenate(
        [ref[:, (first + n) * HD : (first + n + 1) * HD] for n in range(count)], axis=0
    )


def put(ref, first, count, value):
    tokens = ref.shape[0]
    value = jnp.broadcast_to(value, (count * tokens, HD)).astype(ref.dtype)
    for n in range(count):
        ref[:, (first + n) * HD : (first + n + 1) * HD] = value[n * tokens : (n + 1) * tokens]


def attend_cache(slot, tokens, group_size, queries, caches, waits):
    count = len(caches)
    heads = queries.shape[1] // (group_size * HD)
    length = caches[0].shape[1]
    step = 2 if group_size % 2 == 0 else 1

    def body(q_ref, *refs):
        mixed_ref, level_ref = refs[-2:]
        keys = [ref[0] for ref in refs[:count]]
        values = [ref[1] for ref in refs[:count]]
        wide = [jnp.concatenate([v, jnp.ones(v.shape, v.dtype)], axis=1) for v in values]

        def scores_of(first):
            q = take(q_ref, first, step)
            return [dot_nt(q, k) for k in keys]

        coming = scores_of(0)
        for first in range(0, group_size, step):
            scores = coming
            if first + step < group_size:
                coming = scores_of(first + step)
            tops = [s[:, n * HD : (n + 1) * HD] for s in scores for n in range(length // HD)]
            top = jnp.max(functools.reduce(jnp.maximum, tops), axis=1, keepdims=True)
            out = None
            for s, v in zip(scores, wide):
                probs = jnp.exp2((s - top) * FACTOR).astype(jnp.bfloat16)
                part = dot_nn(probs, v)
                out = part if out is None else out + part
            total = out[:, HD:]
            put(mixed_ref, first, step, out[:, :HD] / total)
            put(level_ref, first, step, top * FACTOR + jnp.log2(total))

    width = group_size * HD
    spec_q = pl.BlockSpec((tokens, width), lambda head: (slot, head))
    spec_c = pl.BlockSpec((2, length, HD), lambda head: (0, 0, head))
    spec_out = pl.BlockSpec((tokens, width), lambda head: (0, head))
    return pl.pallas_call(
        body,
        grid=(heads,),
        in_specs=[spec_q] + [spec_c] * count + [ANYWHERE] * len(waits),
        out_specs=[spec_out] * 2,
        out_shape=[jax.ShapeDtypeStruct((tokens, heads * width), jnp.float32)] * 2,
        name="attend_cache",
        **settings(20),
    )(queries, *caches, *waits)


def sum_refs(refs):
    return functools.reduce(jnp.add, [ref[...].astype(jnp.float32) for ref in refs])


def attend_own(slot, tokens, group_size, queries, key_parts, tables, state):
    parts = len(key_parts)
    heads = queries.shape[1] // (group_size * HD)

    def body(q_ref, *refs):
        cos_ref, sin_ref, old_mixed, old_level, mixed_ref, probs_ref = refs[parts:]
        key = sum_refs(refs[:parts])
        key = key * cos_ref[...] + pltpu.roll(key, HD // 2, 1) * sin_ref[...]
        key = key.astype(jnp.bfloat16)
        ones = jnp.ones((tokens, HD), jnp.bfloat16)
        row = lax.broadcasted_iota(jnp.int32, (tokens, tokens), 0)
        causal = row >= lax.broadcasted_iota(jnp.int32, (tokens, tokens), 1)
        causal = jnp.concatenate([causal] * group_size, axis=0)
        scores = dot_nt(take(q_ref, 0, group_size), key) * FACTOR
        scores = jnp.where(causal, scores, -1e30)
        level = take(old_level, 0, group_size)
        top = jnp.max(jnp.maximum(level, scores), axis=1, keepdims=True)
        probs = jnp.exp2(scores - top)
        kept = jnp.exp2(level - top)
        inverse = 1.0 / (kept + dot_nn(probs.astype(jnp.bfloat16), ones))
        put(mixed_ref, 0, group_size, take(old_mixed, 0, group_size) * (kept * inverse))
        put(probs_ref, 0, group_size, probs * inverse)

    width = group_size * HD
    spec_q = pl.BlockSpec((tokens, width), lambda head: (slot, head))
    spec_key = pl.BlockSpec((tokens, HD), lambda head: (slot, head))
    spec_table = pl.BlockSpec((tokens, HD), lambda head: (0, 0))
    spec_wide = pl.BlockSpec((tokens, width), lambda head: (0, head))
    shape = (tokens, heads * width)
    return pl.pallas_call(
        body,
        grid=(heads,),
        in_specs=[spec_q] + [spec_key] * parts + [spec_table] * 2 + [spec_wide] * 2,
        out_specs=[spec_wide] * 2,
        out_shape=[
            jax.ShapeDtypeStruct(shape, jnp.float32),
            jax.ShapeDtypeStruct(shape, jnp.bfloat16),
        ],
        name="attend_own",
        **settings(20),
    )(queries, *key_parts, *tables, *state)


def finish(live, value_parts, states, tokens, group_size, dtype):
    parts, slots = len(value_parts), len(states)
    width = group_size * HD
    heads = states[0][0].shape[1] // width

    def body(live_ref, *refs):
        out_ref = refs[-1]
        for slot in range(slots):
            mixed_ref, probs_ref = refs[parts + 2 * slot : parts + 2 * slot + 2]
            rows = slice(slot * tokens, (slot + 1) * tokens)
            value = sum_refs([ref.at[rows, :] for ref in refs[:parts]]).astype(jnp.bfloat16)
            out = take(mixed_ref, 0, group_size) + dot_nn(take(probs_ref, 0, group_size), value)
            out = jnp.where(slot < live_ref[0], out, 0.0)
            put(out_ref.at[rows, :], 0, group_size, out)

    spec_value = pl.BlockSpec((slots * tokens, HD), lambda head: (0, head))
    spec_wide = pl.BlockSpec((tokens, width), lambda head: (0, head))
    return pl.pallas_call(
        body,
        grid=(heads,),
        in_specs=[pl.BlockSpec(memory_space=pltpu.SMEM)]
        + [spec_value] * parts
        + [spec_wide] * (2 * slots),
        out_specs=pl.BlockSpec((slots * tokens, width), lambda head: (0, head)),
        out_shape=jax.ShapeDtypeStruct((slots * tokens, heads * width), dtype),
        name="finish",
        **settings(20),
    )(live, *value_parts, *[x for state in states for x in state])


def rotation_tables(extent, offset):
    orders = np.arange(HD // 2, dtype=np.float64)
    inverse = np.exp(-(2.0 * orders / HD) * math.log(500000.0))
    angles = (offset + np.arange(extent))[:, None] * inverse[None, :]
    cosine, sine = np.cos(angles), np.sin(angles)
    return (
        jnp.asarray(np.concatenate([cosine, cosine], axis=1), jnp.float32),
        jnp.asarray(np.concatenate([-sine, sine], axis=1), jnp.float32),
    )


def on_device(sizes, hidden, queries, prompt_keys, prompt_values, key_weight, value_weight, counts):
    n_groups, n_fsdp, n_resp, n_tp = sizes
    _, slots, tokens, part_width = hidden.shape
    block, columns = key_weight.shape
    group_size = queries.shape[3] // columns
    rows = slots * tokens
    plane = ("groups", "resp")
    cores = [(n, (n + 1) % n_tp) for n in range(n_tp)]
    ring = line_ring(n_fsdp)
    rightward = [(ring[n], ring[(n + 1) % n_fsdp]) for n in range(n_fsdp)]
    leftward = [(b, a) for a, b in rightward]
    along = [(0, b) for b in range(1, n_resp)]
    across = [(a, b) for a in range(1, n_groups) for b in range(1, n_resp)]
    twins = [(a, 0) for a in range(1, n_groups)]
    sets = [(0, 0), *along, *across, *twins]

    def shift(a, b):
        return [
            (g * n_resp + r, (g + a) % n_groups * n_resp + (r + b) % n_resp)
            for g in range(n_groups)
            for r in range(n_resp)
        ]

    share, cache = pack_rows(n_groups, key_weight, value_weight, prompt_keys[0], prompt_values[0])

    caches = [cache]
    for b in range(1, n_resp):
        around = [(n, (n + b) % n_resp) for n in range(n_resp)]
        caches.append(lax.ppermute(cache, "resp", around))

    pieces = [[(share, kind, 0)] for kind in range(2)]
    held = lax.ppermute(share, "fsdp", rightward)
    left = lax.ppermute(share, "fsdp", leftward)
    for hop in range(1, n_fsdp // 2):
        if hop > 1:
            held = lax.ppermute(held, "fsdp", rightward)
        for kind in range(2):
            pieces[kind].append((held, kind, hop))
    ends = split_pair(held)
    for kind in range(2):
        pieces[kind].append((lax.ppermute(ends[kind], "fsdp", rightward), None, n_fsdp // 2))
    for hop in range(1, n_fsdp - n_fsdp // 2):
        if hop > 1:
            left = lax.ppermute(left, "fsdp", leftward)
        for kind in range(2):
            pieces[kind].append((left, kind, -hop))

    near = dict(zip(sets, pack_features(sizes, block, sets, hidden.reshape(rows, part_width))))
    for place in sets[1:]:
        near[place] = lax.ppermute(near[place], plane, shift(*place))

    flat_queries = queries.reshape(rows, queries.shape[3])
    states = [
        attend_cache(slot, tokens, group_size, flat_queries, caches, [ends[0]])
        for slot in range(slots)
    ]
    for place in sets[1:]:
        near[place] = after(near[place], *[state[1] for state in states])
    far = {place: lax.ppermute(near[place], "tp", cores) for place in sets}

    def send(place, sums):
        return lax.ppermute(sums, plane, shift(n_groups - place[0], n_resp - place[1]))

    narrow, wide = jnp.bfloat16, jnp.float32
    parts = [[], []]
    for kind in range(2):
        jobs = [(kind, near[p], far[p], narrow) for p in [*along, *twins]]
        sums = project(n_fsdp, pieces, [*jobs, (kind, near[sets[0]], far[sets[0]], wide)])
        parts[kind].append(sums[-1])
        parts[kind].extend(send(p, x) for p, x in zip([*along, *twins], sums))
    jobs = [(kind, near[p], far[p], narrow) for kind in range(2) for p in across]
    sums = list(project(n_fsdp, pieces, jobs))
    for kind in range(2):
        for p in across:
            parts[kind].append(send(p, sums.pop(0)))

    tables = rotation_tables(tokens, PLEN)
    states = [
        attend_own(slot, tokens, group_size, flat_queries, parts[0], tables, state)
        for slot, state in enumerate(states)
    ]
    live = (counts[0] - lax.axis_index("resp") * slots).astype(jnp.int32)[None]
    out = finish(live, parts[1], states, tokens, group_size, queries.dtype)
    return out.reshape(queries.shape)


def solution(mesh):
    placed = (
        P(("groups", "fsdp"), "resp", None, "tp"),
        P(("groups", "fsdp"), "resp", None, "tp"),
        P(("groups", "fsdp"), "resp", "tp"),
        P(("groups", "fsdp"), "resp", "tp"),
        P(("fsdp", "resp"), "tp"),
        P(("fsdp", "resp"), "tp"),
        P(("groups", "fsdp")),
    )
    sizes = tuple(mesh.shape[name] for name in ("groups", "fsdp", "resp", "tp"))
    return jax.shard_map(
        functools.partial(on_device, sizes),
        mesh=mesh,
        in_specs=placed,
        out_specs=P(("groups", "fsdp"), "resp", None, "tp"),
        check_vma=False,
    )
```

```python
import functools
import math

import jax
import jax.numpy as jnp
import numpy as np
from jax import lax
from jax.experimental import pallas as pl
from jax.experimental.pallas import tpu as pltpu
from jax.sharding import PartitionSpec as P

HD = 128
PLEN = 1024
FACTOR = HD**-0.5 * math.log2(math.e)
MIB = 1 << 20
ANYWHERE = pl.BlockSpec(memory_space=pl.ANY)
HBM = pl.BlockSpec(memory_space=pltpu.HBM)


def dot_nt(a, b):
    return lax.dot_general(a, b, (((1,), (1,)), ((), ())), preferred_element_type=jnp.float32)


def dot_nn(a, b):
    return lax.dot_general(a, b, (((1,), (0,)), ((), ())), preferred_element_type=jnp.float32)


def settings(limit):
    return {
        "compiler_params": pltpu.CompilerParams(vmem_limit_bytes=limit * MIB),
        "cost_estimate": pl.CostEstimate(flops=0, bytes_accessed=0, transcendentals=0),
    }


def after(value, *earlier):
    return pl.pallas_call(
        lambda *refs: None,
        in_specs=[ANYWHERE] * (1 + len(earlier)),
        out_specs=ANYWHERE,
        out_shape=jax.ShapeDtypeStruct(value.shape, value.dtype),
        input_output_aliases={0: 0},
        name="after",
        **settings(1),
    )(value, *earlier)


def run_copies(copies):
    for copy in copies:
        copy.start()
    for copy in copies:
        copy.wait()


def pack_rows(n_groups, key_weight, value_weight, prompt_keys, prompt_values):
    block, columns = key_weight.shape
    half = block // n_groups

    arguments = [
        pltpu.with_memory_space_constraint(x, pltpu.HBM)
        for x in (key_weight, value_weight, prompt_keys, prompt_values)
    ]

    def body(kw_ref, vw_ref, pk_ref, pv_ref, share_ref, cache_ref, ks_ref, vs_ref, sems):
        rows = pl.ds(pl.multiple_of(lax.axis_index("groups") * half, half), half)
        run_copies(
            [
                pltpu.make_async_copy(pk_ref, cache_ref.at[0], sems.at[0]),
                pltpu.make_async_copy(pv_ref, cache_ref.at[1], sems.at[1]),
                pltpu.make_async_copy(kw_ref.at[rows, :], share_ref.at[0], sems.at[2]),
                pltpu.make_async_copy(vw_ref.at[rows, :], share_ref.at[1], sems.at[3]),
                pltpu.make_async_copy(kw_ref.at[rows, :], ks_ref, sems.at[4]),
                pltpu.make_async_copy(vw_ref.at[rows, :], vs_ref, sems.at[5]),
            ]
        )

    return pl.pallas_call(
        body,
        in_specs=[HBM] * 4,
        out_specs=[ANYWHERE] * 4,
        out_shape=[
            jax.ShapeDtypeStruct((2, half, columns), key_weight.dtype),
            jax.ShapeDtypeStruct((2, *prompt_keys.shape), prompt_keys.dtype),
            jax.ShapeDtypeStruct((half, columns), key_weight.dtype),
            jax.ShapeDtypeStruct((half, columns), key_weight.dtype),
        ],
        scratch_shapes=[pltpu.SemaphoreType.DMA((6,))],
        name="pack_rows",
        **settings(1),
    )(*arguments)


def pack_features(sizes, block, sets, hidden):
    n_groups, n_fsdp, n_resp, n_tp = sizes
    rows, width = hidden.shape
    per_core = n_fsdp // n_tp
    half = block // n_groups

    def start_of(place, n):
        group = (lax.axis_index("groups") + place[0]) % n_groups
        resp = (lax.axis_index("resp") + place[1]) % n_resp
        return (n * n_resp + resp) * block + group * half

    if half % HD:
        return [
            jnp.concatenate(
                [
                    lax.dynamic_slice_in_dim(hidden, start_of(place, n), half, axis=1)
                    for n in range(per_core)
                ],
                axis=1,
            )
            for place in sets
        ]

    step = rows // 4

    def body(hidden_ref, *refs):
        outs, (held, sems) = refs[: len(sets)], refs[len(sets) :]
        copies = []
        for n in range(rows // step):
            part = pl.ds(n * step, step)
            copies.append(
                pltpu.make_async_copy(hidden_ref.at[part, :], held.at[part, :], sems.at[n])
            )
        for copy in copies:
            copy.start()
        for n, copy in enumerate(copies):
            copy.wait()
            part = slice(n * step, (n + 1) * step)
            for place, out in zip(sets, outs):
                for k in range(per_core):
                    first = pl.multiple_of(start_of(place, k), HD)
                    out[part, k * half : (k + 1) * half] = held[part, pl.ds(first, half)]

    shape = (rows, per_core * half)
    return pl.pallas_call(
        body,
        grid=(1,),
        in_specs=[HBM],
        out_specs=[pl.BlockSpec(shape, lambda _: (0, 0))] * len(sets),
        out_shape=[jax.ShapeDtypeStruct(shape, hidden.dtype)] * len(sets),
        scratch_shapes=[pltpu.VMEM((rows, width), hidden.dtype), pltpu.SemaphoreType.DMA((4,))],
        name="pack_features",
        **settings(12),
    )(pltpu.with_memory_space_constraint(hidden, pltpu.HBM))


def line_ring(size):
    return list(range(0, size, 2)) + list(range(1, size, 2))[::-1]


def owner_of(n_fsdp, hops):
    fsdp = lax.axis_index("fsdp")
    place = jnp.where(fsdp % 2 == 0, fsdp // 2, n_fsdp - (fsdp + 1) // 2)
    at = (place - hops + n_fsdp) % n_fsdp
    return jnp.where(at < n_fsdp // 2, 2 * at, 2 * n_fsdp - 1 - 2 * at)


def project(n_fsdp, pieces, kinds, pairs, types, waits=()):
    half, columns = pieces[0][0][0].shape[-2:]
    rows, depth = pairs[0][0].shape
    dtype = pairs[0][0].dtype
    listed = [piece for kind in kinds for piece in pieces[kind]]
    total, count = len(listed), len(pairs)
    each = total // len(kinds)

    def body(*refs):
        piece_refs, refs = refs[:total], refs[total:]
        pair_refs, refs = refs[: 2 * count], refs[2 * count + len(waits) :]
        outs, weights = refs[:-1], refs[-1]
        core = lax.axis_index("tp")
        owners = [owner_of(n_fsdp, hops) for _, _, hops in listed[:each]]
        for k in range(len(kinds)):
            for ref, owner in zip(piece_refs[k * each : (k + 1) * each], owners):
                rows_here = pl.ds(pl.multiple_of(owner * half, half), half)
                weights[k, rows_here, :] = ref[0] if len(ref.shape) == 3 else ref[...]
        first = pl.ds(pl.multiple_of(core * depth, depth), depth)
        second = pl.ds(pl.multiple_of((1 - core) * depth, depth), depth)
        for n in range(count):
            near_ref, far_ref = pair_refs[2 * n : 2 * n + 2]
            for k in range(len(kinds)):
                sums = dot_nn(near_ref[...], weights[k, first, :])
                sums = sums + dot_nn(far_ref[...], weights[k, second, :])
                out = outs[n * len(kinds) + k]
                out[...] = sums.astype(out.dtype)

    def whole(shape):
        return pl.BlockSpec(shape, lambda _: (0,) * len(shape))

    def piece_spec(index):
        if index is None:
            return whole((half, columns))
        return pl.BlockSpec((1, half, columns), lambda _: (index, 0, 0))

    types = [t for t in types for _ in kinds]
    return pl.pallas_call(
        body,
        grid=(1,),
        in_specs=[piece_spec(index) for _, index, _ in listed]
        + [whole((rows, depth))] * (2 * count)
        + [ANYWHERE] * len(waits),
        out_specs=[whole((rows, columns))] * len(types),
        out_shape=[jax.ShapeDtypeStruct((rows, columns), t) for t in types],
        scratch_shapes=[pltpu.VMEM((len(kinds), n_fsdp * half, columns), dtype)],
        name="project",
        **settings(24),
    )(*[x for x, _, _ in listed], *[x for pair in pairs for x in pair], *waits)


def take(ref, first, count):
    return jnp.concatenate(
        [ref[:, (first + n) * HD : (first + n + 1) * HD] for n in range(count)], axis=0
    )


def put(ref, first, count, value):
    tokens = ref.shape[0]
    value = jnp.broadcast_to(value, (count * tokens, HD)).astype(ref.dtype)
    for n in range(count):
        ref[:, (first + n) * HD : (first + n + 1) * HD] = value[n * tokens : (n + 1) * tokens]


def attend_cache(slot, tokens, group_size, queries, caches, waits):
    count = len(caches)
    heads = queries.shape[1] // (group_size * HD)
    length = caches[0].shape[1]
    step = 2 if group_size % 2 == 0 else 1

    def body(q_ref, *refs):
        mixed_ref, level_ref, mark_ref = refs[-3:]
        mark_ref[...] = jnp.zeros(mark_ref.shape, mark_ref.dtype)
        keys = [ref[0] for ref in refs[:count]]
        values = [ref[1] for ref in refs[:count]]
        wide = [jnp.concatenate([v, jnp.ones(v.shape, v.dtype)], axis=1) for v in values]

        def scores_of(first):
            q = take(q_ref, first, step)
            return [dot_nt(q, k) for k in keys]

        coming = scores_of(0)
        for first in range(0, group_size, step):
            scores = coming
            if first + step < group_size:
                coming = scores_of(first + step)
            tops = [s[:, n * HD : (n + 1) * HD] for s in scores for n in range(length // HD)]
            top = jnp.max(functools.reduce(jnp.maximum, tops), axis=1, keepdims=True)
            out = None
            for s, v in zip(scores, wide):
                probs = jnp.exp2((s - top) * FACTOR).astype(jnp.bfloat16)
                part = dot_nn(probs, v)
                out = part if out is None else out + part
            total = out[:, HD:]
            put(mixed_ref, first, step, out[:, :HD] / total)
            put(level_ref, first, step, top * FACTOR + jnp.log2(total))

    width = group_size * HD
    spec_q = pl.BlockSpec((tokens, width), lambda head: (slot, head))
    spec_c = pl.BlockSpec((2, length, HD), lambda head: (0, 0, head))
    spec_out = pl.BlockSpec((tokens, width), lambda head: (0, head))
    return pl.pallas_call(
        body,
        grid=(heads,),
        in_specs=[spec_q] + [spec_c] * count + [ANYWHERE] * len(waits),
        out_specs=[spec_out] * 2 + [pl.BlockSpec((8, HD), lambda head: (0, 0))],
        out_shape=[jax.ShapeDtypeStruct((tokens, heads * width), jnp.float32)] * 2
        + [jax.ShapeDtypeStruct((8, HD), jnp.float32)],
        name="attend_cache",
        **settings(20),
    )(queries, *caches, *waits)


def sum_refs(refs, rows=slice(None)):
    views = [ref[0, rows] if len(ref.shape) == 3 else ref[rows] for ref in refs]
    return functools.reduce(jnp.add, [view.astype(jnp.float32) for view in views])


def part_spec(part, kind, rows, index):
    if len(part.shape) == 3:
        return pl.BlockSpec((1, rows, HD), lambda head: (kind, index, head))
    return pl.BlockSpec((rows, HD), lambda head: (index, head))


def attend_own(slot, tokens, group_size, queries, key_parts, table, state):
    parts = len(key_parts)
    heads = queries.shape[1] // (group_size * HD)

    def body(q_ref, *refs):
        table_ref, old_mixed, old_level, mixed_ref, probs_ref, table, sem = refs[parts:]

        @pl.when(pl.program_id(0) == 0)
        def _():
            copy = pltpu.make_async_copy(table_ref, table, sem)
            copy.start()
            copy.wait()

        key = sum_refs(refs[:parts])
        key = key * table[0] + pltpu.roll(key, HD // 2, 1) * table[1]
        key = key.astype(jnp.bfloat16)
        ones = jnp.ones((tokens, HD), jnp.bfloat16)
        row = lax.broadcasted_iota(jnp.int32, (tokens, tokens), 0)
        causal = row >= lax.broadcasted_iota(jnp.int32, (tokens, tokens), 1)
        causal = jnp.concatenate([causal] * group_size, axis=0)
        scores = dot_nt(take(q_ref, 0, group_size), key) * FACTOR
        scores = jnp.where(causal, scores, -1e30)
        level = take(old_level, 0, group_size)
        top = jnp.max(jnp.maximum(level, scores), axis=1, keepdims=True)
        probs = jnp.exp2(scores - top)
        kept = jnp.exp2(level - top)
        inverse = 1.0 / (kept + dot_nn(probs.astype(jnp.bfloat16), ones))
        put(mixed_ref, 0, group_size, take(old_mixed, 0, group_size) * (kept * inverse))
        put(probs_ref, 0, group_size, probs * inverse)

    width = group_size * HD
    spec_q = pl.BlockSpec((tokens, width), lambda head: (slot, head))
    spec_keys = [part_spec(part, 0, tokens, slot) for part in key_parts]
    spec_wide = pl.BlockSpec((tokens, width), lambda head: (0, head))
    shape = (tokens, heads * width)
    return pl.pallas_call(
        body,
        grid=(heads,),
        in_specs=[spec_q] + spec_keys + [HBM] + [spec_wide] * 2,
        out_specs=[spec_wide] * 2,
        out_shape=[
            jax.ShapeDtypeStruct(shape, jnp.float32),
            jax.ShapeDtypeStruct(shape, jnp.bfloat16),
        ],
        scratch_shapes=[pltpu.VMEM(table.shape, table.dtype), pltpu.SemaphoreType.DMA],
        name="attend_own",
        **settings(20),
    )(queries, *key_parts, pltpu.with_memory_space_constraint(table, pltpu.HBM), *state)


def finish(live, value_parts, states, tokens, group_size, dtype):
    parts, slots = len(value_parts), len(states)
    width = group_size * HD
    heads = states[0][0].shape[1] // width

    def body(live_ref, *refs):
        out_ref = refs[-1]
        for slot in range(slots):
            mixed_ref, probs_ref = refs[parts + 2 * slot : parts + 2 * slot + 2]
            rows = slice(slot * tokens, (slot + 1) * tokens)
            value = sum_refs(refs[:parts], rows).astype(jnp.bfloat16)
            out = take(mixed_ref, 0, group_size) + dot_nn(take(probs_ref, 0, group_size), value)
            out = jnp.where(slot < live_ref[0], out, 0.0)
            put(out_ref.at[rows, :], 0, group_size, out)

    spec_values = [part_spec(part, 1, slots * tokens, 0) for part in value_parts]
    spec_wide = pl.BlockSpec((tokens, width), lambda head: (0, head))
    return pl.pallas_call(
        body,
        grid=(heads,),
        in_specs=[pl.BlockSpec(memory_space=pltpu.SMEM)]
        + spec_values
        + [spec_wide] * (2 * slots),
        out_specs=pl.BlockSpec((slots * tokens, width), lambda head: (0, head)),
        out_shape=jax.ShapeDtypeStruct((slots * tokens, heads * width), dtype),
        name="finish",
        **settings(20),
    )(live, *value_parts, *[x for state in states for x in state])


def rotation_tables(extent, offset):
    orders = np.arange(HD // 2, dtype=np.float64)
    inverse = np.exp(-(2.0 * orders / HD) * math.log(500000.0))
    angles = (offset + np.arange(extent))[:, None] * inverse[None, :]
    cosine, sine = np.cos(angles), np.sin(angles)
    halves = [np.concatenate([cosine, cosine], axis=1), np.concatenate([-sine, sine], axis=1)]
    return jnp.asarray(np.stack(halves), jnp.float32)


def on_device(sizes, hidden, queries, prompt_keys, prompt_values, key_weight, value_weight, counts):
    n_groups, n_fsdp, n_resp, n_tp = sizes
    _, slots, tokens, part_width = hidden.shape
    block, columns = key_weight.shape
    group_size = queries.shape[3] // columns
    rows = slots * tokens
    plane = ("groups", "resp")
    cores = [(n, (n + 1) % n_tp) for n in range(n_tp)]
    ring = line_ring(n_fsdp)
    rightward = [(ring[n], ring[(n + 1) % n_fsdp]) for n in range(n_fsdp)]
    leftward = [(b, a) for a, b in rightward]
    along = [(0, b) for b in range(1, n_resp)]
    across = [(a, b) for a in range(1, n_groups) for b in range(1, n_resp)]
    twins = [(a, 0) for a in range(1, n_groups)]
    sets = [(0, 0), *across, *along, *twins]

    def shift(a, b):
        return [
            (g * n_resp + r, (g + a) % n_groups * n_resp + (r + b) % n_resp)
            for g in range(n_groups)
            for r in range(n_resp)
        ]

    share, cache, key_share, value_share = pack_rows(n_groups, key_weight, value_weight, prompt_keys[0], prompt_values[0])

    caches = [cache]
    for b in range(1, n_resp):
        around = [(n, (n + b) % n_resp) for n in range(n_resp)]
        caches.append(lax.ppermute(cache, "resp", around))

    pieces = [[(share, kind, 0)] for kind in range(2)]
    held = share
    for hop in range(1, n_fsdp // 2 + 1):
        held = lax.ppermute(held, "fsdp", rightward)
        for kind in range(2):
            pieces[kind].append((held, kind, hop))
    first_hop, far_hop = pieces[0][1][0], held
    held = share
    for hop in range(1, n_fsdp - n_fsdp // 2 - 1):
        held = lax.ppermute(held, "fsdp", leftward)
        for kind in range(2):
            pieces[kind].append((held, kind, -hop))
    ends = (key_share, value_share) if held is share else (held[0], held[1])
    ends = [lax.ppermute(x, "fsdp", leftward) for x in ends]
    for kind in range(2):
        pieces[kind].append((ends[kind], None, 1 + n_fsdp // 2 - n_fsdp))

    flat_queries = queries.reshape(rows, queries.shape[3])
    states, marks = [], []
    for slot in range(slots):
        *state, mark = attend_cache(slot, tokens, group_size, flat_queries, caches, [first_hop])
        states.append(state)
        marks.append(mark)

    near = dict(zip(sets, pack_features(sizes, block, sets, hidden.reshape(rows, part_width))))
    for place in twins:
        near[place] = after(near[place], first_hop)
    for place in sets[1:]:
        waits = [ends[1]] if place in along else [far_hop, ends[0]]
        moved = lax.ppermute(near[place], plane, shift(*place))
        near[place] = after(moved, *marks, *waits)
    far = {place: lax.ppermute(near[place], "tp", cores) for place in sets}

    def send(place, sums):
        return lax.ppermute(sums, plane, shift(n_groups - place[0], n_resp - place[1]))

    narrow, wide = jnp.bfloat16, jnp.float32
    soon = [sets[0], *across, *twins]
    types = [wide] + [narrow] * (len(soon) - 1)
    pairs = [(near[p], far[p]) for p in soon]
    parts = [[], []]
    for kind in range(2):
        waits = [near[p] for p in along] if kind else []
        sums = project(n_fsdp, pieces, [kind], pairs, types, waits)
        parts[kind].append(sums[0])
        parts[kind].extend(send(p, x) for p, x in zip(soon[1:], sums[1:]))
    pairs = [(near[p], far[p]) for p in along]
    sums = project(n_fsdp, pieces, [0, 1], pairs, [narrow] * len(along))
    for n, p in enumerate(along):
        for kind in range(2):
            parts[kind].append(send(p, sums[2 * n + kind]))

    table = rotation_tables(tokens, PLEN)
    states = [
        attend_own(slot, tokens, group_size, flat_queries, parts[0], table, state)
        for slot, state in enumerate(states)
    ]
    live = (counts[0] - lax.axis_index("resp") * slots).astype(jnp.int32)[None]
    out = finish(live, parts[1], states, tokens, group_size, queries.dtype)
    return out.reshape(queries.shape)


def solution(mesh):
    placed = (
        P(("groups", "fsdp"), "resp", None, "tp"),
        P(("groups", "fsdp"), "resp", None, "tp"),
        P(("groups", "fsdp"), "resp", "tp"),
        P(("groups", "fsdp"), "resp", "tp"),
        P(("fsdp", "resp"), "tp"),
        P(("fsdp", "resp"), "tp"),
        P(("groups", "fsdp")),
    )
    sizes = tuple(mesh.shape[name] for name in ("groups", "fsdp", "resp", "tp"))
    return jax.shard_map(
        functools.partial(on_device, sizes),
        mesh=mesh,
        in_specs=placed,
        out_specs=P(("groups", "fsdp"), "resp", None, "tp"),
        check_vma=False,
    )
```

```python
import functools
import math

import jax
import jax.numpy as jnp
import numpy as np
from jax import lax
from jax.experimental import pallas as pl
from jax.experimental.pallas import tpu as pltpu
from jax.sharding import PartitionSpec as P

HD = 128
PLEN = 1024
FACTOR = HD**-0.5 * math.log2(math.e)
MIB = 1 << 20
ANYWHERE = pl.BlockSpec(memory_space=pl.ANY)
HBM = pl.BlockSpec(memory_space=pltpu.HBM)


def dot_nt(a, b):
    return lax.dot_general(a, b, (((1,), (1,)), ((), ())), preferred_element_type=jnp.float32)


def dot_nn(a, b):
    return lax.dot_general(a, b, (((1,), (0,)), ((), ())), preferred_element_type=jnp.float32)


def settings(limit):
    return {
        "compiler_params": pltpu.CompilerParams(vmem_limit_bytes=limit * MIB),
        "cost_estimate": pl.CostEstimate(flops=0, bytes_accessed=0, transcendentals=0),
    }


def after(value, *earlier):
    return pl.pallas_call(
        lambda *refs: None,
        in_specs=[ANYWHERE] * (1 + len(earlier)),
        out_specs=ANYWHERE,
        out_shape=jax.ShapeDtypeStruct(value.shape, value.dtype),
        input_output_aliases={0: 0},
        name="after",
        **settings(1),
    )(value, *earlier)


def run_copies(copies):
    for copy in copies:
        copy.start()
    for copy in copies:
        copy.wait()


def pack_rows(n_groups, key_weight, value_weight, prompt_keys, prompt_values):
    block, columns = key_weight.shape
    half = block // n_groups

    arguments = [
        pltpu.with_memory_space_constraint(x, pltpu.HBM)
        for x in (key_weight, value_weight, prompt_keys, prompt_values)
    ]

    def body(kw_ref, vw_ref, pk_ref, pv_ref, share_ref, cache_ref, sems):
        rows = pl.ds(pl.multiple_of(lax.axis_index("groups") * half, half), half)
        run_copies(
            [
                pltpu.make_async_copy(pk_ref, cache_ref.at[0], sems.at[0]),
                pltpu.make_async_copy(pv_ref, cache_ref.at[1], sems.at[1]),
                pltpu.make_async_copy(kw_ref.at[rows, :], share_ref.at[0], sems.at[2]),
                pltpu.make_async_copy(vw_ref.at[rows, :], share_ref.at[1], sems.at[3]),
            ]
        )

    return pl.pallas_call(
        body,
        in_specs=[HBM] * 4,
        out_specs=[ANYWHERE] * 2,
        out_shape=[
            jax.ShapeDtypeStruct((2, half, columns), key_weight.dtype),
            jax.ShapeDtypeStruct((2, *prompt_keys.shape), prompt_keys.dtype),
        ],
        scratch_shapes=[pltpu.SemaphoreType.DMA((4,))],
        name="pack_rows",
        **settings(1),
    )(*arguments)


def pack_features(sizes, block, sets, hidden):
    n_groups, n_fsdp, n_resp, n_tp = sizes
    rows, width = hidden.shape
    per_core = n_fsdp // n_tp
    half = block // n_groups

    def start_of(place, n):
        group = (lax.axis_index("groups") + place[0]) % n_groups
        resp = (lax.axis_index("resp") + place[1]) % n_resp
        return (n * n_resp + resp) * block + group * half

    if half % HD:
        return [
            jnp.concatenate(
                [
                    lax.dynamic_slice_in_dim(hidden, start_of(place, n), half, axis=1)
                    for n in range(per_core)
                ],
                axis=1,
            )
            for place in sets
        ]

    step = rows // 4

    def body(hidden_ref, *refs):
        outs, (held, sems) = refs[: len(sets)], refs[len(sets) :]
        copies = []
        for n in range(rows // step):
            part = pl.ds(n * step, step)
            copies.append(
                pltpu.make_async_copy(hidden_ref.at[part, :], held.at[part, :], sems.at[n])
            )
        for copy in copies:
            copy.start()
        for n, copy in enumerate(copies):
            copy.wait()
            part = slice(n * step, (n + 1) * step)
            for place, out in zip(sets, outs):
                for k in range(per_core):
                    first = pl.multiple_of(start_of(place, k), HD)
                    out[part, k * half : (k + 1) * half] = held[part, pl.ds(first, half)]

    shape = (rows, per_core * half)
    return pl.pallas_call(
        body,
        grid=(1,),
        in_specs=[HBM],
        out_specs=[pl.BlockSpec(shape, lambda _: (0, 0))] * len(sets),
        out_shape=[jax.ShapeDtypeStruct(shape, hidden.dtype)] * len(sets),
        scratch_shapes=[pltpu.VMEM((rows, width), hidden.dtype), pltpu.SemaphoreType.DMA((4,))],
        name="pack_features",
        **settings(12),
    )(pltpu.with_memory_space_constraint(hidden, pltpu.HBM))


def line_ring(size):
    return list(range(0, size, 2)) + list(range(1, size, 2))[::-1]


def owner_of(n_fsdp, hops):
    fsdp = lax.axis_index("fsdp")
    place = jnp.where(fsdp % 2 == 0, fsdp // 2, n_fsdp - (fsdp + 1) // 2)
    at = (place - hops + n_fsdp) % n_fsdp
    return jnp.where(at < n_fsdp // 2, 2 * at, 2 * n_fsdp - 1 - 2 * at)


def project(n_fsdp, pieces, pairs, types, waits=()):
    kinds, half, columns = pieces[0][0].shape
    rows, depth = pairs[0][0].shape
    dtype = pairs[0][0].dtype
    total, count = len(pieces), len(pairs)

    def body(*refs):
        piece_refs, refs = refs[:total], refs[total:]
        pair_refs, refs = refs[: 2 * count], refs[2 * count + len(waits) :]
        outs, weights = refs[:-1], refs[-1]
        core = lax.axis_index("tp")
        for ref, (_, hops) in zip(piece_refs, pieces):
            place = pl.ds(pl.multiple_of(owner_of(n_fsdp, hops) * half, half), half)
            for kind in range(kinds):
                weights[kind, place, :] = ref[kind]
        first = pl.ds(pl.multiple_of(core * depth, depth), depth)
        second = pl.ds(pl.multiple_of((1 - core) * depth, depth), depth)
        for n in range(count):
            near_ref, far_ref = pair_refs[2 * n : 2 * n + 2]
            for kind in range(kinds):
                sums = dot_nn(near_ref[...], weights[kind, first, :])
                sums = sums + dot_nn(far_ref[...], weights[kind, second, :])
                outs[n][kind] = sums.astype(outs[n].dtype)

    def whole(shape):
        return pl.BlockSpec(shape, lambda _: (0,) * len(shape))

    shape = (kinds, rows, columns)
    return pl.pallas_call(
        body,
        grid=(1,),
        in_specs=[whole((kinds, half, columns))] * total
        + [whole((rows, depth))] * (2 * count)
        + [ANYWHERE] * len(waits),
        out_specs=[whole(shape)] * count,
        out_shape=[jax.ShapeDtypeStruct(shape, t) for t in types],
        scratch_shapes=[pltpu.VMEM((kinds, n_fsdp * half, columns), dtype)],
        name="project",
        **settings(24),
    )(*[x for x, _ in pieces], *[x for pair in pairs for x in pair], *waits)


def take(ref, first, count):
    return jnp.concatenate(
        [ref[:, (first + n) * HD : (first + n + 1) * HD] for n in range(count)], axis=0
    )


def put(ref, first, count, value):
    tokens = ref.shape[0]
    value = jnp.broadcast_to(value, (count * tokens, HD)).astype(ref.dtype)
    for n in range(count):
        ref[:, (first + n) * HD : (first + n + 1) * HD] = value[n * tokens : (n + 1) * tokens]


def attend_cache(slots, group_size, queries, caches, waits):
    count = len(caches)
    tokens = queries.shape[0] // slots
    heads = queries.shape[1] // (group_size * HD)
    length = caches[0].shape[1]
    step = 2 if group_size % 2 == 0 else 1

    def body(q_ref, *refs):
        mixed_ref, level_ref, mark_ref = refs[-3:]
        mark_ref[...] = jnp.zeros(mark_ref.shape, mark_ref.dtype)
        keys = [ref[0] for ref in refs[:count]]
        values = [ref[1] for ref in refs[:count]]
        wide = [jnp.concatenate([v, jnp.ones(v.shape, v.dtype)], axis=1) for v in values]

        def scores_of(first):
            q = take(q_ref, first, step)
            return [dot_nt(q, k) for k in keys]

        coming = scores_of(0)
        for first in range(0, group_size, step):
            scores = coming
            if first + step < group_size:
                coming = scores_of(first + step)
            tops = [s[:, n * HD : (n + 1) * HD] for s in scores for n in range(length // HD)]
            top = jnp.max(functools.reduce(jnp.maximum, tops), axis=1, keepdims=True)
            out = None
            for s, v in zip(scores, wide):
                probs = jnp.exp2((s - top) * FACTOR).astype(jnp.bfloat16)
                part = dot_nn(probs, v)
                out = part if out is None else out + part
            total = out[:, HD:]
            put(mixed_ref, first, step, out[:, :HD] / total)
            put(level_ref, first, step, top * FACTOR + jnp.log2(total))

    spec_wide = pl.BlockSpec((tokens, group_size * HD), lambda head, slot: (slot, head))
    spec_c = pl.BlockSpec((2, length, HD), lambda head, slot: (0, 0, head))
    spec_mark = pl.BlockSpec((8, HD), lambda head, slot: (0, 0))
    return pl.pallas_call(
        body,
        grid=(heads, slots),
        in_specs=[spec_wide] + [spec_c] * count + [ANYWHERE] * len(waits),
        out_specs=[spec_wide] * 2 + [spec_mark],
        out_shape=[jax.ShapeDtypeStruct(queries.shape, jnp.float32)] * 2
        + [jax.ShapeDtypeStruct((8, HD), jnp.float32)],
        name="attend_cache",
        **settings(20),
    )(queries, *caches, *waits)


def attend_own(slots, group_size, live, queries, parts, table, state):
    count = len(parts)
    tokens = queries.shape[0] // slots
    heads = queries.shape[1] // (group_size * HD)

    def body(live_ref, q_ref, *refs):
        part_refs = refs[:count]
        table_ref, mixed_ref, level_ref, out_ref = refs[count:]
        slot = pl.program_id(0)

        def summed(kind):
            return functools.reduce(jnp.add, [ref[kind].astype(jnp.float32) for ref in part_refs])

        key = summed(0)
        key = key * table_ref[0] + pltpu.roll(key, HD // 2, 1) * table_ref[1]
        key = key.astype(jnp.bfloat16)
        value = summed(1).astype(jnp.bfloat16)
        wide = jnp.concatenate([value, jnp.ones((tokens, HD), jnp.bfloat16)], axis=1)
        row = lax.broadcasted_iota(jnp.int32, (tokens, tokens), 0)
        causal = row >= lax.broadcasted_iota(jnp.int32, (tokens, tokens), 1)
        causal = jnp.concatenate([causal] * group_size, axis=0)
        scores = dot_nt(take(q_ref, 0, group_size), key) * FACTOR
        scores = jnp.where(causal, scores, -1e30)
        level = take(level_ref, 0, group_size)
        top = jnp.max(jnp.maximum(level, scores), axis=1, keepdims=True)
        probs = jnp.exp2(scores - top).astype(jnp.bfloat16)
        kept = jnp.exp2(level - top)
        out = dot_nn(probs, wide)
        mixed = take(mixed_ref, 0, group_size) * kept + out[:, :HD]
        result = mixed / (kept + out[:, HD:])
        put(out_ref, 0, group_size, jnp.where(slot < live_ref[0], result, 0.0))

    spec_wide = pl.BlockSpec((tokens, group_size * HD), lambda slot, head: (slot, head))
    spec_part = pl.BlockSpec((2, tokens, HD), lambda slot, head: (0, slot, head))
    spec_table = pl.BlockSpec(table.shape, lambda slot, head: (0, 0, 0))
    kept_back = [pltpu.with_memory_space_constraint(x, pltpu.HBM) for x in (table, *state)]
    return pl.pallas_call(
        body,
        grid=(slots, heads),
        in_specs=[pl.BlockSpec(memory_space=pltpu.SMEM), spec_wide]
        + [spec_part] * count
        + [spec_table, spec_wide, spec_wide],
        out_specs=spec_wide,
        out_shape=jax.ShapeDtypeStruct(queries.shape, queries.dtype),
        name="attend_own",
        **settings(24),
    )(live, queries, *parts, *kept_back)


def rotation_tables(extent, offset):
    orders = np.arange(HD // 2, dtype=np.float64)
    inverse = np.exp(-(2.0 * orders / HD) * math.log(500000.0))
    angles = (offset + np.arange(extent))[:, None] * inverse[None, :]
    cosine, sine = np.cos(angles), np.sin(angles)
    halves = [np.concatenate([cosine, cosine], axis=1), np.concatenate([-sine, sine], axis=1)]
    return jnp.asarray(np.stack(halves), jnp.float32)


def on_device(sizes, hidden, queries, prompt_keys, prompt_values, key_weight, value_weight, counts):
    n_groups, n_fsdp, n_resp, n_tp = sizes
    _, slots, tokens, part_width = hidden.shape
    block, columns = key_weight.shape
    group_size = queries.shape[3] // columns
    rows = slots * tokens
    plane = ("groups", "resp")
    cores = [(n, (n + 1) % n_tp) for n in range(n_tp)]
    ring = line_ring(n_fsdp)
    rightward = [(ring[n], ring[(n + 1) % n_fsdp]) for n in range(n_fsdp)]
    leftward = [(b, a) for a, b in rightward]
    along = [(0, b) for b in range(1, n_resp)]
    across = [(a, b) for a in range(1, n_groups) for b in range(1, n_resp)]
    twins = [(a, 0) for a in range(1, n_groups)]
    sets = [(0, 0), *along, *twins, *across]

    def shift(a, b):
        return [
            (g * n_resp + r, (g + a) % n_groups * n_resp + (r + b) % n_resp)
            for g in range(n_groups)
            for r in range(n_resp)
        ]

    share, cache = pack_rows(n_groups, key_weight, value_weight, prompt_keys[0], prompt_values[0])

    caches = [cache]
    for b in range(1, n_resp):
        around = [(n, (n + b) % n_resp) for n in range(n_resp)]
        caches.append(lax.ppermute(cache, "resp", around))

    pieces = [(share, 0)]
    held = share
    for hop in range(1, n_fsdp // 2 + 1):
        held = lax.ppermute(held, "fsdp", rightward)
        pieces.append((held, hop))
    first_hop, ends = pieces[1][0], [held]
    held = share
    for hop in range(1, n_fsdp - n_fsdp // 2):
        held = lax.ppermute(held, "fsdp", leftward)
        pieces.append((held, -hop))
    ends.append(held)

    flat_queries = queries.reshape(rows, queries.shape[3])
    *state, mark = attend_cache(slots, group_size, flat_queries, caches, [first_hop])

    near = dict(zip(sets, pack_features(sizes, block, sets, hidden.reshape(rows, part_width))))
    for place in across:
        near[place] = after(near[place], first_hop)
    for place in sets[1:]:
        waits = ends if place in across else []
        moved = lax.ppermute(near[place], plane, shift(*place))
        near[place] = after(moved, mark, *waits)
    far = {place: lax.ppermute(near[place], "tp", cores) for place in sets}

    narrow, wide = jnp.bfloat16, jnp.float32
    parts = []
    for chosen, waits in (([*along, *twins, sets[0]], [near[p] for p in across]), (across, [])):
        types = [narrow if any(p) else wide for p in chosen]
        sums = project(n_fsdp, pieces, [(near[p], far[p]) for p in chosen], types, waits)
        for p, x in zip(chosen, sums):
            back = shift(n_groups - p[0], n_resp - p[1])
            parts.append(lax.ppermute(x, plane, back) if any(p) else x)

    table = rotation_tables(tokens, PLEN)
    live = (counts[0] - lax.axis_index("resp") * slots).astype(jnp.int32)[None]
    out = attend_own(slots, group_size, live, flat_queries, parts, table, state)
    return out.reshape(queries.shape)


def solution(mesh):
    placed = (
        P(("groups", "fsdp"), "resp", None, "tp"),
        P(("groups", "fsdp"), "resp", None, "tp"),
        P(("groups", "fsdp"), "resp", "tp"),
        P(("groups", "fsdp"), "resp", "tp"),
        P(("fsdp", "resp"), "tp"),
        P(("fsdp", "resp"), "tp"),
        P(("groups", "fsdp")),
    )
    sizes = tuple(mesh.shape[name] for name in ("groups", "fsdp", "resp", "tp"))
    return jax.shard_map(
        functools.partial(on_device, sizes),
        mesh=mesh,
        in_specs=placed,
        out_specs=P(("groups", "fsdp"), "resp", None, "tp"),
        check_vma=False,
    )
```

```python
import functools
import math

import jax
import jax.numpy as jnp
import numpy as np
from jax import lax
from jax.experimental import pallas as pl
from jax.experimental.pallas import tpu as pltpu
from jax.sharding import PartitionSpec as P

HD = 128
PLEN = 1024
FACTOR = HD**-0.5 * math.log2(math.e)
MIB = 1 << 20
ATTEND_FLOPS = 1 << 31
ANYWHERE = pl.BlockSpec(memory_space=pl.ANY)
HBM = pl.BlockSpec(memory_space=pltpu.HBM)


def dot_nt(a, b):
    return lax.dot_general(a, b, (((1,), (1,)), ((), ())), preferred_element_type=jnp.float32)


def dot_nn(a, b):
    return lax.dot_general(a, b, (((1,), (0,)), ((), ())), preferred_element_type=jnp.float32)


def settings(limit, flops=0):
    return {
        "compiler_params": pltpu.CompilerParams(vmem_limit_bytes=limit * MIB),
        "cost_estimate": pl.CostEstimate(flops=flops, bytes_accessed=0, transcendentals=0),
    }


def after(value, *earlier):
    return pl.pallas_call(
        lambda *refs: None,
        in_specs=[ANYWHERE] * (1 + len(earlier)),
        out_specs=ANYWHERE,
        out_shape=jax.ShapeDtypeStruct(value.shape, value.dtype),
        input_output_aliases={0: 0},
        name="after",
        **settings(1),
    )(value, *earlier)


def run_copies(copies):
    for copy in copies:
        copy.start()
    for copy in copies:
        copy.wait()


def pack_rows(n_groups, key_weight, value_weight, prompt_keys, prompt_values):
    block, columns = key_weight.shape
    half = block // n_groups

    arguments = [
        pltpu.with_memory_space_constraint(x, pltpu.HBM)
        for x in (key_weight, value_weight, prompt_keys, prompt_values)
    ]

    def body(kw_ref, vw_ref, pk_ref, pv_ref, share_ref, cache_ref, sems):
        rows = pl.ds(pl.multiple_of(lax.axis_index("groups") * half, half), half)
        run_copies(
            [
                pltpu.make_async_copy(pk_ref, cache_ref.at[0], sems.at[0]),
                pltpu.make_async_copy(pv_ref, cache_ref.at[1], sems.at[1]),
                pltpu.make_async_copy(kw_ref.at[rows, :], share_ref.at[0], sems.at[2]),
                pltpu.make_async_copy(vw_ref.at[rows, :], share_ref.at[1], sems.at[3]),
            ]
        )

    return pl.pallas_call(
        body,
        in_specs=[HBM] * 4,
        out_specs=[ANYWHERE] * 2,
        out_shape=[
            jax.ShapeDtypeStruct((2, half, columns), key_weight.dtype),
            jax.ShapeDtypeStruct((2, *prompt_keys.shape), prompt_keys.dtype),
        ],
        scratch_shapes=[pltpu.SemaphoreType.DMA((4,))],
        name="pack_rows",
        **settings(1),
    )(*arguments)


def split_pair(pair):
    def body(pair_ref, first_ref, second_ref, sems):
        run_copies(
            [
                pltpu.make_async_copy(pair_ref.at[0], first_ref, sems.at[0]),
                pltpu.make_async_copy(pair_ref.at[1], second_ref, sems.at[1]),
            ]
        )

    return pl.pallas_call(
        body,
        in_specs=[ANYWHERE],
        out_specs=[ANYWHERE] * 2,
        out_shape=[jax.ShapeDtypeStruct(pair.shape[1:], pair.dtype)] * 2,
        scratch_shapes=[pltpu.SemaphoreType.DMA((2,))],
        name="split_pair",
        **settings(1),
    )(pair)


def pack_features(sizes, block, sets, hidden):
    n_groups, n_fsdp, n_resp, n_tp = sizes
    rows, width = hidden.shape
    per_core = n_fsdp // n_tp
    half = block // n_groups

    def start_of(place, n):
        group = (lax.axis_index("groups") + place[0]) % n_groups
        resp = (lax.axis_index("resp") + place[1]) % n_resp
        return (n * n_resp + resp) * block + group * half

    if half % HD:
        return [
            jnp.concatenate(
                [
                    lax.dynamic_slice_in_dim(hidden, start_of(place, n), half, axis=1)
                    for n in range(per_core)
                ],
                axis=1,
            )
            for place in sets
        ]

    step = rows // 4

    def body(hidden_ref, *refs):
        outs, (held, sems) = refs[: len(sets)], refs[len(sets) :]
        copies = []
        for n in range(rows // step):
            part = pl.ds(n * step, step)
            copies.append(
                pltpu.make_async_copy(hidden_ref.at[part, :], held.at[part, :], sems.at[n])
            )
        for copy in copies:
            copy.start()
        for n, copy in enumerate(copies):
            copy.wait()
            part = slice(n * step, (n + 1) * step)
            for place, out in zip(sets, outs):
                for k in range(per_core):
                    first = pl.multiple_of(start_of(place, k), HD)
                    out[part, k * half : (k + 1) * half] = held[part, pl.ds(first, half)]

    shape = (rows, per_core * half)
    return pl.pallas_call(
        body,
        grid=(1,),
        in_specs=[HBM],
        out_specs=[pl.BlockSpec(shape, lambda _: (0, 0))] * len(sets),
        out_shape=[jax.ShapeDtypeStruct(shape, hidden.dtype)] * len(sets),
        scratch_shapes=[pltpu.VMEM((rows, width), hidden.dtype), pltpu.SemaphoreType.DMA((4,))],
        name="pack_features",
        **settings(12),
    )(pltpu.with_memory_space_constraint(hidden, pltpu.HBM))


def line_ring(size):
    return list(range(0, size, 2)) + list(range(1, size, 2))[::-1]


def owner_of(n_fsdp, hops):
    fsdp = lax.axis_index("fsdp")
    place = jnp.where(fsdp % 2 == 0, fsdp // 2, n_fsdp - (fsdp + 1) // 2)
    at = (place - hops + n_fsdp) % n_fsdp
    return jnp.where(at < n_fsdp // 2, 2 * at, 2 * n_fsdp - 1 - 2 * at)


def project(n_fsdp, pieces, pairs, types, waits=()):
    half, columns = pieces[0][0].shape[-2:]
    rows, depth = pairs[0][0].shape
    dtype = pairs[0][0].dtype
    total, count = len(pieces), len(pairs)

    def body(*refs):
        piece_refs, refs = refs[:total], refs[total:]
        pair_refs, refs = refs[: 2 * count], refs[2 * count + len(waits) :]
        outs, weights = refs[:-1], refs[-1]
        core = lax.axis_index("tp")
        for ref, (_, _, hops) in zip(piece_refs, pieces):
            place = pl.ds(pl.multiple_of(owner_of(n_fsdp, hops) * half, half), half)
            weights[place, :] = ref[0] if len(ref.shape) == 3 else ref[...]
        first = pl.ds(pl.multiple_of(core * depth, depth), depth)
        second = pl.ds(pl.multiple_of((1 - core) * depth, depth), depth)
        for n in range(count):
            near_ref, far_ref = pair_refs[2 * n : 2 * n + 2]
            sums = dot_nn(near_ref[...], weights[first, :])
            sums = sums + dot_nn(far_ref[...], weights[second, :])
            outs[n][...] = sums.astype(outs[n].dtype)

    def whole(shape):
        return pl.BlockSpec(shape, lambda _: (0,) * len(shape))

    def piece_spec(index):
        if index is None:
            return whole((half, columns))
        return pl.BlockSpec((1, half, columns), lambda _: (index, 0, 0))

    return pl.pallas_call(
        body,
        grid=(1,),
        in_specs=[piece_spec(index) for _, index, _ in pieces]
        + [whole((rows, depth))] * (2 * count)
        + [ANYWHERE] * len(waits),
        out_specs=[whole((rows, columns))] * count,
        out_shape=[jax.ShapeDtypeStruct((rows, columns), t) for t in types],
        scratch_shapes=[pltpu.VMEM((n_fsdp * half, columns), dtype)],
        name="project",
        **settings(24),
    )(*[x for x, _, _ in pieces], *[x for pair in pairs for x in pair], *waits)


def take(ref, first, count):
    return jnp.concatenate(
        [ref[:, (first + n) * HD : (first + n + 1) * HD] for n in range(count)], axis=0
    )


def put(ref, first, count, value):
    tokens = ref.shape[0]
    value = jnp.broadcast_to(value, (count * tokens, HD)).astype(ref.dtype)
    for n in range(count):
        ref[:, (first + n) * HD : (first + n + 1) * HD] = value[n * tokens : (n + 1) * tokens]


def attend(slots, group_size, queries, caches, key_parts, table):
    count, parts = len(caches), len(key_parts)
    tokens = queries.shape[0] // slots
    heads = queries.shape[1] // (group_size * HD)
    length = caches[0].shape[1]
    step = 2 if group_size % 2 == 0 else 1

    def body(q_ref, *refs):
        cache_refs, key_refs = refs[:count], refs[count : count + parts]
        table_ref, mixed_ref, probs_ref = refs[count + parts :]
        keys = [ref[0] for ref in cache_refs]
        wide = [
            jnp.concatenate([ref[1], jnp.ones((length, HD), ref.dtype)], axis=1)
            for ref in cache_refs
        ]
        key = functools.reduce(jnp.add, [ref[...].astype(jnp.float32) for ref in key_refs])
        key = key * table_ref[0] + pltpu.roll(key, HD // 2, 1) * table_ref[1]
        key = key.astype(jnp.bfloat16)
        ones = jnp.ones((tokens, HD), jnp.bfloat16)
        row = lax.broadcasted_iota(jnp.int32, (tokens, tokens), 0)
        causal = row >= lax.broadcasted_iota(jnp.int32, (tokens, tokens), 1)
        causal = jnp.concatenate([causal] * step, axis=0)

        def scores_of(first):
            q = take(q_ref, first, step)
            return [dot_nt(q, k) for k in keys], jnp.where(causal, dot_nt(q, key), -1e30)

        coming = scores_of(0)
        for first in range(0, group_size, step):
            scores, own = coming
            if first + step < group_size:
                coming = scores_of(first + step)
            tops = [s[:, n * HD : (n + 1) * HD] for s in scores for n in range(length // HD)]
            top = jnp.max(functools.reduce(jnp.maximum, [own, *tops]), axis=1, keepdims=True)
            probs = jnp.exp2((own - top) * FACTOR)
            out = None
            for s, v in zip(scores, wide):
                weights = jnp.exp2((s - top) * FACTOR).astype(jnp.bfloat16)
                part = dot_nn(weights, v)
                out = part if out is None else out + part
            inverse = 1.0 / (out[:, HD:] + dot_nn(probs.astype(jnp.bfloat16), ones))
            put(mixed_ref, first, step, out[:, :HD] * inverse)
            put(probs_ref, first, step, probs * inverse)

    spec_wide = pl.BlockSpec((tokens, group_size * HD), lambda head, slot: (slot, head))
    spec_c = pl.BlockSpec((2, length, HD), lambda head, slot: (0, 0, head))
    spec_key = pl.BlockSpec((tokens, HD), lambda head, slot: (slot, head))
    spec_table = pl.BlockSpec(table.shape, lambda head, slot: (0, 0, 0))
    return pl.pallas_call(
        body,
        grid=(heads, slots),
        in_specs=[spec_wide] + [spec_c] * count + [spec_key] * parts + [spec_table],
        out_specs=[spec_wide] * 2,
        out_shape=[
            jax.ShapeDtypeStruct(queries.shape, jnp.float32),
            jax.ShapeDtypeStruct(queries.shape, jnp.bfloat16),
        ],
        name="attend",
        **settings(20, 4 * ATTEND_FLOPS),
    )(queries, *caches, *key_parts, pltpu.with_memory_space_constraint(table, pltpu.HBM))


def finish(slots, group_size, live, mixed, probs, value_parts):
    parts = len(value_parts)
    tokens = mixed.shape[0] // slots
    heads = mixed.shape[1] // (group_size * HD)

    def body(live_ref, mixed_ref, probs_ref, *refs):
        value = functools.reduce(jnp.add, [ref[...].astype(jnp.float32) for ref in refs[:parts]])
        value = value.astype(jnp.bfloat16)
        out = take(mixed_ref, 0, group_size) + dot_nn(take(probs_ref, 0, group_size), value)
        put(refs[-1], 0, group_size, jnp.where(pl.program_id(0) < live_ref[0], out, 0.0))

    spec_wide = pl.BlockSpec((tokens, group_size * HD), lambda slot, head: (slot, head))
    spec_value = pl.BlockSpec((tokens, HD), lambda slot, head: (slot, head))
    return pl.pallas_call(
        body,
        grid=(slots, heads),
        in_specs=[pl.BlockSpec(memory_space=pltpu.SMEM)]
        + [spec_wide] * 2
        + [spec_value] * parts,
        out_specs=spec_wide,
        out_shape=jax.ShapeDtypeStruct(mixed.shape, jnp.bfloat16),
        name="finish",
        **settings(20),
    )(live, mixed, probs, *value_parts)


def rotation_tables(extent, offset):
    orders = np.arange(HD // 2, dtype=np.float64)
    inverse = np.exp(-(2.0 * orders / HD) * math.log(500000.0))
    angles = (offset + np.arange(extent))[:, None] * inverse[None, :]
    cosine, sine = np.cos(angles), np.sin(angles)
    halves = [np.concatenate([cosine, cosine], axis=1), np.concatenate([-sine, sine], axis=1)]
    return jnp.asarray(np.stack(halves), jnp.float32)


def on_device(sizes, hidden, queries, prompt_keys, prompt_values, key_weight, value_weight, counts):
    n_groups, n_fsdp, n_resp, n_tp = sizes
    _, slots, tokens, part_width = hidden.shape
    block, columns = key_weight.shape
    group_size = queries.shape[3] // columns
    rows = slots * tokens
    plane = ("groups", "resp")
    cores = [(n, (n + 1) % n_tp) for n in range(n_tp)]
    ring = line_ring(n_fsdp)
    rightward = [(ring[n], ring[(n + 1) % n_fsdp]) for n in range(n_fsdp)]
    leftward = [(b, a) for a, b in rightward]
    along = [(0, b) for b in range(1, n_resp)]
    across = [(a, b) for a in range(1, n_groups) for b in range(1, n_resp)]
    twins = [(a, 0) for a in range(1, n_groups)]
    sets = [(0, 0), *along, *twins, *across]

    def shift(a, b):
        return [
            (g * n_resp + r, (g + a) % n_groups * n_resp + (r + b) % n_resp)
            for g in range(n_groups)
            for r in range(n_resp)
        ]

    share, cache = pack_rows(n_groups, key_weight, value_weight, prompt_keys[0], prompt_values[0])

    caches = [cache]
    for b in range(1, n_resp):
        around = [(n, (n + b) % n_resp) for n in range(n_resp)]
        caches.append(lax.ppermute(cache, "resp", around))

    pieces = [[(share, kind, 0)] for kind in range(2)]
    held = share
    for hop in range(1, n_fsdp // 2):
        held = lax.ppermute(held, "fsdp", rightward)
        for kind in range(2):
            pieces[kind].append((held, kind, hop))
    first_hop = held
    for kind, end in enumerate(split_pair(held)):
        pieces[kind].append((lax.ppermute(end, "fsdp", rightward), None, n_fsdp // 2))
    held = share
    for hop in range(1, n_fsdp - n_fsdp // 2):
        held = lax.ppermute(held, "fsdp", leftward)
        for kind in range(2):
            pieces[kind].append((held, kind, -hop))

    near = dict(zip(sets, pack_features(sizes, block, sets, hidden.reshape(rows, part_width))))
    for place in sets[1:]:
        near[place] = lax.ppermute(near[place], plane, shift(*place))
    far = {place: lax.ppermute(near[place], "tp", cores) for place in sets}

    parts, done = [], []
    order = [*across, *along, *twins, sets[0]]
    types = [jnp.bfloat16 if any(p) else jnp.float32 for p in order]
    for kind in range(2):
        sums = project(n_fsdp, pieces[kind], [(near[p], far[p]) for p in order], types, done)
        done = [sums[-1]]
        back = [shift(n_groups - p[0], n_resp - p[1]) for p in order[:-1]]
        parts.append([sums[-1], *[lax.ppermute(x, plane, b) for x, b in zip(sums, back)]])

    flat_queries = queries.reshape(rows, queries.shape[3])
    table = rotation_tables(tokens, PLEN)
    state = attend(slots, group_size, flat_queries, caches, parts[0], table)
    live = (counts[0] - lax.axis_index("resp") * slots).astype(jnp.int32)[None]
    out = finish(slots, group_size, live, *state, parts[1])
    return out.reshape(queries.shape)


def solution(mesh):
    placed = (
        P(("groups", "fsdp"), "resp", None, "tp"),
        P(("groups", "fsdp"), "resp", None, "tp"),
        P(("groups", "fsdp"), "resp", "tp"),
        P(("groups", "fsdp"), "resp", "tp"),
        P(("fsdp", "resp"), "tp"),
        P(("fsdp", "resp"), "tp"),
        P(("groups", "fsdp")),
    )
    sizes = tuple(mesh.shape[name] for name in ("groups", "fsdp", "resp", "tp"))
    return jax.shard_map(
        functools.partial(on_device, sizes),
        mesh=mesh,
        in_specs=placed,
        out_specs=P(("groups", "fsdp"), "resp", None, "tp"),
        check_vma=False,
    )
```

```python
import functools
import math

import jax
import jax.numpy as jnp
import numpy as np
from jax import lax
from jax.experimental import pallas as pl
from jax.experimental.pallas import tpu as pltpu
from jax.sharding import PartitionSpec as P

HD = 128
PLEN = 1024
FACTOR = HD**-0.5 * math.log2(math.e)
MIB = 1 << 20
ANYWHERE = pl.BlockSpec(memory_space=pl.ANY)
HBM = pl.BlockSpec(memory_space=pltpu.HBM)


def dot_nt(a, b):
    return lax.dot_general(a, b, (((1,), (1,)), ((), ())), preferred_element_type=jnp.float32)


def dot_nn(a, b):
    return lax.dot_general(a, b, (((1,), (0,)), ((), ())), preferred_element_type=jnp.float32)


def settings(limit):
    return {
        "compiler_params": pltpu.CompilerParams(vmem_limit_bytes=limit * MIB),
        "cost_estimate": pl.CostEstimate(flops=0, bytes_accessed=0, transcendentals=0),
    }


def after(value, *earlier):
    return pl.pallas_call(
        lambda *refs: None,
        in_specs=[ANYWHERE] * (1 + len(earlier)),
        out_specs=ANYWHERE,
        out_shape=jax.ShapeDtypeStruct(value.shape, value.dtype),
        input_output_aliases={0: 0},
        name="after",
        **settings(1),
    )(value, *earlier)


def run_copies(copies):
    for copy in copies:
        copy.start()
    for copy in copies:
        copy.wait()


def pack_rows(n_groups, key_weight, value_weight, prompt_keys, prompt_values):
    block, columns = key_weight.shape
    half = block // n_groups

    arguments = [
        pltpu.with_memory_space_constraint(x, pltpu.HBM)
        for x in (key_weight, value_weight, prompt_keys, prompt_values)
    ]

    def body(kw_ref, vw_ref, pk_ref, pv_ref, share_ref, cache_ref, sems):
        rows = pl.ds(pl.multiple_of(lax.axis_index("groups") * half, half), half)
        run_copies(
            [
                pltpu.make_async_copy(pk_ref, cache_ref.at[0], sems.at[0]),
                pltpu.make_async_copy(pv_ref, cache_ref.at[1], sems.at[1]),
                pltpu.make_async_copy(kw_ref.at[rows, :], share_ref.at[0], sems.at[2]),
                pltpu.make_async_copy(vw_ref.at[rows, :], share_ref.at[1], sems.at[3]),
            ]
        )

    return pl.pallas_call(
        body,
        in_specs=[HBM] * 4,
        out_specs=[ANYWHERE] * 2,
        out_shape=[
            jax.ShapeDtypeStruct((2, half, columns), key_weight.dtype),
            jax.ShapeDtypeStruct((2, *prompt_keys.shape), prompt_keys.dtype),
        ],
        scratch_shapes=[pltpu.SemaphoreType.DMA((4,))],
        name="pack_rows",
        **settings(1),
    )(*arguments)


def pack_features(sizes, block, sets, hidden):
    n_groups, n_fsdp, n_resp, n_tp = sizes
    rows, width = hidden.shape
    per_core = n_fsdp // n_tp
    half = block // n_groups

    def start_of(place, n):
        group = (lax.axis_index("groups") + place[0]) % n_groups
        resp = (lax.axis_index("resp") + place[1]) % n_resp
        return (n * n_resp + resp) * block + group * half

    if half % HD:
        return [
            jnp.concatenate(
                [
                    lax.dynamic_slice_in_dim(hidden, start_of(place, n), half, axis=1)
                    for n in range(per_core)
                ],
                axis=1,
            )
            for place in sets
        ]

    step = rows // 4

    def body(hidden_ref, *refs):
        outs, (held, sems) = refs[: len(sets)], refs[len(sets) :]
        copies = []
        for n in range(rows // step):
            part = pl.ds(n * step, step)
            copies.append(
                pltpu.make_async_copy(hidden_ref.at[part, :], held.at[part, :], sems.at[n])
            )
        for copy in copies:
            copy.start()
        for n, copy in enumerate(copies):
            copy.wait()
            part = slice(n * step, (n + 1) * step)
            for place, out in zip(sets, outs):
                for k in range(per_core):
                    first = pl.multiple_of(start_of(place, k), HD)
                    out[part, k * half : (k + 1) * half] = held[part, pl.ds(first, half)]

    shape = (rows, per_core * half)
    return pl.pallas_call(
        body,
        grid=(1,),
        in_specs=[HBM],
        out_specs=[pl.BlockSpec(shape, lambda _: (0, 0))] * len(sets),
        out_shape=[jax.ShapeDtypeStruct(shape, hidden.dtype)] * len(sets),
        scratch_shapes=[pltpu.VMEM((rows, width), hidden.dtype), pltpu.SemaphoreType.DMA((4,))],
        name="pack_features",
        **settings(12),
    )(pltpu.with_memory_space_constraint(hidden, pltpu.HBM))


def line_ring(size):
    return list(range(0, size, 2)) + list(range(1, size, 2))[::-1]


def owner_of(n_fsdp, hops):
    fsdp = lax.axis_index("fsdp")
    place = jnp.where(fsdp % 2 == 0, fsdp // 2, n_fsdp - (fsdp + 1) // 2)
    at = (place - hops + n_fsdp) % n_fsdp
    return jnp.where(at < n_fsdp // 2, 2 * at, 2 * n_fsdp - 1 - 2 * at)


def project(n_fsdp, pieces, pairs, kind_of_sum, waits=(), apart=False):
    kinds, half, columns = pieces[0][0].shape
    rows, depth = pairs[0][0].shape
    dtype = pairs[0][0].dtype
    total, count = len(pieces), len(pairs)

    def body(*refs):
        piece_refs, refs = refs[:total], refs[total:]
        pair_refs, refs = refs[: 2 * count], refs[2 * count + len(waits) :]
        outs, weights = refs[:-1], refs[-1]
        core = lax.axis_index("tp")
        for ref, (_, hops) in zip(piece_refs, pieces):
            place = pl.ds(pl.multiple_of(owner_of(n_fsdp, hops) * half, half), half)
            for kind in range(kinds):
                weights[kind, place, :] = ref[kind]
        first = pl.ds(pl.multiple_of(core * depth, depth), depth)
        second = pl.ds(pl.multiple_of((1 - core) * depth, depth), depth)
        for n in range(count):
            near_ref, far_ref = pair_refs[2 * n : 2 * n + 2]
            for kind in range(kinds):
                sums = dot_nn(near_ref[...], weights[kind, first, :])
                sums = sums + dot_nn(far_ref[...], weights[kind, second, :])
                out = outs[n * kinds + kind] if apart else outs[n].at[kind]
                out[...] = sums.astype(out.dtype)

    def whole(shape):
        return pl.BlockSpec(shape, lambda _: (0,) * len(shape))

    shape = (rows, columns) if apart else (kinds, rows, columns)
    number = count * kinds if apart else count
    return pl.pallas_call(
        body,
        grid=(1,),
        in_specs=[whole((kinds, half, columns))] * total
        + [whole((rows, depth))] * (2 * count)
        + [ANYWHERE] * len(waits),
        out_specs=[whole(shape)] * number,
        out_shape=[jax.ShapeDtypeStruct(shape, kind_of_sum)] * number,
        scratch_shapes=[pltpu.VMEM((kinds, n_fsdp * half, columns), dtype)],
        name="project",
        **settings(24),
    )(*[x for x, _ in pieces], *[x for pair in pairs for x in pair], *waits)


def take(ref, first, count):
    return jnp.concatenate(
        [ref[:, (first + n) * HD : (first + n + 1) * HD] for n in range(count)], axis=0
    )


def put(ref, first, count, value):
    tokens = ref.shape[0]
    value = jnp.broadcast_to(value, (count * tokens, HD)).astype(ref.dtype)
    for n in range(count):
        ref[:, (first + n) * HD : (first + n + 1) * HD] = value[n * tokens : (n + 1) * tokens]


def attend_cache(slots, group_size, queries, caches, waits):
    count = len(caches)
    tokens = queries.shape[0] // slots
    heads = queries.shape[1] // (group_size * HD)
    length = caches[0].shape[1]
    step = 2 if group_size % 2 == 0 else 1

    def body(q_ref, *refs):
        mixed_ref, level_ref, mark_ref = refs[-3:]
        mark_ref[...] = jnp.zeros(mark_ref.shape, mark_ref.dtype)
        keys = [ref[0] for ref in refs[:count]]
        values = [ref[1] for ref in refs[:count]]
        wide = [jnp.concatenate([v, jnp.ones(v.shape, v.dtype)], axis=1) for v in values]

        def scores_of(first):
            q = take(q_ref, first, step)
            return [dot_nt(q, k) for k in keys]

        coming = scores_of(0)
        for first in range(0, group_size, step):
            scores = coming
            if first + step < group_size:
                coming = scores_of(first + step)
            tops = [s[:, n * HD : (n + 1) * HD] for s in scores for n in range(length // HD)]
            top = jnp.max(functools.reduce(jnp.maximum, tops), axis=1, keepdims=True)
            out = None
            for s, v in zip(scores, wide):
                probs = jnp.exp2((s - top) * FACTOR).astype(jnp.bfloat16)
                part = dot_nn(probs, v)
                out = part if out is None else out + part
            total = out[:, HD:]
            put(mixed_ref, first, step, out[:, :HD] / total)
            put(level_ref, first, step, top * FACTOR + jnp.log2(total))

    spec_wide = pl.BlockSpec((tokens, group_size * HD), lambda head, slot: (slot, head))
    spec_c = pl.BlockSpec((2, length, HD), lambda head, slot: (0, 0, head))
    spec_mark = pl.BlockSpec((8, HD), lambda head, slot: (0, 0))
    return pl.pallas_call(
        body,
        grid=(heads, slots),
        in_specs=[spec_wide] + [spec_c] * count + [ANYWHERE] * len(waits),
        out_specs=[spec_wide] * 2 + [spec_mark],
        out_shape=[jax.ShapeDtypeStruct(queries.shape, jnp.float32)] * 2
        + [jax.ShapeDtypeStruct((8, HD), jnp.float32)],
        name="attend_cache",
        **settings(20),
    )(queries, *caches, *waits)


def part_spec(part, kind, tokens):
    if len(part.shape) == 3:
        return pl.BlockSpec((None, tokens, HD), lambda slot, head: (kind, slot, head))
    return pl.BlockSpec((tokens, HD), lambda slot, head: (slot, head))


def sum_refs(refs):
    return functools.reduce(jnp.add, [ref[...].astype(jnp.float32) for ref in refs])


def attend_own(slots, group_size, queries, parts, table, state):
    count = len(parts)
    tokens = queries.shape[0] // slots
    heads = queries.shape[1] // (group_size * HD)

    def body(q_ref, *refs):
        table_ref, mixed_ref, level_ref, out_ref, probs_ref = refs[count:]
        key = sum_refs(refs[:count])
        key = key * table_ref[0] + pltpu.roll(key, HD // 2, 1) * table_ref[1]
        key = key.astype(jnp.bfloat16)
        ones = jnp.ones((tokens, HD), jnp.bfloat16)
        row = lax.broadcasted_iota(jnp.int32, (tokens, tokens), 0)
        causal = row >= lax.broadcasted_iota(jnp.int32, (tokens, tokens), 1)
        causal = jnp.concatenate([causal] * group_size, axis=0)
        scores = dot_nt(take(q_ref, 0, group_size), key) * FACTOR
        scores = jnp.where(causal, scores, -1e30)
        level = take(level_ref, 0, group_size)
        top = jnp.max(jnp.maximum(level, scores), axis=1, keepdims=True)
        probs = jnp.exp2(scores - top)
        kept = jnp.exp2(level - top)
        inverse = 1.0 / (kept + dot_nn(probs.astype(jnp.bfloat16), ones))
        put(out_ref, 0, group_size, take(mixed_ref, 0, group_size) * (kept * inverse))
        put(probs_ref, 0, group_size, probs * inverse)

    spec_wide = pl.BlockSpec((tokens, group_size * HD), lambda slot, head: (slot, head))
    spec_table = pl.BlockSpec(table.shape, lambda slot, head: (0, 0, 0))
    kept_back = [pltpu.with_memory_space_constraint(x, pltpu.HBM) for x in (table, *state)]
    return pl.pallas_call(
        body,
        grid=(slots, heads),
        in_specs=[spec_wide]
        + [part_spec(part, 0, tokens) for part in parts]
        + [spec_table, spec_wide, spec_wide],
        out_specs=[spec_wide] * 2,
        out_shape=[
            jax.ShapeDtypeStruct(queries.shape, jnp.float32),
            jax.ShapeDtypeStruct(queries.shape, queries.dtype),
        ],
        name="attend_own",
        **settings(24),
    )(queries, *parts, *kept_back)


def finish(slots, group_size, live, mixed, probs, parts):
    count = len(parts)
    tokens = mixed.shape[0] // slots
    heads = mixed.shape[1] // (group_size * HD)

    def body(live_ref, mixed_ref, probs_ref, *refs):
        value = sum_refs(refs[:count]).astype(jnp.bfloat16)
        out = take(mixed_ref, 0, group_size) + dot_nn(take(probs_ref, 0, group_size), value)
        put(refs[-1], 0, group_size, jnp.where(pl.program_id(0) < live_ref[0], out, 0.0))

    spec_wide = pl.BlockSpec((tokens, group_size * HD), lambda slot, head: (slot, head))
    return pl.pallas_call(
        body,
        grid=(slots, heads),
        in_specs=[pl.BlockSpec(memory_space=pltpu.SMEM)]
        + [spec_wide] * 2
        + [part_spec(part, 1, tokens) for part in parts],
        out_specs=spec_wide,
        out_shape=jax.ShapeDtypeStruct(mixed.shape, jnp.bfloat16),
        name="finish",
        **settings(20),
    )(live, mixed, probs, *parts)


def rotation_tables(extent, offset):
    orders = np.arange(HD // 2, dtype=np.float64)
    inverse = np.exp(-(2.0 * orders / HD) * math.log(500000.0))
    angles = (offset + np.arange(extent))[:, None] * inverse[None, :]
    cosine, sine = np.cos(angles), np.sin(angles)
    halves = [np.concatenate([cosine, cosine], axis=1), np.concatenate([-sine, sine], axis=1)]
    return jnp.asarray(np.stack(halves), jnp.float32)


def on_device(sizes, hidden, queries, prompt_keys, prompt_values, key_weight, value_weight, counts):
    n_groups, n_fsdp, n_resp, n_tp = sizes
    _, slots, tokens, part_width = hidden.shape
    block, columns = key_weight.shape
    group_size = queries.shape[3] // columns
    rows = slots * tokens
    plane = ("groups", "resp")
    cores = [(n, (n + 1) % n_tp) for n in range(n_tp)]
    ring = line_ring(n_fsdp)
    rightward = [(ring[n], ring[(n + 1) % n_fsdp]) for n in range(n_fsdp)]
    leftward = [(b, a) for a, b in rightward]
    along = [(0, b) for b in range(1, n_resp)]
    across = [(a, b) for a in range(1, n_groups) for b in range(1, n_resp)]
    twins = [(a, 0) for a in range(1, n_groups)]
    sets = [(0, 0), *along, *twins, *across]

    def shift(a, b):
        return [
            (g * n_resp + r, (g + a) % n_groups * n_resp + (r + b) % n_resp)
            for g in range(n_groups)
            for r in range(n_resp)
        ]

    share, cache = pack_rows(n_groups, key_weight, value_weight, prompt_keys[0], prompt_values[0])

    caches = [cache]
    for b in range(1, n_resp):
        around = [(n, (n + b) % n_resp) for n in range(n_resp)]
        caches.append(lax.ppermute(cache, "resp", around))

    pieces = [(share, 0)]
    held = share
    for hop in range(1, n_fsdp // 2 + 1):
        held = lax.ppermute(held, "fsdp", rightward)
        pieces.append((held, hop))
    first_hop, ends = pieces[1][0], [held]
    held = share
    for hop in range(1, n_fsdp - n_fsdp // 2):
        held = lax.ppermute(held, "fsdp", leftward)
        pieces.append((held, -hop))
    ends.append(held)

    flat_queries = queries.reshape(rows, queries.shape[3])
    *state, mark = attend_cache(slots, group_size, flat_queries, caches, [first_hop])

    near = dict(zip(sets, pack_features(sizes, block, sets, hidden.reshape(rows, part_width))))
    for place in across:
        near[place] = after(near[place], first_hop)
    for place in sets[1:]:
        waits = ends if place in across else []
        moved = lax.ppermute(near[place], plane, shift(*place))
        near[place] = after(moved, mark, *waits)
    far = {place: lax.ppermute(near[place], "tp", cores) for place in sets}

    def send(p, x):
        return lax.ppermute(x, plane, shift(n_groups - p[0], n_resp - p[1]))

    narrow, wide = jnp.bfloat16, jnp.float32
    pairs = {p: (near[p], far[p]) for p in sets}
    sides = [*along, *twins]
    sums = project(
        n_fsdp, pieces, [pairs[p] for p in sides], narrow, waits=[near[p] for p in across]
    )
    both = [send(p, x) for p, x in zip(sides, sums)]
    far_sums = project(n_fsdp, pieces, [pairs[p] for p in across], narrow, apart=True)
    far_sums = [send(across[n // 2], x) for n, x in enumerate(far_sums)]
    own = project(n_fsdp, pieces, [pairs[sets[0]]], wide, waits=[sums[0]])
    key_parts = [*own, *both, *far_sums[0::2]]
    value_parts = [*own, *both, *far_sums[1::2]]

    table = rotation_tables(tokens, PLEN)
    state = attend_own(slots, group_size, flat_queries, key_parts, table, state)
    live = (counts[0] - lax.axis_index("resp") * slots).astype(jnp.int32)[None]
    out = finish(slots, group_size, live, *state, value_parts)
    return out.reshape(queries.shape)


def solution(mesh):
    placed = (
        P(("groups", "fsdp"), "resp", None, "tp"),
        P(("groups", "fsdp"), "resp", None, "tp"),
        P(("groups", "fsdp"), "resp", "tp"),
        P(("groups", "fsdp"), "resp", "tp"),
        P(("fsdp", "resp"), "tp"),
        P(("fsdp", "resp"), "tp"),
        P(("groups", "fsdp")),
    )
    sizes = tuple(mesh.shape[name] for name in ("groups", "fsdp", "resp", "tp"))
    return jax.shard_map(
        functools.partial(on_device, sizes),
        mesh=mesh,
        in_specs=placed,
        out_specs=P(("groups", "fsdp"), "resp", None, "tp"),
        check_vma=False,
    )
```

```python
import functools
import math

import jax
import jax.numpy as jnp
import numpy as np
from jax import lax
from jax.experimental import pallas as pl
from jax.experimental.pallas import tpu as pltpu
from jax.sharding import PartitionSpec as P

HD = 128
PLEN = 1024
FACTOR = HD**-0.5 * math.log2(math.e)
MIB = 1 << 20
ANYWHERE = pl.BlockSpec(memory_space=pl.ANY)
HBM = pl.BlockSpec(memory_space=pltpu.HBM)


def dot_nt(a, b):
    return lax.dot_general(a, b, (((1,), (1,)), ((), ())), preferred_element_type=jnp.float32)


def dot_nn(a, b):
    return lax.dot_general(a, b, (((1,), (0,)), ((), ())), preferred_element_type=jnp.float32)


def settings(limit):
    return {
        "compiler_params": pltpu.CompilerParams(vmem_limit_bytes=limit * MIB),
        "cost_estimate": pl.CostEstimate(flops=0, bytes_accessed=0, transcendentals=0),
    }


def after(value, *earlier):
    return pl.pallas_call(
        lambda *refs: None,
        in_specs=[ANYWHERE] * (1 + len(earlier)),
        out_specs=ANYWHERE,
        out_shape=jax.ShapeDtypeStruct(value.shape, value.dtype),
        input_output_aliases={0: 0},
        name="after",
        **settings(1),
    )(value, *earlier)


def run_copies(copies):
    for copy in copies:
        copy.start()
    for copy in copies:
        copy.wait()


def pack_rows(n_groups, key_weight, value_weight, prompt_keys, prompt_values):
    block, columns = key_weight.shape
    half = block // n_groups

    arguments = [
        pltpu.with_memory_space_constraint(x, pltpu.HBM)
        for x in (key_weight, value_weight, prompt_keys, prompt_values)
    ]

    def body(kw_ref, vw_ref, pk_ref, pv_ref, share_ref, cache_ref, sems):
        rows = pl.ds(pl.multiple_of(lax.axis_index("groups") * half, half), half)
        run_copies(
            [
                pltpu.make_async_copy(pk_ref, cache_ref.at[0], sems.at[0]),
                pltpu.make_async_copy(pv_ref, cache_ref.at[1], sems.at[1]),
                pltpu.make_async_copy(kw_ref.at[rows, :], share_ref.at[0], sems.at[2]),
                pltpu.make_async_copy(vw_ref.at[rows, :], share_ref.at[1], sems.at[3]),
            ]
        )

    return pl.pallas_call(
        body,
        in_specs=[HBM] * 4,
        out_specs=[ANYWHERE] * 2,
        out_shape=[
            jax.ShapeDtypeStruct((2, half, columns), key_weight.dtype),
            jax.ShapeDtypeStruct((2, *prompt_keys.shape), prompt_keys.dtype),
        ],
        scratch_shapes=[pltpu.SemaphoreType.DMA((4,))],
        name="pack_rows",
        **settings(1),
    )(*arguments)


def pack_features(sizes, block, sets, hidden):
    n_groups, n_fsdp, n_resp, n_tp = sizes
    rows, width = hidden.shape
    per_core = n_fsdp // n_tp
    half = block // n_groups

    def start_of(place, n):
        group = (lax.axis_index("groups") + place[0]) % n_groups
        resp = (lax.axis_index("resp") + place[1]) % n_resp
        return (n * n_resp + resp) * block + group * half

    if half % HD:
        return [
            jnp.concatenate(
                [
                    lax.dynamic_slice_in_dim(hidden, start_of(place, n), half, axis=1)
                    for n in range(per_core)
                ],
                axis=1,
            )
            for place in sets
        ]

    step = rows // 4

    def body(hidden_ref, *refs):
        outs, (held, sems) = refs[: len(sets)], refs[len(sets) :]
        copies = []
        for n in range(rows // step):
            part = pl.ds(n * step, step)
            copies.append(
                pltpu.make_async_copy(hidden_ref.at[part, :], held.at[part, :], sems.at[n])
            )
        for copy in copies:
            copy.start()
        for n, copy in enumerate(copies):
            copy.wait()
            part = slice(n * step, (n + 1) * step)
            for place, out in zip(sets, outs):
                for k in range(per_core):
                    first = pl.multiple_of(start_of(place, k), HD)
                    out[part, k * half : (k + 1) * half] = held[part, pl.ds(first, half)]

    shape = (rows, per_core * half)
    return pl.pallas_call(
        body,
        grid=(1,),
        in_specs=[HBM],
        out_specs=[pl.BlockSpec(shape, lambda _: (0, 0))] * len(sets),
        out_shape=[jax.ShapeDtypeStruct(shape, hidden.dtype)] * len(sets),
        scratch_shapes=[pltpu.VMEM((rows, width), hidden.dtype), pltpu.SemaphoreType.DMA((4,))],
        name="pack_features",
        **settings(12),
    )(pltpu.with_memory_space_constraint(hidden, pltpu.HBM))


def line_ring(size):
    return list(range(0, size, 2)) + list(range(1, size, 2))[::-1]


def owner_of(n_fsdp, hops):
    fsdp = lax.axis_index("fsdp")
    place = jnp.where(fsdp % 2 == 0, fsdp // 2, n_fsdp - (fsdp + 1) // 2)
    at = (place - hops + n_fsdp) % n_fsdp
    return jnp.where(at < n_fsdp // 2, 2 * at, 2 * n_fsdp - 1 - 2 * at)


def project(n_fsdp, pieces, pairs, types, waits=()):
    kinds, half, columns = pieces[0][0].shape
    rows, depth = pairs[0][0].shape
    dtype = pairs[0][0].dtype
    total, count = len(pieces), len(pairs)

    def body(*refs):
        piece_refs, refs = refs[:total], refs[total:]
        pair_refs, refs = refs[: 2 * count], refs[2 * count + len(waits) :]
        outs, weights = refs[:-1], refs[-1]
        core = lax.axis_index("tp")
        for ref, (_, hops) in zip(piece_refs, pieces):
            place = pl.ds(pl.multiple_of(owner_of(n_fsdp, hops) * half, half), half)
            for kind in range(kinds):
                weights[kind, place, :] = ref[kind]
        first = pl.ds(pl.multiple_of(core * depth, depth), depth)
        second = pl.ds(pl.multiple_of((1 - core) * depth, depth), depth)
        for n in range(count):
            near_ref, far_ref = pair_refs[2 * n : 2 * n + 2]
            for kind in range(kinds):
                sums = dot_nn(near_ref[...], weights[kind, first, :])
                sums = sums + dot_nn(far_ref[...], weights[kind, second, :])
                outs[n][kind] = sums.astype(outs[n].dtype)

    def whole(shape):
        return pl.BlockSpec(shape, lambda _: (0,) * len(shape))

    shape = (kinds, rows, columns)
    return pl.pallas_call(
        body,
        grid=(1,),
        in_specs=[whole((kinds, half, columns))] * total
        + [whole((rows, depth))] * (2 * count)
        + [ANYWHERE] * len(waits),
        out_specs=[whole(shape)] * count,
        out_shape=[jax.ShapeDtypeStruct(shape, t) for t in types],
        scratch_shapes=[pltpu.VMEM((kinds, n_fsdp * half, columns), dtype)],
        name="project",
        **settings(24),
    )(*[x for x, _ in pieces], *[x for pair in pairs for x in pair], *waits)


def take(ref, first, count):
    return jnp.concatenate(
        [ref[:, (first + n) * HD : (first + n + 1) * HD] for n in range(count)], axis=0
    )


def put(ref, first, count, value):
    tokens = ref.shape[0]
    value = jnp.broadcast_to(value, (count * tokens, HD)).astype(ref.dtype)
    for n in range(count):
        ref[:, (first + n) * HD : (first + n + 1) * HD] = value[n * tokens : (n + 1) * tokens]


def attend_cache(slots, group_size, queries, caches, waits):
    count = len(caches)
    tokens = queries.shape[0] // slots
    heads = queries.shape[1] // (group_size * HD)
    length = caches[0].shape[1]
    step = 2 if group_size % 2 == 0 else 1

    def body(q_ref, *refs):
        mixed_ref, level_ref, mark_ref = refs[-3:]
        mark_ref[...] = jnp.zeros(mark_ref.shape, mark_ref.dtype)
        keys = [ref[0] for ref in refs[:count]]
        values = [ref[1] for ref in refs[:count]]
        wide = [jnp.concatenate([v, jnp.ones(v.shape, v.dtype)], axis=1) for v in values]

        def scores_of(first):
            q = take(q_ref, first, step)
            return [dot_nt(q, k) for k in keys]

        lane = lax.broadcasted_iota(jnp.int32, (tokens, HD), 1)
        levels = jnp.zeros((tokens, HD), jnp.float32)
        coming = scores_of(0)
        for first in range(0, group_size, step):
            scores = coming
            if first + step < group_size:
                coming = scores_of(first + step)
            tops = [s[:, n * HD : (n + 1) * HD] for s in scores for n in range(length // HD)]
            top = jnp.max(functools.reduce(jnp.maximum, tops), axis=1, keepdims=True)
            out = None
            for s, v in zip(scores, wide):
                probs = jnp.exp2((s - top) * FACTOR).astype(jnp.bfloat16)
                part = dot_nn(probs, v)
                out = part if out is None else out + part
            total = out[:, HD:]
            put(mixed_ref, first, step, out[:, :HD] / total)
            level = top * FACTOR + jnp.log2(total)
            for n in range(step):
                levels = jnp.where(lane == first + n, level[n * tokens : (n + 1) * tokens], levels)
        level_ref[...] = levels

    spec_wide = pl.BlockSpec((tokens, group_size * HD), lambda head, slot: (slot, head))
    spec_c = pl.BlockSpec((2, length, HD), lambda head, slot: (0, 0, head))
    spec_level = pl.BlockSpec((tokens, HD), lambda head, slot: (slot, head))
    spec_mark = pl.BlockSpec((8, HD), lambda head, slot: (0, 0))
    return pl.pallas_call(
        body,
        grid=(heads, slots),
        in_specs=[spec_wide] + [spec_c] * count + [ANYWHERE] * len(waits),
        out_specs=[spec_wide, spec_level, spec_mark],
        out_shape=[
            jax.ShapeDtypeStruct(queries.shape, queries.dtype),
            jax.ShapeDtypeStruct((slots * tokens, heads * HD), jnp.float32),
            jax.ShapeDtypeStruct((8, HD), jnp.float32),
        ],
        name="attend_cache",
        **settings(20),
    )(queries, *caches, *waits)


def attend_own(slots, group_size, live, queries, parts, table, state):
    count = len(parts)
    tokens = queries.shape[0] // slots
    heads = queries.shape[1] // (group_size * HD)

    def body(live_ref, q_ref, *refs):
        part_refs = refs[:count]
        table_ref, mixed_ref, level_ref, out_ref = refs[count:]
        slot = pl.program_id(0)

        def summed(kind):
            return functools.reduce(jnp.add, [ref[kind].astype(jnp.float32) for ref in part_refs])

        key = summed(0)
        key = key * table_ref[0] + pltpu.roll(key, HD // 2, 1) * table_ref[1]
        key = key.astype(jnp.bfloat16)
        value = summed(1).astype(jnp.bfloat16)
        wide = jnp.concatenate([value, jnp.ones((tokens, HD), jnp.bfloat16)], axis=1)
        row = lax.broadcasted_iota(jnp.int32, (tokens, tokens), 0)
        causal = row >= lax.broadcasted_iota(jnp.int32, (tokens, tokens), 1)
        causal = jnp.concatenate([causal] * group_size, axis=0)
        scores = dot_nt(take(q_ref, 0, group_size), key) * FACTOR
        scores = jnp.where(causal, scores, -1e30)
        level = jnp.concatenate([level_ref[:, n : n + 1] for n in range(group_size)], axis=0)
        top = jnp.maximum(level, jnp.max(scores, axis=1, keepdims=True))
        probs = jnp.exp2(scores - top).astype(jnp.bfloat16)
        kept = jnp.exp2(level - top)
        out = dot_nn(probs, wide)
        mixed = take(mixed_ref, 0, group_size).astype(jnp.float32) * kept + out[:, :HD]
        total = kept + out[:, HD:]
        inverse = pl.reciprocal(total, approx=True)
        result = mixed * (inverse * (2.0 - total * inverse))
        put(out_ref, 0, group_size, jnp.where(slot < live_ref[0], result, 0.0))

    spec_wide = pl.BlockSpec((tokens, group_size * HD), lambda slot, head: (slot, head))
    spec_part = pl.BlockSpec((2, tokens, HD), lambda slot, head: (0, slot, head))
    spec_part_level = pl.BlockSpec((tokens, HD), lambda slot, head: (slot, head))
    spec_table = pl.BlockSpec(table.shape, lambda slot, head: (0, 0, 0))
    kept_back = [pltpu.with_memory_space_constraint(x, pltpu.HBM) for x in (table, *state)]
    return pl.pallas_call(
        body,
        grid=(slots, heads),
        in_specs=[pl.BlockSpec(memory_space=pltpu.SMEM), spec_wide]
        + [spec_part] * count
        + [spec_table, spec_wide, spec_part_level],
        out_specs=spec_wide,
        out_shape=jax.ShapeDtypeStruct(queries.shape, queries.dtype),
        name="attend_own",
        **settings(24),
    )(live, queries, *parts, *kept_back)


def rotation_tables(extent, offset):
    orders = np.arange(HD // 2, dtype=np.float64)
    inverse = np.exp(-(2.0 * orders / HD) * math.log(500000.0))
    angles = (offset + np.arange(extent))[:, None] * inverse[None, :]
    cosine, sine = np.cos(angles), np.sin(angles)
    halves = [np.concatenate([cosine, cosine], axis=1), np.concatenate([-sine, sine], axis=1)]
    return jnp.asarray(np.stack(halves), jnp.float32)


def on_device(sizes, hidden, queries, prompt_keys, prompt_values, key_weight, value_weight, counts):
    n_groups, n_fsdp, n_resp, n_tp = sizes
    _, slots, tokens, part_width = hidden.shape
    block, columns = key_weight.shape
    group_size = queries.shape[3] // columns
    rows = slots * tokens
    plane = ("groups", "resp")
    cores = [(n, (n + 1) % n_tp) for n in range(n_tp)]
    ring = line_ring(n_fsdp)
    rightward = [(ring[n], ring[(n + 1) % n_fsdp]) for n in range(n_fsdp)]
    leftward = [(b, a) for a, b in rightward]
    along = [(0, b) for b in range(1, n_resp)]
    across = [(a, b) for a in range(1, n_groups) for b in range(1, n_resp)]
    twins = [(a, 0) for a in range(1, n_groups)]
    sets = [(0, 0), *along, *twins, *across]

    def shift(a, b):
        return [
            (g * n_resp + r, (g + a) % n_groups * n_resp + (r + b) % n_resp)
            for g in range(n_groups)
            for r in range(n_resp)
        ]

    share, cache = pack_rows(n_groups, key_weight, value_weight, prompt_keys[0], prompt_values[0])

    caches = [cache]
    for b in range(1, n_resp):
        around = [(n, (n + b) % n_resp) for n in range(n_resp)]
        caches.append(lax.ppermute(cache, "resp", around))

    pieces = [(share, 0)]
    held = share
    for hop in range(1, n_fsdp // 2 + 1):
        held = lax.ppermute(held, "fsdp", rightward)
        pieces.append((held, hop))
    first_hop, ends = pieces[1][0], [held]
    held = share
    for hop in range(1, n_fsdp - n_fsdp // 2):
        held = lax.ppermute(held, "fsdp", leftward)
        pieces.append((held, -hop))
    ends.append(held)

    flat_queries = queries.reshape(rows, queries.shape[3])
    *state, mark = attend_cache(slots, group_size, flat_queries, caches, [first_hop])

    near = dict(zip(sets, pack_features(sizes, block, sets, hidden.reshape(rows, part_width))))
    for place in across:
        near[place] = after(near[place], first_hop)
    for place in sets[1:]:
        waits = ends if place in across else []
        moved = lax.ppermute(near[place], plane, shift(*place))
        near[place] = after(moved, mark, *waits)
    far = {place: lax.ppermute(near[place], "tp", cores) for place in sets}

    narrow, wide = jnp.bfloat16, jnp.float32
    parts = []
    for chosen, waits in (([*along, *twins, sets[0]], [near[p] for p in across]), (across, [])):
        types = [narrow if any(p) else wide for p in chosen]
        sums = project(n_fsdp, pieces, [(near[p], far[p]) for p in chosen], types, waits)
        for p, x in zip(chosen, sums):
            back = shift(n_groups - p[0], n_resp - p[1])
            parts.append(lax.ppermute(x, plane, back) if any(p) else x)

    table = rotation_tables(tokens, PLEN)
    live = (counts[0] - lax.axis_index("resp") * slots).astype(jnp.int32)[None]
    out = attend_own(slots, group_size, live, flat_queries, parts, table, state)
    return out.reshape(queries.shape)


def solution(mesh):
    placed = (
        P(("groups", "fsdp"), "resp", None, "tp"),
        P(("groups", "fsdp"), "resp", None, "tp"),
        P(("groups", "fsdp"), "resp", "tp"),
        P(("groups", "fsdp"), "resp", "tp"),
        P(("fsdp", "resp"), "tp"),
        P(("fsdp", "resp"), "tp"),
        P(("groups", "fsdp")),
    )
    sizes = tuple(mesh.shape[name] for name in ("groups", "fsdp", "resp", "tp"))
    return jax.shard_map(
        functools.partial(on_device, sizes),
        mesh=mesh,
        in_specs=placed,
        out_specs=P(("groups", "fsdp"), "resp", None, "tp"),
        check_vma=False,
    )
```

```python
import functools
import math

import jax
import jax.numpy as jnp
import numpy as np
from jax import lax
from jax.experimental import pallas as pl
from jax.experimental.pallas import tpu as pltpu
from jax.sharding import PartitionSpec as P

HD = 128
PLEN = 1024
FACTOR = HD**-0.5 * math.log2(math.e)
MIB = 1 << 20
ANYWHERE = pl.BlockSpec(memory_space=pl.ANY)
HBM = pl.BlockSpec(memory_space=pltpu.HBM)


def dot_nt(a, b):
    return lax.dot_general(a, b, (((1,), (1,)), ((), ())), preferred_element_type=jnp.float32)


def dot_nn(a, b):
    return lax.dot_general(a, b, (((1,), (0,)), ((), ())), preferred_element_type=jnp.float32)


def settings(limit):
    return {
        "compiler_params": pltpu.CompilerParams(vmem_limit_bytes=limit * MIB),
        "cost_estimate": pl.CostEstimate(flops=0, bytes_accessed=0, transcendentals=0),
    }


def after(value, *earlier):
    return pl.pallas_call(
        lambda *refs: None,
        in_specs=[ANYWHERE] * (1 + len(earlier)),
        out_specs=ANYWHERE,
        out_shape=jax.ShapeDtypeStruct(value.shape, value.dtype),
        input_output_aliases={0: 0},
        name="after",
        **settings(1),
    )(value, *earlier)


def run_copies(copies):
    for copy in copies:
        copy.start()
    for copy in copies:
        copy.wait()


def pack_rows(n_groups, key_weight, value_weight, prompt_keys, prompt_values):
    block, columns = key_weight.shape
    half = block // n_groups

    arguments = [
        pltpu.with_memory_space_constraint(x, pltpu.HBM)
        for x in (key_weight, value_weight, prompt_keys, prompt_values)
    ]

    def body(kw_ref, vw_ref, pk_ref, pv_ref, share_ref, cache_ref, sems):
        rows = pl.ds(pl.multiple_of(lax.axis_index("groups") * half, half), half)
        run_copies(
            [
                pltpu.make_async_copy(pk_ref, cache_ref.at[0], sems.at[0]),
                pltpu.make_async_copy(pv_ref, cache_ref.at[1], sems.at[1]),
                pltpu.make_async_copy(kw_ref.at[rows, :], share_ref.at[0], sems.at[2]),
                pltpu.make_async_copy(vw_ref.at[rows, :], share_ref.at[1], sems.at[3]),
            ]
        )

    return pl.pallas_call(
        body,
        in_specs=[HBM] * 4,
        out_specs=[ANYWHERE] * 2,
        out_shape=[
            jax.ShapeDtypeStruct((2, half, columns), key_weight.dtype),
            jax.ShapeDtypeStruct((2, *prompt_keys.shape), prompt_keys.dtype),
        ],
        scratch_shapes=[pltpu.SemaphoreType.DMA((4,))],
        name="pack_rows",
        **settings(1),
    )(*arguments)


def pack_features(sizes, block, sets, hidden):
    n_groups, n_fsdp, n_resp, n_tp = sizes
    rows, width = hidden.shape
    per_core = n_fsdp // n_tp
    half = block // n_groups

    def start_of(place, n):
        group = (lax.axis_index("groups") + place[0]) % n_groups
        resp = (lax.axis_index("resp") + place[1]) % n_resp
        return (n * n_resp + resp) * block + group * half

    if half % HD:
        return [
            jnp.concatenate(
                [
                    lax.dynamic_slice_in_dim(hidden, start_of(place, n), half, axis=1)
                    for n in range(per_core)
                ],
                axis=1,
            )
            for place in sets
        ]

    step = rows // 4

    def body(hidden_ref, *refs):
        outs, (held, sems) = refs[: len(sets)], refs[len(sets) :]
        copies = []
        for n in range(rows // step):
            part = pl.ds(n * step, step)
            copies.append(
                pltpu.make_async_copy(hidden_ref.at[part, :], held.at[part, :], sems.at[n])
            )
        for copy in copies:
            copy.start()
        for n, copy in enumerate(copies):
            copy.wait()
            part = slice(n * step, (n + 1) * step)
            for place, out in zip(sets, outs):
                for k in range(per_core):
                    first = pl.multiple_of(start_of(place, k), HD)
                    out[part, k * half : (k + 1) * half] = held[part, pl.ds(first, half)]

    shape = (rows, per_core * half)
    return pl.pallas_call(
        body,
        grid=(1,),
        in_specs=[HBM],
        out_specs=[pl.BlockSpec(shape, lambda _: (0, 0))] * len(sets),
        out_shape=[jax.ShapeDtypeStruct(shape, hidden.dtype)] * len(sets),
        scratch_shapes=[pltpu.VMEM((rows, width), hidden.dtype), pltpu.SemaphoreType.DMA((4,))],
        name="pack_features",
        **settings(12),
    )(pltpu.with_memory_space_constraint(hidden, pltpu.HBM))


def line_ring(size):
    return list(range(0, size, 2)) + list(range(1, size, 2))[::-1]


def owner_of(n_fsdp, hops):
    fsdp = lax.axis_index("fsdp")
    place = jnp.where(fsdp % 2 == 0, fsdp // 2, n_fsdp - (fsdp + 1) // 2)
    at = (place - hops + n_fsdp) % n_fsdp
    return jnp.where(at < n_fsdp // 2, 2 * at, 2 * n_fsdp - 1 - 2 * at)


def project(n_fsdp, pieces, pairs, types, waits=()):
    kinds, half, columns = pieces[0][0].shape
    rows, depth = pairs[0][0].shape
    dtype = pairs[0][0].dtype
    total, count = len(pieces), len(pairs)

    def body(*refs):
        piece_refs, refs = refs[:total], refs[total:]
        pair_refs, refs = refs[: 2 * count], refs[2 * count + len(waits) :]
        outs, weights = refs[:-1], refs[-1]
        core = lax.axis_index("tp")
        for ref, (_, hops) in zip(piece_refs, pieces):
            place = pl.ds(pl.multiple_of(owner_of(n_fsdp, hops) * half, half), half)
            for kind in range(kinds):
                weights[kind, place, :] = ref[kind]
        first = pl.ds(pl.multiple_of(core * depth, depth), depth)
        second = pl.ds(pl.multiple_of((1 - core) * depth, depth), depth)
        for n in range(count):
            near_ref, far_ref = pair_refs[2 * n : 2 * n + 2]
            for kind in range(kinds):
                sums = dot_nn(near_ref[...], weights[kind, first, :])
                sums = sums + dot_nn(far_ref[...], weights[kind, second, :])
                outs[n][kind] = sums.astype(outs[n].dtype)

    def whole(shape):
        return pl.BlockSpec(shape, lambda _: (0,) * len(shape))

    shape = (kinds, rows, columns)
    return pl.pallas_call(
        body,
        grid=(1,),
        in_specs=[whole((kinds, half, columns))] * total
        + [whole((rows, depth))] * (2 * count)
        + [ANYWHERE] * len(waits),
        out_specs=[whole(shape)] * count,
        out_shape=[jax.ShapeDtypeStruct(shape, t) for t in types],
        scratch_shapes=[pltpu.VMEM((kinds, n_fsdp * half, columns), dtype)],
        name="project",
        **settings(24),
    )(*[x for x, _ in pieces], *[x for pair in pairs for x in pair], *waits)


def take(ref, first, count):
    return jnp.concatenate(
        [ref[:, (first + n) * HD : (first + n + 1) * HD] for n in range(count)], axis=0
    )


def put(ref, first, count, value):
    tokens = ref.shape[0]
    value = jnp.broadcast_to(value, (count * tokens, HD)).astype(ref.dtype)
    for n in range(count):
        ref[:, (first + n) * HD : (first + n + 1) * HD] = value[n * tokens : (n + 1) * tokens]


def attend_cache(slots, group_size, queries, caches, waits):
    count = len(caches)
    tokens = queries.shape[0] // slots
    heads = queries.shape[1] // (group_size * HD)
    length = caches[0].shape[1]
    step = 2 if group_size % 2 == 0 else 1

    def body(q_ref, *refs):
        mixed_ref, level_ref, mark_ref = refs[-3:]
        mark_ref[...] = jnp.zeros(mark_ref.shape, mark_ref.dtype)
        keys = [ref[0] for ref in refs[:count]]
        values = [ref[1] for ref in refs[:count]]
        wide = [jnp.concatenate([v, jnp.ones(v.shape, v.dtype)], axis=1) for v in values]

        def scores_of(first):
            q = take(q_ref, first, step)
            return [dot_nt(q, k) for k in keys]

        coming = scores_of(0)
        for first in range(0, group_size, step):
            scores = coming
            if first + step < group_size:
                coming = scores_of(first + step)
            tops = [s[:, n * HD : (n + 1) * HD] for s in scores for n in range(length // HD)]
            top = jnp.max(functools.reduce(jnp.maximum, tops), axis=1, keepdims=True)
            out = None
            for s, v in zip(scores, wide):
                probs = jnp.exp2((s - top) * FACTOR).astype(jnp.bfloat16)
                part = dot_nn(probs, v)
                out = part if out is None else out + part
            total = out[:, HD:]
            put(mixed_ref, first, step, out[:, :HD] / total)
            put(level_ref, first, step, top * FACTOR + jnp.log2(total))

    spec_wide = pl.BlockSpec((tokens, group_size * HD), lambda head, slot: (slot, head))
    spec_c = pl.BlockSpec((2, length, HD), lambda head, slot: (0, 0, head))
    spec_mark = pl.BlockSpec((8, HD), lambda head, slot: (0, 0))
    return pl.pallas_call(
        body,
        grid=(heads, slots),
        in_specs=[spec_wide] + [spec_c] * count + [ANYWHERE] * len(waits),
        out_specs=[spec_wide] * 2 + [spec_mark],
        out_shape=[jax.ShapeDtypeStruct(queries.shape, jnp.float32)] * 2
        + [jax.ShapeDtypeStruct((8, HD), jnp.float32)],
        name="attend_cache",
        **settings(20),
    )(queries, *caches, *waits)


def attend_own(slots, group_size, live, queries, parts, table, state):
    count = len(parts)
    tokens = queries.shape[0] // slots
    heads = queries.shape[1] // (group_size * HD)

    def body(live_ref, q_ref, *refs):
        part_refs = refs[:count]
        table_ref, mixed_ref, level_ref, out_ref = refs[count:]
        slot = pl.program_id(0)

        def summed(kind):
            return functools.reduce(jnp.add, [ref[kind].astype(jnp.float32) for ref in part_refs])

        key = summed(0)
        key = key * table_ref[0] + pltpu.roll(key, HD // 2, 1) * table_ref[1]
        key = key.astype(jnp.bfloat16)
        value = summed(1).astype(jnp.bfloat16)
        wide = jnp.concatenate([value, jnp.ones((tokens, HD), jnp.bfloat16)], axis=1)
        row = lax.broadcasted_iota(jnp.int32, (tokens, tokens), 0)
        causal = row >= lax.broadcasted_iota(jnp.int32, (tokens, tokens), 1)
        causal = jnp.concatenate([causal] * group_size, axis=0)
        scores = dot_nt(take(q_ref, 0, group_size), key) * FACTOR
        scores = jnp.where(causal, scores, -1e30)
        level = take(level_ref, 0, group_size)
        top = jnp.max(jnp.maximum(level, scores), axis=1, keepdims=True)
        probs = jnp.exp2(scores - top).astype(jnp.bfloat16)
        kept = jnp.exp2(level - top)
        out = dot_nn(probs, wide)
        mixed = take(mixed_ref, 0, group_size) * kept + out[:, :HD]
        total = kept + out[:, HD:]
        inverse = pl.reciprocal(total, approx=True)
        result = mixed * (inverse * (2.0 - total * inverse))
        put(out_ref, 0, group_size, jnp.where(slot < live_ref[0], result, 0.0))

    spec_wide = pl.BlockSpec((tokens, group_size * HD), lambda slot, head: (slot, head))
    spec_part = pl.BlockSpec((2, tokens, HD), lambda slot, head: (0, slot, head))
    spec_table = pl.BlockSpec(table.shape, lambda slot, head: (0, 0, 0))
    kept_back = [pltpu.with_memory_space_constraint(x, pltpu.HBM) for x in (table, *state)]
    return pl.pallas_call(
        body,
        grid=(slots, heads),
        in_specs=[pl.BlockSpec(memory_space=pltpu.SMEM), spec_wide]
        + [spec_part] * count
        + [spec_table, spec_wide, spec_wide],
        out_specs=spec_wide,
        out_shape=jax.ShapeDtypeStruct(queries.shape, queries.dtype),
        name="attend_own",
        **settings(24),
    )(live, queries, *parts, *kept_back)


def rotation_tables(extent, offset):
    orders = np.arange(HD // 2, dtype=np.float64)
    inverse = np.exp(-(2.0 * orders / HD) * math.log(500000.0))
    angles = (offset + np.arange(extent))[:, None] * inverse[None, :]
    cosine, sine = np.cos(angles), np.sin(angles)
    halves = [np.concatenate([cosine, cosine], axis=1), np.concatenate([-sine, sine], axis=1)]
    return jnp.asarray(np.stack(halves), jnp.float32)


def on_device(sizes, hidden, queries, prompt_keys, prompt_values, key_weight, value_weight, counts):
    n_groups, n_fsdp, n_resp, n_tp = sizes
    _, slots, tokens, part_width = hidden.shape
    block, columns = key_weight.shape
    group_size = queries.shape[3] // columns
    rows = slots * tokens
    plane = ("groups", "resp")
    cores = [(n, (n + 1) % n_tp) for n in range(n_tp)]
    ring = line_ring(n_fsdp)
    rightward = [(ring[n], ring[(n + 1) % n_fsdp]) for n in range(n_fsdp)]
    leftward = [(b, a) for a, b in rightward]
    along = [(0, b) for b in range(1, n_resp)]
    across = [(a, b) for a in range(1, n_groups) for b in range(1, n_resp)]
    twins = [(a, 0) for a in range(1, n_groups)]
    sets = [(0, 0), *across, *twins, *along]

    def shift(a, b):
        return [
            (g * n_resp + r, (g + a) % n_groups * n_resp + (r + b) % n_resp)
            for g in range(n_groups)
            for r in range(n_resp)
        ]

    share, cache = pack_rows(n_groups, key_weight, value_weight, prompt_keys[0], prompt_values[0])

    caches = [cache]
    for b in range(1, n_resp):
        around = [(n, (n + b) % n_resp) for n in range(n_resp)]
        caches.append(lax.ppermute(cache, "resp", around))

    pieces = [(share, 0)]
    held = share
    for hop in range(1, n_fsdp // 2 + 1):
        held = lax.ppermute(held, "fsdp", rightward)
        pieces.append((held, hop))
    first_hop, ends = pieces[1][0], [held]
    held = share
    for hop in range(1, n_fsdp - n_fsdp // 2):
        held = lax.ppermute(held, "fsdp", leftward)
        pieces.append((held, -hop))
    ends.append(held)

    flat_queries = queries.reshape(rows, queries.shape[3])
    *state, mark = attend_cache(slots, group_size, flat_queries, caches, [first_hop])

    near = dict(zip(sets, pack_features(sizes, block, sets, hidden.reshape(rows, part_width))))
    for place in along:
        near[place] = after(near[place], first_hop)
    for place in sets[1:]:
        waits = ends if place in along else []
        moved = lax.ppermute(near[place], plane, shift(*place))
        near[place] = after(moved, mark, *waits)
    far = {place: lax.ppermute(near[place], "tp", cores) for place in sets}

    narrow, wide = jnp.bfloat16, jnp.float32
    parts = []
    for chosen, waits in (([*across, *twins, sets[0]], [near[p] for p in along]), (along, [])):
        types = [narrow if any(p) else wide for p in chosen]
        sums = project(n_fsdp, pieces, [(near[p], far[p]) for p in chosen], types, waits)
        for p, x in zip(chosen, sums):
            back = shift(n_groups - p[0], n_resp - p[1])
            parts.append(lax.ppermute(x, plane, back) if any(p) else x)

    table = rotation_tables(tokens, PLEN)
    live = (counts[0] - lax.axis_index("resp") * slots).astype(jnp.int32)[None]
    out = attend_own(slots, group_size, live, flat_queries, parts, table, state)
    return out.reshape(queries.shape)


def solution(mesh):
    placed = (
        P(("groups", "fsdp"), "resp", None, "tp"),
        P(("groups", "fsdp"), "resp", None, "tp"),
        P(("groups", "fsdp"), "resp", "tp"),
        P(("groups", "fsdp"), "resp", "tp"),
        P(("fsdp", "resp"), "tp"),
        P(("fsdp", "resp"), "tp"),
        P(("groups", "fsdp")),
    )
    sizes = tuple(mesh.shape[name] for name in ("groups", "fsdp", "resp", "tp"))
    return jax.shard_map(
        functools.partial(on_device, sizes),
        mesh=mesh,
        in_specs=placed,
        out_specs=P(("groups", "fsdp"), "resp", None, "tp"),
        check_vma=False,
    )
```

```python
import functools
import math

import jax
import jax.numpy as jnp
import numpy as np
from jax import lax
from jax.experimental import pallas as pl
from jax.experimental.pallas import tpu as pltpu
from jax.sharding import PartitionSpec as P

HD = 128
PLEN = 1024
FACTOR = HD**-0.5 * math.log2(math.e)
MIB = 1 << 20
ANYWHERE = pl.BlockSpec(memory_space=pl.ANY)
HBM = pl.BlockSpec(memory_space=pltpu.HBM)


def dot_nt(a, b):
    return lax.dot_general(a, b, (((1,), (1,)), ((), ())), preferred_element_type=jnp.float32)


def dot_nn(a, b):
    return lax.dot_general(a, b, (((1,), (0,)), ((), ())), preferred_element_type=jnp.float32)


def settings(limit):
    return {
        "compiler_params": pltpu.CompilerParams(vmem_limit_bytes=limit * MIB),
        "cost_estimate": pl.CostEstimate(flops=0, bytes_accessed=0, transcendentals=0),
    }


def after(value, *earlier):
    return pl.pallas_call(
        lambda *refs: None,
        in_specs=[ANYWHERE] * (1 + len(earlier)),
        out_specs=ANYWHERE,
        out_shape=jax.ShapeDtypeStruct(value.shape, value.dtype),
        input_output_aliases={0: 0},
        name="after",
        **settings(1),
    )(value, *earlier)


def run_copies(copies):
    for copy in copies:
        copy.start()
    for copy in copies:
        copy.wait()


def pack_rows(n_groups, key_weight, value_weight, prompt_keys, prompt_values):
    block, columns = key_weight.shape
    half = block // n_groups

    arguments = [
        pltpu.with_memory_space_constraint(x, pltpu.HBM)
        for x in (key_weight, value_weight, prompt_keys, prompt_values)
    ]

    def body(kw_ref, vw_ref, pk_ref, pv_ref, share_ref, cache_ref, sems):
        rows = pl.ds(pl.multiple_of(lax.axis_index("groups") * half, half), half)
        run_copies(
            [
                pltpu.make_async_copy(pk_ref, cache_ref.at[0], sems.at[0]),
                pltpu.make_async_copy(pv_ref, cache_ref.at[1], sems.at[1]),
                pltpu.make_async_copy(kw_ref.at[rows, :], share_ref.at[0], sems.at[2]),
                pltpu.make_async_copy(vw_ref.at[rows, :], share_ref.at[1], sems.at[3]),
            ]
        )

    return pl.pallas_call(
        body,
        in_specs=[HBM] * 4,
        out_specs=[ANYWHERE] * 2,
        out_shape=[
            jax.ShapeDtypeStruct((2, half, columns), key_weight.dtype),
            jax.ShapeDtypeStruct((2, *prompt_keys.shape), prompt_keys.dtype),
        ],
        scratch_shapes=[pltpu.SemaphoreType.DMA((4,))],
        name="pack_rows",
        **settings(1),
    )(*arguments)


def pack_features(sizes, block, sets, hidden):
    n_groups, n_fsdp, n_resp, n_tp = sizes
    rows, width = hidden.shape
    per_core = n_fsdp // n_tp
    half = block // n_groups

    def start_of(place, n):
        group = (lax.axis_index("groups") + place[0]) % n_groups
        resp = (lax.axis_index("resp") + place[1]) % n_resp
        return (n * n_resp + resp) * block + group * half

    if half % HD:
        return [
            jnp.concatenate(
                [
                    lax.dynamic_slice_in_dim(hidden, start_of(place, n), half, axis=1)
                    for n in range(per_core)
                ],
                axis=1,
            )
            for place in sets
        ]

    step = rows // 4

    def body(hidden_ref, *refs):
        outs, (held, sems) = refs[: len(sets)], refs[len(sets) :]
        copies = []
        for n in range(rows // step):
            part = pl.ds(n * step, step)
            copies.append(
                pltpu.make_async_copy(hidden_ref.at[part, :], held.at[part, :], sems.at[n])
            )
        for copy in copies:
            copy.start()
        for n, copy in enumerate(copies):
            copy.wait()
            part = slice(n * step, (n + 1) * step)
            for place, out in zip(sets, outs):
                for k in range(per_core):
                    first = pl.multiple_of(start_of(place, k), HD)
                    out[part, k * half : (k + 1) * half] = held[part, pl.ds(first, half)]

    shape = (rows, per_core * half)
    return pl.pallas_call(
        body,
        grid=(1,),
        in_specs=[HBM],
        out_specs=[pl.BlockSpec(shape, lambda _: (0, 0))] * len(sets),
        out_shape=[jax.ShapeDtypeStruct(shape, hidden.dtype)] * len(sets),
        scratch_shapes=[pltpu.VMEM((rows, width), hidden.dtype), pltpu.SemaphoreType.DMA((4,))],
        name="pack_features",
        **settings(12),
    )(pltpu.with_memory_space_constraint(hidden, pltpu.HBM))


def line_ring(size):
    return list(range(0, size, 2)) + list(range(1, size, 2))[::-1]


def owner_of(n_fsdp, hops):
    fsdp = lax.axis_index("fsdp")
    place = jnp.where(fsdp % 2 == 0, fsdp // 2, n_fsdp - (fsdp + 1) // 2)
    at = (place - hops + n_fsdp) % n_fsdp
    return jnp.where(at < n_fsdp // 2, 2 * at, 2 * n_fsdp - 1 - 2 * at)


def project(n_fsdp, pieces, pairs, types, waits=()):
    kinds, half, columns = pieces[0][0].shape
    rows, depth = pairs[0][0].shape
    dtype = pairs[0][0].dtype
    total, count = len(pieces), len(pairs)

    def body(*refs):
        piece_refs, refs = refs[:total], refs[total:]
        pair_refs, refs = refs[: 2 * count], refs[2 * count + len(waits) :]
        outs, weights = refs[:-1], refs[-1]
        core = lax.axis_index("tp")
        for ref, (_, hops) in zip(piece_refs, pieces):
            place = pl.ds(pl.multiple_of(owner_of(n_fsdp, hops) * half, half), half)
            for kind in range(kinds):
                weights[kind, place, :] = ref[kind]
        first = pl.ds(pl.multiple_of(core * depth, depth), depth)
        second = pl.ds(pl.multiple_of((1 - core) * depth, depth), depth)
        for n in range(count):
            near_ref, far_ref = pair_refs[2 * n : 2 * n + 2]
            for kind in range(kinds):
                sums = dot_nn(near_ref[...], weights[kind, first, :])
                sums = sums + dot_nn(far_ref[...], weights[kind, second, :])
                outs[n][kind] = sums.astype(outs[n].dtype)

    def whole(shape):
        return pl.BlockSpec(shape, lambda _: (0,) * len(shape))

    shape = (kinds, rows, columns)
    return pl.pallas_call(
        body,
        grid=(1,),
        in_specs=[whole((kinds, half, columns))] * total
        + [whole((rows, depth))] * (2 * count)
        + [ANYWHERE] * len(waits),
        out_specs=[whole(shape)] * count,
        out_shape=[jax.ShapeDtypeStruct(shape, t) for t in types],
        scratch_shapes=[pltpu.VMEM((kinds, n_fsdp * half, columns), dtype)],
        name="project",
        **settings(24),
    )(*[x for x, _ in pieces], *[x for pair in pairs for x in pair], *waits)


def take(ref, first, count):
    return jnp.concatenate(
        [ref[:, (first + n) * HD : (first + n + 1) * HD] for n in range(count)], axis=0
    )


def put(ref, first, count, value):
    tokens = ref.shape[0]
    value = jnp.broadcast_to(value, (count * tokens, HD)).astype(ref.dtype)
    for n in range(count):
        ref[:, (first + n) * HD : (first + n + 1) * HD] = value[n * tokens : (n + 1) * tokens]


def attend_cache(slots, group_size, queries, caches, waits):
    count = len(caches)
    tokens = queries.shape[0] // slots
    heads = queries.shape[1] // (group_size * HD)
    length = caches[0].shape[1]
    step = 2 if group_size % 2 == 0 else 1

    def body(q_ref, *refs):
        mixed_ref, level_ref, mark_ref = refs[-3:]
        mark_ref[...] = jnp.zeros(mark_ref.shape, mark_ref.dtype)
        keys = [ref[0] for ref in refs[:count]]
        values = [ref[1] for ref in refs[:count]]
        wide = [jnp.concatenate([v, jnp.ones(v.shape, v.dtype)], axis=1) for v in values]

        def scores_of(first):
            q = take(q_ref, first, step)
            return [dot_nt(q, k) for k in keys]

        coming = scores_of(0)
        for first in range(0, group_size, step):
            scores = coming
            if first + step < group_size:
                coming = scores_of(first + step)
            tops = [s[:, n * HD : (n + 1) * HD] for s in scores for n in range(length // HD)]
            top = jnp.max(functools.reduce(jnp.maximum, tops), axis=1, keepdims=True)
            out = None
            for s, v in zip(scores, wide):
                probs = jnp.exp2((s - top) * FACTOR).astype(jnp.bfloat16)
                part = dot_nn(probs, v)
                out = part if out is None else out + part
            total = out[:, HD:]
            put(mixed_ref, first, step, out[:, :HD] / total)
            put(level_ref, first, step, top * FACTOR + jnp.log2(total))

    spec_wide = pl.BlockSpec((tokens, group_size * HD), lambda head, slot: (slot, head))
    spec_c = pl.BlockSpec((2, length, HD), lambda head, slot: (0, 0, head))
    spec_mark = pl.BlockSpec((8, HD), lambda head, slot: (0, 0))
    return pl.pallas_call(
        body,
        grid=(heads, slots),
        in_specs=[spec_wide] + [spec_c] * count + [ANYWHERE] * len(waits),
        out_specs=[spec_wide] * 2 + [spec_mark],
        out_shape=[jax.ShapeDtypeStruct(queries.shape, jnp.float32)] * 2
        + [jax.ShapeDtypeStruct((8, HD), jnp.float32)],
        name="attend_cache",
        **settings(20),
    )(queries, *caches, *waits)


def attend_own(slots, group_size, live, queries, parts, table, state):
    count = len(parts)
    tokens = queries.shape[0] // slots
    heads = queries.shape[1] // (group_size * HD)

    def body(live_ref, q_ref, *refs):
        part_refs = refs[:count]
        table_ref, mixed_ref, level_ref, out_ref = refs[count:]
        slot = pl.program_id(0)

        def summed(kind):
            return functools.reduce(jnp.add, [ref[kind].astype(jnp.float32) for ref in part_refs])

        key = summed(0)
        key = key * table_ref[0] + pltpu.roll(key, HD // 2, 1) * table_ref[1]
        key = key.astype(jnp.bfloat16)
        value = summed(1).astype(jnp.bfloat16)
        wide = jnp.concatenate([value, jnp.ones((tokens, HD), jnp.bfloat16)], axis=1)
        row = lax.broadcasted_iota(jnp.int32, (tokens, tokens), 0)
        causal = row >= lax.broadcasted_iota(jnp.int32, (tokens, tokens), 1)
        causal = jnp.concatenate([causal] * group_size, axis=0)
        scores = dot_nt(take(q_ref, 0, group_size), key) * FACTOR
        scores = jnp.where(causal, scores, -1e30)
        level = take(level_ref, 0, group_size)
        top = jnp.max(jnp.maximum(level, scores), axis=1, keepdims=True)
        probs = jnp.exp2(scores - top).astype(jnp.bfloat16)
        kept = jnp.exp2(level - top)
        out = dot_nn(probs, wide)
        mixed = take(mixed_ref, 0, group_size) * kept + out[:, :HD]
        total = kept + out[:, HD:]
        inverse = pl.reciprocal(total, approx=True)
        result = mixed * (inverse * (2.0 - total * inverse))
        put(out_ref, 0, group_size, jnp.where(slot < live_ref[0], result, 0.0))

    spec_wide = pl.BlockSpec((tokens, group_size * HD), lambda slot, head: (slot, head))
    spec_part = pl.BlockSpec((2, tokens, HD), lambda slot, head: (0, slot, head))
    spec_table = pl.BlockSpec(table.shape, lambda slot, head: (0, 0, 0))
    kept_back = [pltpu.with_memory_space_constraint(x, pltpu.HBM) for x in (table, *state)]
    return pl.pallas_call(
        body,
        grid=(slots, heads),
        in_specs=[pl.BlockSpec(memory_space=pltpu.SMEM), spec_wide]
        + [spec_part] * count
        + [spec_table, spec_wide, spec_wide],
        out_specs=spec_wide,
        out_shape=jax.ShapeDtypeStruct(queries.shape, queries.dtype),
        name="attend_own",
        **settings(24),
    )(live, queries, *parts, *kept_back)


def rotation_tables(extent, offset):
    orders = np.arange(HD // 2, dtype=np.float64)
    inverse = np.exp(-(2.0 * orders / HD) * math.log(500000.0))
    angles = (offset + np.arange(extent))[:, None] * inverse[None, :]
    cosine, sine = np.cos(angles), np.sin(angles)
    halves = [np.concatenate([cosine, cosine], axis=1), np.concatenate([-sine, sine], axis=1)]
    return jnp.asarray(np.stack(halves), jnp.float32)


def on_device(sizes, hidden, queries, prompt_keys, prompt_values, key_weight, value_weight, counts):
    n_groups, n_fsdp, n_resp, n_tp = sizes
    _, slots, tokens, part_width = hidden.shape
    block, columns = key_weight.shape
    group_size = queries.shape[3] // columns
    rows = slots * tokens
    plane = ("groups", "resp")
    cores = [(n, (n + 1) % n_tp) for n in range(n_tp)]
    ring = line_ring(n_fsdp)
    rightward = [(ring[n], ring[(n + 1) % n_fsdp]) for n in range(n_fsdp)]
    leftward = [(b, a) for a, b in rightward]
    along = [(0, b) for b in range(1, n_resp)]
    across = [(a, b) for a in range(1, n_groups) for b in range(1, n_resp)]
    twins = [(a, 0) for a in range(1, n_groups)]
    sets = [(0, 0), *across, *twins, *along]

    def shift(a, b):
        return [
            (g * n_resp + r, (g + a) % n_groups * n_resp + (r + b) % n_resp)
            for g in range(n_groups)
            for r in range(n_resp)
        ]

    share, cache = pack_rows(n_groups, key_weight, value_weight, prompt_keys[0], prompt_values[0])

    caches = [cache]
    for b in range(1, n_resp):
        around = [(n, (n + b) % n_resp) for n in range(n_resp)]
        caches.append(lax.ppermute(cache, "resp", around))

    pieces = [(share, 0)]
    held = share
    for hop in range(1, n_fsdp // 2 + 1):
        held = lax.ppermute(held, "fsdp", rightward)
        pieces.append((held, hop))
    first_hop, ends = pieces[1][0], [held]
    held = share
    for hop in range(1, n_fsdp - n_fsdp // 2):
        held = lax.ppermute(held, "fsdp", leftward)
        pieces.append((held, -hop))
    ends.append(held)

    flat_queries = queries.reshape(rows, queries.shape[3])
    *state, mark = attend_cache(slots, group_size, flat_queries, caches, [first_hop])

    near = dict(zip(sets, pack_features(sizes, block, sets, hidden.reshape(rows, part_width))))
    for place in along:
        near[place] = after(near[place], first_hop)
    for place in sets[1:]:
        waits = ends if place in along else []
        moved = lax.ppermute(near[place], plane, shift(*place))
        near[place] = after(moved, mark, *waits)
    far = {place: lax.ppermute(near[place], "tp", cores) for place in sets}

    parts, waits = [], [*(near[p] for p in along), far[sets[0]]]
    for chosen in (across, twins, along, sets[:1]):
        kind = jnp.bfloat16 if any(chosen[0]) else jnp.float32
        pairs = [(near[p], far[p]) for p in chosen]
        sums = project(n_fsdp, pieces, pairs, [kind] * len(chosen), waits)
        waits = [sums[0]]
        for p, x in zip(chosen, sums):
            back = shift(n_groups - p[0], n_resp - p[1])
            parts.append(lax.ppermute(x, plane, back) if any(p) else x)

    table = rotation_tables(tokens, PLEN)
    live = (counts[0] - lax.axis_index("resp") * slots).astype(jnp.int32)[None]
    out = attend_own(slots, group_size, live, flat_queries, parts, table, state)
    return out.reshape(queries.shape)


def solution(mesh):
    placed = (
        P(("groups", "fsdp"), "resp", None, "tp"),
        P(("groups", "fsdp"), "resp", None, "tp"),
        P(("groups", "fsdp"), "resp", "tp"),
        P(("groups", "fsdp"), "resp", "tp"),
        P(("fsdp", "resp"), "tp"),
        P(("fsdp", "resp"), "tp"),
        P(("groups", "fsdp")),
    )
    sizes = tuple(mesh.shape[name] for name in ("groups", "fsdp", "resp", "tp"))
    return jax.shard_map(
        functools.partial(on_device, sizes),
        mesh=mesh,
        in_specs=placed,
        out_specs=P(("groups", "fsdp"), "resp", None, "tp"),
        check_vma=False,
    )
```

```python
import functools
import math

import jax
import jax.numpy as jnp
import numpy as np
from jax import lax
from jax.experimental import pallas as pl
from jax.experimental.pallas import tpu as pltpu
from jax.sharding import PartitionSpec as P

HD = 128
PLEN = 1024
FACTOR = HD**-0.5 * math.log2(math.e)
MIB = 1 << 20
ANYWHERE = pl.BlockSpec(memory_space=pl.ANY)
HBM = pl.BlockSpec(memory_space=pltpu.HBM)


def dot_nt(a, b):
    return lax.dot_general(a, b, (((1,), (1,)), ((), ())), preferred_element_type=jnp.float32)


def dot_nn(a, b):
    return lax.dot_general(a, b, (((1,), (0,)), ((), ())), preferred_element_type=jnp.float32)


def settings(limit):
    return {
        "compiler_params": pltpu.CompilerParams(vmem_limit_bytes=limit * MIB),
        "cost_estimate": pl.CostEstimate(flops=0, bytes_accessed=0, transcendentals=0),
    }


def after(value, *earlier):
    return pl.pallas_call(
        lambda *refs: None,
        in_specs=[ANYWHERE] * (1 + len(earlier)),
        out_specs=ANYWHERE,
        out_shape=jax.ShapeDtypeStruct(value.shape, value.dtype),
        input_output_aliases={0: 0},
        name="after",
        **settings(1),
    )(value, *earlier)


def run_copies(copies):
    for copy in copies:
        copy.start()
    for copy in copies:
        copy.wait()


def pack_rows(n_groups, key_weight, value_weight, prompt_keys, prompt_values):
    block, columns = key_weight.shape
    half = block // n_groups

    arguments = [
        pltpu.with_memory_space_constraint(x, pltpu.HBM)
        for x in (key_weight, value_weight, prompt_keys, prompt_values)
    ]

    def body(kw_ref, vw_ref, pk_ref, pv_ref, share_ref, cache_ref, sems):
        rows = pl.ds(pl.multiple_of(lax.axis_index("groups") * half, half), half)
        run_copies(
            [
                pltpu.make_async_copy(pk_ref, cache_ref.at[0], sems.at[0]),
                pltpu.make_async_copy(pv_ref, cache_ref.at[1], sems.at[1]),
                pltpu.make_async_copy(kw_ref.at[rows, :], share_ref.at[0], sems.at[2]),
                pltpu.make_async_copy(vw_ref.at[rows, :], share_ref.at[1], sems.at[3]),
            ]
        )

    return pl.pallas_call(
        body,
        in_specs=[HBM] * 4,
        out_specs=[ANYWHERE] * 2,
        out_shape=[
            jax.ShapeDtypeStruct((2, half, columns), key_weight.dtype),
            jax.ShapeDtypeStruct((2, *prompt_keys.shape), prompt_keys.dtype),
        ],
        scratch_shapes=[pltpu.SemaphoreType.DMA((4,))],
        name="pack_rows",
        **settings(1),
    )(*arguments)


def pack_features(sizes, block, sets, hidden):
    n_groups, n_fsdp, n_resp, n_tp = sizes
    rows, width = hidden.shape
    per_core = n_fsdp // n_tp
    half = block // n_groups

    def start_of(place, n):
        group = (lax.axis_index("groups") + place[0]) % n_groups
        resp = (lax.axis_index("resp") + place[1]) % n_resp
        return (n * n_resp + resp) * block + group * half

    if half % HD:
        return [
            jnp.concatenate(
                [
                    lax.dynamic_slice_in_dim(hidden, start_of(place, n), half, axis=1)
                    for n in range(per_core)
                ],
                axis=1,
            )
            for place in sets
        ]

    step = rows // 4

    def body(hidden_ref, *refs):
        outs, (held, sems) = refs[: len(sets)], refs[len(sets) :]
        copies = []
        for n in range(rows // step):
            part = pl.ds(n * step, step)
            copies.append(
                pltpu.make_async_copy(hidden_ref.at[part, :], held.at[part, :], sems.at[n])
            )
        for copy in copies:
            copy.start()
        for n, copy in enumerate(copies):
            copy.wait()
            part = slice(n * step, (n + 1) * step)
            for place, out in zip(sets, outs):
                for k in range(per_core):
                    first = pl.multiple_of(start_of(place, k), HD)
                    out[part, k * half : (k + 1) * half] = held[part, pl.ds(first, half)]

    shape = (rows, per_core * half)
    return pl.pallas_call(
        body,
        grid=(1,),
        in_specs=[HBM],
        out_specs=[pl.BlockSpec(shape, lambda _: (0, 0))] * len(sets),
        out_shape=[jax.ShapeDtypeStruct(shape, hidden.dtype)] * len(sets),
        scratch_shapes=[pltpu.VMEM((rows, width), hidden.dtype), pltpu.SemaphoreType.DMA((4,))],
        name="pack_features",
        **settings(12),
    )(pltpu.with_memory_space_constraint(hidden, pltpu.HBM))


def line_ring(size):
    return list(range(0, size, 2)) + list(range(1, size, 2))[::-1]


def owner_of(n_fsdp, hops):
    fsdp = lax.axis_index("fsdp")
    place = jnp.where(fsdp % 2 == 0, fsdp // 2, n_fsdp - (fsdp + 1) // 2)
    at = (place - hops + n_fsdp) % n_fsdp
    return jnp.where(at < n_fsdp // 2, 2 * at, 2 * n_fsdp - 1 - 2 * at)


def project(n_fsdp, pieces, pairs, types, waits=()):
    kinds, half, columns = pieces[0][0].shape
    rows, depth = pairs[0][0].shape
    dtype = pairs[0][0].dtype
    total, count = len(pieces), len(pairs)

    def body(*refs):
        piece_refs, refs = refs[:total], refs[total:]
        pair_refs, refs = refs[: 2 * count], refs[2 * count + len(waits) :]
        outs, weights = refs[:-1], refs[-1]
        core = lax.axis_index("tp")
        for ref, (_, hops) in zip(piece_refs, pieces):
            place = pl.ds(pl.multiple_of(owner_of(n_fsdp, hops) * half, half), half)
            for kind in range(kinds):
                weights[kind, place, :] = ref[kind]
        first = pl.ds(pl.multiple_of(core * depth, depth), depth)
        second = pl.ds(pl.multiple_of((1 - core) * depth, depth), depth)
        for n in range(count):
            near_ref, far_ref = pair_refs[2 * n : 2 * n + 2]
            for kind in range(kinds):
                sums = dot_nn(near_ref[...], weights[kind, first, :])
                sums = sums + dot_nn(far_ref[...], weights[kind, second, :])
                outs[n][kind] = sums.astype(outs[n].dtype)

    def whole(shape):
        return pl.BlockSpec(shape, lambda _: (0,) * len(shape))

    shape = (kinds, rows, columns)
    return pl.pallas_call(
        body,
        grid=(1,),
        in_specs=[whole((kinds, half, columns))] * total
        + [whole((rows, depth))] * (2 * count)
        + [ANYWHERE] * len(waits),
        out_specs=[whole(shape)] * count,
        out_shape=[jax.ShapeDtypeStruct(shape, t) for t in types],
        scratch_shapes=[pltpu.VMEM((kinds, n_fsdp * half, columns), dtype)],
        name="project",
        **settings(24),
    )(*[x for x, _ in pieces], *[x for pair in pairs for x in pair], *waits)


def take(ref, first, count):
    return jnp.concatenate(
        [ref[:, (first + n) * HD : (first + n + 1) * HD] for n in range(count)], axis=0
    )


def put(ref, first, count, value):
    tokens = ref.shape[0]
    value = jnp.broadcast_to(value, (count * tokens, HD)).astype(ref.dtype)
    for n in range(count):
        ref[:, (first + n) * HD : (first + n + 1) * HD] = value[n * tokens : (n + 1) * tokens]


def attend_cache(slots, group_size, queries, caches, waits):
    count = len(caches)
    tokens = queries.shape[0] // slots
    heads = queries.shape[1] // (group_size * HD)
    length = caches[0].shape[1]
    step = 2 if group_size % 2 == 0 else 1

    def body(q_ref, *refs):
        mixed_ref, level_ref, mark_ref = refs[-3:]
        mark_ref[...] = jnp.zeros(mark_ref.shape, mark_ref.dtype)
        keys = [ref[0] for ref in refs[:count]]
        values = [ref[1] for ref in refs[:count]]
        wide = [jnp.concatenate([v, jnp.ones(v.shape, v.dtype)], axis=1) for v in values]

        def scores_of(first):
            q = take(q_ref, first, step)
            return [dot_nt(q, k) for k in keys]

        coming = scores_of(0)
        for first in range(0, group_size, step):
            scores = coming
            if first + step < group_size:
                coming = scores_of(first + step)
            tops = [s[:, n * HD : (n + 1) * HD] for s in scores for n in range(length // HD)]
            top = jnp.max(functools.reduce(jnp.maximum, tops), axis=1, keepdims=True)
            out = None
            for s, v in zip(scores, wide):
                probs = jnp.exp2((s - top) * FACTOR).astype(jnp.bfloat16)
                part = dot_nn(probs, v)
                out = part if out is None else out + part
            total = out[:, HD:]
            put(mixed_ref, first, step, out[:, :HD] / total)
            put(level_ref, first, step, top * FACTOR + jnp.log2(total))

    spec_wide = pl.BlockSpec((tokens, group_size * HD), lambda head, slot: (slot, head))
    spec_c = pl.BlockSpec((2, length, HD), lambda head, slot: (0, 0, head))
    spec_mark = pl.BlockSpec((8, HD), lambda head, slot: (0, 0))
    return pl.pallas_call(
        body,
        grid=(heads, slots),
        in_specs=[spec_wide] + [spec_c] * count + [ANYWHERE] * len(waits),
        out_specs=[spec_wide] * 2 + [spec_mark],
        out_shape=[jax.ShapeDtypeStruct(queries.shape, jnp.float32)] * 2
        + [jax.ShapeDtypeStruct((8, HD), jnp.float32)],
        name="attend_cache",
        **settings(20),
    )(queries, *caches, *waits)


def attend_own(slots, group_size, live, queries, parts, table, state):
    count = len(parts)
    tokens = queries.shape[0] // slots
    heads = queries.shape[1] // (group_size * HD)

    def body(live_ref, q_ref, *refs):
        part_refs = refs[:count]
        table_ref, mixed_ref, level_ref, out_ref = refs[count:]
        slot = pl.program_id(0)

        def summed(kind):
            return functools.reduce(jnp.add, [ref[kind].astype(jnp.float32) for ref in part_refs])

        key = summed(0)
        key = key * table_ref[0] + pltpu.roll(key, HD // 2, 1) * table_ref[1]
        key = key.astype(jnp.bfloat16)
        value = summed(1).astype(jnp.bfloat16)
        wide = jnp.concatenate([value, jnp.ones((tokens, HD), jnp.bfloat16)], axis=1)
        row = lax.broadcasted_iota(jnp.int32, (tokens, tokens), 0)
        causal = row >= lax.broadcasted_iota(jnp.int32, (tokens, tokens), 1)
        hidden_later = jnp.where(causal, 0.0, -1e30)
        hidden_later = jnp.concatenate([hidden_later] * group_size, axis=0)
        scores = dot_nt(take(q_ref, 0, group_size), key) * FACTOR + hidden_later
        level = take(level_ref, 0, group_size)
        top = jnp.max(jnp.maximum(level, scores), axis=1, keepdims=True)
        probs = jnp.exp2(scores - top).astype(jnp.bfloat16)
        kept = jnp.exp2(level - top)
        out = dot_nn(probs, wide)
        mixed = take(mixed_ref, 0, group_size) * kept + out[:, :HD]
        total = kept + out[:, HD:]
        inverse = pl.reciprocal(total, approx=True)
        result = mixed * (inverse * (2.0 - total * inverse))
        put(out_ref, 0, group_size, jnp.where(slot < live_ref[0], result, 0.0))

    spec_wide = pl.BlockSpec((tokens, group_size * HD), lambda slot, head: (slot, head))
    spec_part = pl.BlockSpec((2, tokens, HD), lambda slot, head: (0, slot, head))
    spec_table = pl.BlockSpec(table.shape, lambda slot, head: (0, 0, 0))
    kept_back = [pltpu.with_memory_space_constraint(x, pltpu.HBM) for x in (table, *state)]
    return pl.pallas_call(
        body,
        grid=(slots, heads),
        in_specs=[pl.BlockSpec(memory_space=pltpu.SMEM), spec_wide]
        + [spec_part] * count
        + [spec_table, spec_wide, spec_wide],
        out_specs=spec_wide,
        out_shape=jax.ShapeDtypeStruct(queries.shape, queries.dtype),
        name="attend_own",
        **settings(24),
    )(live, queries, *parts, *kept_back)


def rotation_tables(extent, offset):
    orders = np.arange(HD // 2, dtype=np.float64)
    inverse = np.exp(-(2.0 * orders / HD) * math.log(500000.0))
    angles = (offset + np.arange(extent))[:, None] * inverse[None, :]
    cosine, sine = np.cos(angles), np.sin(angles)
    halves = [np.concatenate([cosine, cosine], axis=1), np.concatenate([-sine, sine], axis=1)]
    return jnp.asarray(np.stack(halves), jnp.float32)


def on_device(sizes, hidden, queries, prompt_keys, prompt_values, key_weight, value_weight, counts):
    n_groups, n_fsdp, n_resp, n_tp = sizes
    _, slots, tokens, part_width = hidden.shape
    block, columns = key_weight.shape
    group_size = queries.shape[3] // columns
    rows = slots * tokens
    plane = ("groups", "resp")
    cores = [(n, (n + 1) % n_tp) for n in range(n_tp)]
    ring = line_ring(n_fsdp)
    rightward = [(ring[n], ring[(n + 1) % n_fsdp]) for n in range(n_fsdp)]
    leftward = [(b, a) for a, b in rightward]
    along = [(0, b) for b in range(1, n_resp)]
    across = [(a, b) for a in range(1, n_groups) for b in range(1, n_resp)]
    twins = [(a, 0) for a in range(1, n_groups)]
    sets = [(0, 0), *across, *twins, *along]

    def shift(a, b):
        return [
            (g * n_resp + r, (g + a) % n_groups * n_resp + (r + b) % n_resp)
            for g in range(n_groups)
            for r in range(n_resp)
        ]

    share, cache = pack_rows(n_groups, key_weight, value_weight, prompt_keys[0], prompt_values[0])

    caches = [cache]
    for b in range(1, n_resp):
        around = [(n, (n + b) % n_resp) for n in range(n_resp)]
        caches.append(lax.ppermute(cache, "resp", around))

    pieces = [(share, 0)]
    held = share
    for hop in range(1, n_fsdp // 2 + 1):
        held = lax.ppermute(held, "fsdp", rightward)
        pieces.append((held, hop))
    first_hop, ends = pieces[1][0], [held]
    held = share
    for hop in range(1, n_fsdp - n_fsdp // 2):
        held = lax.ppermute(held, "fsdp", leftward)
        pieces.append((held, -hop))
    ends.append(held)

    flat_queries = queries.reshape(rows, queries.shape[3])
    *state, mark = attend_cache(slots, group_size, flat_queries, caches, [first_hop])

    near = dict(zip(sets, pack_features(sizes, block, sets, hidden.reshape(rows, part_width))))
    for place in along:
        near[place] = after(near[place], first_hop)
    for place in sets[1:]:
        waits = ends if place in along else []
        moved = lax.ppermute(near[place], plane, shift(*place))
        near[place] = after(moved, mark, *waits)
    far = {place: lax.ppermute(near[place], "tp", cores) for place in sets}

    narrow, wide = jnp.bfloat16, jnp.float32
    parts = []
    for chosen, waits in (([*across, *twins, sets[0]], [near[p] for p in along]), (along, [])):
        types = [narrow if any(p) else wide for p in chosen]
        sums = project(n_fsdp, pieces, [(near[p], far[p]) for p in chosen], types, waits)
        for p, x in zip(chosen, sums):
            back = shift(n_groups - p[0], n_resp - p[1])
            parts.append(lax.ppermute(x, plane, back) if any(p) else x)

    table = rotation_tables(tokens, PLEN)
    live = (counts[0] - lax.axis_index("resp") * slots).astype(jnp.int32)[None]
    out = attend_own(slots, group_size, live, flat_queries, parts, table, state)
    return out.reshape(queries.shape)


def solution(mesh):
    placed = (
        P(("groups", "fsdp"), "resp", None, "tp"),
        P(("groups", "fsdp"), "resp", None, "tp"),
        P(("groups", "fsdp"), "resp", "tp"),
        P(("groups", "fsdp"), "resp", "tp"),
        P(("fsdp", "resp"), "tp"),
        P(("fsdp", "resp"), "tp"),
        P(("groups", "fsdp")),
    )
    sizes = tuple(mesh.shape[name] for name in ("groups", "fsdp", "resp", "tp"))
    return jax.shard_map(
        functools.partial(on_device, sizes),
        mesh=mesh,
        in_specs=placed,
        out_specs=P(("groups", "fsdp"), "resp", None, "tp"),
        check_vma=False,
    )
```
